128 devices in a mesh: outer: 2 (over core), inner: 64 (over z, y, x).
Axes of the slice: x: 4, y: 4, z: 4, core: 2. Of those that a mesh axis runs over, the one named last changes fastest.
Arguments:
- matrix: float32 [65536, 1024], P(('outer', 'inner'))
- sign_flip: int32 [65536], P(('outer', 'inner')), may hold values from -1 to 1, as said below
- keep_list: int32 [128, 2], replicated, may hold values from 0 to 3, as said below
- ridge_weights: float32 [1024], replicated, may hold values from 0.05 to 1
Outputs:
- sketch: float32 [32768, 1024], P(('outer', 'inner'))
- factor: float32 [1024, 1024], P(('outer', 'inner'))
The draws below stay inside these ranges and needn't reach their ends.
Inputs may be any that keep to these rules, and one draw needn't show every extreme that they name: `sign_flip`: each entry is 1 or -1. `keep_list`: row s lists 2 different block numbers of device s's rows in increasing order.
All inputs are finite; a program needn't handle non-finite values.
Results may differ from the reference program's by a relative error of at most 0.00026.
Values sent between devices are 32-bit elements; how exact they have to be, the bound alone decides.
No kernel may reach another device: no remote copies, remote signals or barrier semaphores. Data moves between devices by JAX's collectives and lax.ppermute only.
A program may use at most 128 MiB of HBM per device.

```python
import math
import jax
import jax.numpy as jnp
from jax import lax

FEAT = 1024
ROWS_DEV = 512
SHARDS = 128
ROWS = 65536
BLOCKS = 4
KEEP_BLK = 2
KEPT = 32768
SPREAD = 4
N_OUTER = 2
N_INNER = 64


def draw_matrix(key, part):
    noise_key = jax.random.fold_in(key, 11)
    row_key = jax.random.fold_in(key, 12)
    column_key = jax.random.fold_in(key, 13)
    shared_key = jax.random.fold_in(key, 14)
    weight_key = jax.random.fold_in(key, 15)
    amp_key = jax.random.fold_in(key, 16)
    shared = jnp.zeros((ROWS, FEAT), jnp.float32)
    noise = jax.random.normal(noise_key, (ROWS, FEAT), jnp.float32)
    row_scale = jnp.exp(jax.random.uniform(row_key, (ROWS, 1), jnp.float32, math.log(0.3), math.log(3.0)))
    column_scale = jnp.exp(jax.random.uniform(column_key, (1, FEAT), jnp.float32, math.log(0.5), math.log(5.0)))
    for number in range(8):
        rows_term = jax.random.normal(jax.random.fold_in(shared_key, number), (ROWS, 1), jnp.float32)
        cols_term = jax.random.normal(jax.random.fold_in(weight_key, number), (1, FEAT), jnp.float32)
        amplitude = jnp.exp(jax.random.uniform(jax.random.fold_in(amp_key, number), (), jnp.float32, math.log(0.35), math.log(0.8)))
        shared = shared + amplitude * rows_term * cols_term
    return (noise + shared) * row_scale * column_scale


def draw_sign_flip(key, part):
    coins = jax.random.randint(jax.random.fold_in(key, 21), (ROWS,), 0, 2)
    return (2 * coins - 1).astype(jnp.int32)


def draw_keep_list(key, part):
    subkeys = jax.random.split(jax.random.fold_in(key, 31), SHARDS)
    orders = jax.vmap(lambda single_key: jax.random.permutation(single_key, BLOCKS))(subkeys)
    chosen = jnp.sort(orders[:, :KEEP_BLK], axis=1).astype(jnp.int32)
    last_row = jax.random.randint(jax.random.fold_in(key, 32), (), 0, SHARDS)
    other_row = (last_row + 1 + jax.random.randint(jax.random.fold_in(key, 33), (), 0, SHARDS - 1)) % SHARDS
    row_index = lax.iota(jnp.int32, SHARDS)[:, None]
    low_blocks = lax.iota(jnp.int32, KEEP_BLK)[None, :]
    high_blocks = low_blocks + (BLOCKS - KEEP_BLK)
    chosen = jnp.where(row_index == last_row, high_blocks, chosen)
    chosen = jnp.where(row_index == other_row, low_blocks, chosen)
    return chosen.astype(jnp.int32)


def setup_inputs(seed: int = 0) -> dict:
    keys = jax.random.split(jax.random.key(seed), 5)
    matrix = draw_matrix(jax.random.fold_in(keys[4], 71), 0)
    sign_flip = draw_sign_flip(jax.random.fold_in(keys[4], 71), 0)
    keep_list = draw_keep_list(jax.random.fold_in(keys[4], 71), 0)
    ridge_weights = jnp.clip(jnp.exp(jax.random.uniform(keys[3], (FEAT,), jnp.float32, math.log(0.05), math.log(1.0))), 0.05, 1.0)
    return {"matrix": matrix, "sign_flip": sign_flip, "keep_list": keep_list, "ridge_weights": ridge_weights}


precise = lax.Precision.HIGHEST

def sign_table(extent):
    index_list = lax.iota(jnp.int32, extent)
    common_bits = jnp.bitwise_and(index_list[:, None], index_list[None, :])
    parity = jnp.zeros((extent, extent), jnp.int32)
    for shift_by in range(max(extent.bit_length() - 1, 0)):
        parity = parity + jnp.bitwise_and(jnp.right_shift(common_bits, shift_by), 1)
    return (1 - 2 * (parity % 2)).astype(jnp.float32)

def transform_axis(values, dim_index, extent):
    rotated = jnp.tensordot(sign_table(extent), values, axes=((1,), (dim_index,)), precision=precise)
    return jnp.moveaxis(rotated, 0, dim_index)

def reference(matrix, sign_flip, keep_list, ridge_weights):
    flipped = matrix * sign_flip.astype(jnp.float32)[:, None]
    first_len = 2 ** ((ROWS_DEV.bit_length() - 1) // 2)
    row_grid = flipped.reshape(N_OUTER, N_INNER, first_len, ROWS_DEV // first_len, FEAT)
    row_grid = transform_axis(row_grid, 3, ROWS_DEV // first_len)
    row_grid = transform_axis(row_grid, 2, first_len)
    row_grid = transform_axis(row_grid, 1, N_INNER)
    row_grid = transform_axis(row_grid, 0, N_OUTER) * (1.0 / math.sqrt(ROWS))
    row_grid = row_grid.reshape(N_OUTER, N_INNER, N_INNER, N_OUTER, SPREAD, FEAT)
    row_grid = jnp.transpose(row_grid, (3, 2, 1, 0, 4, 5)).reshape(SHARDS, BLOCKS, 128, FEAT)
    kept_rows = jax.vmap(lambda device_rows, chosen: device_rows[chosen])(row_grid, keep_list)
    sketch = kept_rows.reshape(KEPT, FEAT)
    gram = lax.dot_general(sketch.astype(jnp.float32), sketch.astype(jnp.float32), (((0,), (0,)), ((), ())), precision=precise, preferred_element_type=jnp.float32) / KEPT + jnp.diag(ridge_weights)
    factor = jnp.transpose(jnp.linalg.cholesky(gram))
    return (sketch, factor)
```

```python
import functools

import jax
import jax.numpy as jnp
import numpy as np
from jax import lax
from jax.experimental import pallas as pl
from jax.experimental.pallas import tpu as pltpu
from jax.sharding import PartitionSpec as P

precise = lax.Precision.HIGHEST
f32 = jnp.float32
bf16 = jnp.bfloat16
VMEM = pl.BlockSpec(memory_space=pltpu.VMEM)
SMEM = pl.BlockSpec(memory_space=pltpu.SMEM)
FEAT = 1024
NB = 128
PANELS = FEAT // NB
STRIPS = ((0, 3, 4, 7), (1, 2, 5, 6))
HALF_BLOCKS = 18
Z_GROUPS = [[i + 16 * j for j in range(4)] for i in range(16)]
PLANES = [[16 * j + i for i in range(16)] for j in range(4)]


def params(mib=48):
    return pltpu.CompilerParams(vmem_limit_bytes=mib << 20)


def parity_sign(left, right):
    common = left & right
    parity = np.zeros_like(common)
    for shift_by in range(10):
        parity ^= (common >> shift_by) & 1
    return 1 - 2 * parity


def local_table():
    az, c, axy, e = np.meshgrid(range(4), range(2), range(16), range(4), indexing="ij")
    k = (az * 128 + axy * 8 + c * 4 + e).reshape(-1, 1)
    return parity_sign(k, np.arange(512)[None, :]).astype(np.float32).astype(bf16)


def final_table():
    j, i, o, e = (v.reshape(-1, 1) for v in np.meshgrid(range(2), range(16), range(2), range(4), indexing="ij"))
    ip, op, jp, ep = (v.reshape(1, -1) for v in np.meshgrid(range(16), range(2), range(2), range(4), indexing="ij"))
    table = parity_sign(i, ip) * parity_sign(o, op) * (j == jp) * (e == ep)
    return table.astype(np.float32).astype(bf16)


def halves(x):
    high = x.astype(bf16)
    return high, (x - high.astype(f32)).astype(bf16)


def mm(a, b):
    return jnp.dot(a, b, preferred_element_type=f32)


def tmm(a, b):
    return lax.dot_general(a, b, (((0,), (0,)), ((), ())), preferred_element_type=f32)


def local_mix_kernel(table_ref, sign_ref, x_ref, o_ref, signed):
    @pl.when(pl.program_id(0) == 0)
    def _():
        signed[...] = (table_ref[...].astype(f32) * (sign_ref[...].astype(f32) * 2.0**-13)).astype(bf16)

    high, low = halves(x_ref[...])
    o_ref[...] = mm(signed[...], high) + mm(signed[...], low)


def local_mix(matrix, sign_flip):
    rows, features = matrix.shape
    cols = 256
    return pl.pallas_call(
        local_mix_kernel,
        grid=(features // cols,),
        out_shape=jax.ShapeDtypeStruct((rows, features), f32),
        in_specs=[
            pl.BlockSpec((rows, rows), lambda g: (0, 0)),
            pl.BlockSpec((1, rows), lambda g: (0, 0)),
            pl.BlockSpec((rows, cols), lambda g: (0, g)),
        ],
        out_specs=pl.BlockSpec((rows, cols), lambda g: (0, g)),
        scratch_shapes=[pltpu.VMEM((rows, rows), bf16)],
        compiler_params=params(),
    )(jnp.asarray(local_table()), sign_flip.reshape(1, rows), matrix)


def select_kernel(keep_ref, y_ref, v_ref):
    y0, y1, y2, y3 = (y_ref[z] for z in range(4))
    s, d, s2, d2 = y0 + y1, y0 - y1, y2 + y3, y2 - y3

    def combo(which):
        low = (which & 1) == 1
        first = jnp.where(low, d, s)
        second = jnp.where(low, d2, s2)
        return first + jnp.where((which & 2) == 2, -second, second)

    shape = s.shape
    v0 = combo(jnp.broadcast_to(keep_ref[:, 0:1], shape))
    v1 = combo(jnp.broadcast_to(keep_ref[:, 1:2], shape))
    upper = (lax.broadcasted_iota(jnp.int32, shape, 0) & 7) < 4
    even = jnp.where(upper, v0, pltpu.roll(v1, 4, axis=0))
    odd = jnp.where(upper, pltpu.roll(v0, shape[0] - 4, axis=0), v1)
    v_ref[:, 0] = even.reshape(16, 8, shape[1])
    v_ref[:, 1] = odd.reshape(16, 8, shape[1])


def select_rows(keep_rows, y):
    cols = 256
    features = y.shape[2]
    return pl.pallas_call(
        select_kernel,
        grid=(features // cols,),
        out_shape=jax.ShapeDtypeStruct((16, 2, 8, features), f32),
        in_specs=[
            pl.BlockSpec((128, 2), lambda g: (0, 0)),
            pl.BlockSpec((4, 128, cols), lambda g: (0, 0, g)),
        ],
        out_specs=pl.BlockSpec((16, 2, 8, cols), lambda g: (0, 0, 0, g)),
        compiler_params=params(),
    )(keep_rows, y)


def gram_kernel(ids_ref, v_ref, w_ref, g_ref, s_ref, high, low):
    core = ids_ref[0]
    for part, ref in enumerate((v_ref, w_ref)):
        h, l = halves(ref[...])
        high[256 * part : 256 * part + 256, :] = h
        low[256 * part : 256 * part + 256, :] = l
        own = ref[pl.ds(pl.multiple_of(core * 128, 128), 128), :]
        s_ref[:, part] = own.reshape(16, 8, FEAT)
    for which, strips in enumerate(STRIPS):

        @pl.when(core == which)
        def _():
            slot = 0
            for strip in strips:
                at = NB * strip
                h, l = high[:, at : at + NB], low[:, at : at + NB]
                right, right_low = high[:, at:], low[:, at:]
                total = tmm(h, right) + (tmm(h, right_low) + tmm(l, right))
                for block in range(PANELS - strip):
                    g_ref[slot] = total[:, NB * block : NB * block + NB]
                    slot += 1


def gram_half(ids, mine, theirs):
    rows = mine.shape[0]
    return pl.pallas_call(
        gram_kernel,
        out_shape=(
            jax.ShapeDtypeStruct((HALF_BLOCKS, NB, NB), f32),
            jax.ShapeDtypeStruct((16, 2, 8, FEAT), f32),
        ),
        in_specs=[SMEM, VMEM, VMEM],
        out_specs=(VMEM, VMEM),
        scratch_shapes=[pltpu.VMEM((2 * rows, FEAT), bf16)] * 2,
        compiler_params=params(),
    )(ids, mine, theirs)


def final_kernel(ids_ref, table_ref, r_ref, o_ref):
    high, low = halves(r_ref[...])
    total = mm(table_ref[...], high) + mm(table_ref[...], low)
    odd = (lax.broadcasted_iota(jnp.int32, total.shape, 0) >> 2) & 1
    flip = (odd * ids_ref[0]) == 1
    o_ref[...] = total * jnp.where(flip, -32.0, 32.0)


def final_mix(ids, received):
    rows, features = received.shape
    cols = 256
    return pl.pallas_call(
        final_kernel,
        grid=(features // cols,),
        out_shape=jax.ShapeDtypeStruct((rows, features), f32),
        in_specs=[
            SMEM,
            pl.BlockSpec((rows, rows), lambda g: (0, 0)),
            pl.BlockSpec((rows, cols), lambda g: (0, g)),
        ],
        out_specs=pl.BlockSpec((rows, cols), lambda g: (0, g)),
        compiler_params=params(),
    )(ids, jnp.asarray(final_table()), received)


def lane_splat(x, lane):
    return jnp.broadcast_to(x[:, lane : lane + 1], (8, NB))


def factor_block(w, upper, inverse):
    lane = lax.broadcasted_iota(jnp.int32, (8, NB), 1)
    sub = lax.broadcasted_iota(jnp.int32, (8, NB), 0)
    pairs = [(a, b) for a in range(8) for b in range(a, 8)]

    def row_splat(row):
        return jnp.broadcast_to(w[row : row + 1, :], (8, NB))

    rho = [row_splat(b) for b in range(8)]
    e = {(a, b): lane_splat(rho[a], b) for a, b in pairs}
    for step in range(16):
        base = 8 * step
        inside = (lane >= base) & (lane < base + 8)
        aug = [jnp.where(inside, jnp.where(lane == base + b, 1.0, 0.0), rho[b]) for b in range(8)]
        if step < 15:
            coming = [jnp.where(inside, 0.0, row_splat(base + 8 + a)) for a in range(8)]
            start = {(a, b): lane_splat(coming[a], base + 8 + b) for a, b in pairs}
        u, t = [None] * 8, [None] * 8
        for b in range(8):
            r = lax.rsqrt(e[b, b])
            u[b], t[b] = rho[b] * r, aug[b] * r
            c = {a: e[b, a] * r for a in range(b + 1, 8)}
            for a in range(b + 1, 8):
                for a2 in range(a, 8):
                    e[a, a2] = e[a, a2] - c[a] * c[a2]
            for a in range(b + 1, 8):
                rho[a] = rho[a] - c[a] * u[b]
                aug[a] = aug[a] - c[a] * t[b]
        for b in range(8):
            upper[base + b : base + b + 1, :] = jnp.where(lane >= base + b, u[b], 0.0)[0:1]
            inverse[base + b : base + b + 1, :] = jnp.where(lane <= base + b, t[b], 0.0)[0:1]
        if step < 15:
            c = {(b, a): lane_splat(u[b], base + 8 + a) for b in range(8) for a in range(8)}
            e = {}
            for a, a2 in pairs:
                total = c[0, a] * c[0, a2]
                for b in range(1, 8):
                    total = total + c[b, a] * c[b, a2]
                e[a, a2] = start[a, a2] - total
            for a in range(8):
                total = c[0, a] * t[0]
                for b in range(1, 8):
                    total = total + c[b, a] * t[b]
                coming[a] = coming[a] - total
            rho = coming
        if step < 14:
            after = base + 16
            left, right = u[0], t[0]
            for b in range(1, 8):
                left = jnp.where(sub == b, u[b], left)
                right = jnp.where(sub == b, t[b], right)
            update = lax.dot_general(
                left, right, (((0,), (0,)), ((), ())), precision=precise, preferred_element_type=f32
            )
            rest = lax.broadcasted_iota(jnp.int32, (NB - after, NB), 1)
            cleared = jnp.where((rest >= base) & (rest < base + 8), 0.0, w[after:, :])
            w[after:, :] = cleared - update[after:, :]


def factor_kernel(ids_ref, ridge_ref, own_ref, other_ref, o_ref, a, w, upper, inverse):
    core, position = ids_ref[0], ids_ref[1]
    eye = lax.broadcasted_iota(jnp.int32, (NB, NB), 0) == lax.broadcasted_iota(jnp.int32, (NB, NB), 1)
    for which in range(2):

        @pl.when(core == which)
        def _():
            for ref, strips in ((own_ref, STRIPS[which]), (other_ref, STRIPS[1 - which])):
                slot = 0
                for strip in strips:
                    for block in range(strip, PANELS):
                        piece = ref[slot]
                        if block == strip:
                            ridge = ridge_ref[0:1, NB * strip : NB * strip + NB]
                            piece = piece + jnp.where(eye, ridge, 0.0)
                        a[NB * strip : NB * strip + NB, NB * block : NB * block + NB] = piece
                        slot += 1

    def body(panel, carry):
        at = pl.multiple_of(panel * NB, NB)
        w[...] = a[pl.ds(at, NB), pl.ds(at, NB)]
        factor_block(w, upper, inverse)
        for fixed in range(PANELS):

            @pl.when(panel == fixed)
            def _():
                s0, s1 = NB * fixed, NB * fixed + NB
                a[s0:s1, s0:s1] = upper[...]
                if fixed < PANELS - 1:
                    rows = jnp.dot(inverse[...], a[s0:s1, s1:], precision=precise, preferred_element_type=f32)
                    a[s0:s1, s1:] = rows
                    for strip in range(fixed + 1, PANELS):
                        b0, t0 = NB * (strip - fixed - 1), NB * strip
                        a[t0 : t0 + NB, t0:] = a[t0 : t0 + NB, t0:] - lax.dot_general(
                            rows[:, b0 : b0 + NB],
                            rows[:, b0:],
                            (((0,), (0,)), ((), ())),
                            precision=precise,
                            preferred_element_type=f32,
                        )

        return carry

    lax.fori_loop(0, PANELS, body, 0)
    out = a[pl.ds(pl.multiple_of(position * 8, 8), 8), :]
    lane = lax.broadcasted_iota(jnp.int32, out.shape, 1)
    o_ref[...] = jnp.where(lane >= (position // 16) * NB, out, 0.0)


def factor_rows(ids, ridge, own, other):
    return pl.pallas_call(
        factor_kernel,
        out_shape=jax.ShapeDtypeStruct((8, FEAT), f32),
        in_specs=[SMEM, VMEM, VMEM, VMEM],
        out_specs=VMEM,
        scratch_shapes=[pltpu.VMEM((FEAT, FEAT), f32)] + [pltpu.VMEM((NB, NB), f32)] * 3,
        compiler_params=params(),
        cost_estimate=pl.CostEstimate(flops=40_000_000_000, bytes_accessed=2 << 20, transcendentals=0),
    )(ids, ridge, own, other)


def swap_cores(x):
    return lax.ppermute(x, "outer", [(0, 1), (1, 0)])


def along_z(x, distance):
    return lax.ppermute(x, "inner", [(i, (i + 16 * distance) % 64) for i in range(64)])


def plane_exchange(x):
    return lax.all_to_all(x, "inner", 0, 0, axis_index_groups=PLANES, tiled=True)


def local(matrix, sign_flip, keep_list, ridge_weights):
    core, inner = lax.axis_index("outer"), lax.axis_index("inner")
    ids = jnp.stack([core, core * 64 + inner]).astype(jnp.int32)
    keep_here = lax.dynamic_index_in_dim(keep_list.reshape(2, 4, 16, 2), inner // 16, 1, False)
    keep_rows = jnp.repeat(keep_here.reshape(32, 2), 4, axis=0)
    mixed = local_mix(matrix, sign_flip)
    along = lax.all_to_all(
        mixed.reshape(4, 128, FEAT), "inner", 0, 0, axis_index_groups=Z_GROUPS, tiled=True
    )
    mine = select_rows(keep_rows, along).reshape(256, FEAT)
    theirs = swap_cores(mine)
    gram, to_send = gram_half(ids, mine, theirs)
    pieces = plane_exchange(gram.reshape(16, 144, 128))
    piece = jnp.sum(pieces, axis=0)
    piece = (piece + along_z(piece, 2)) + (along_z(piece, 1) + along_z(piece, 3))
    own = plane_exchange(jnp.broadcast_to(piece[None], (16, 144, 128))).reshape(HALF_BLOCKS, NB, NB)
    other = swap_cores(own)
    to_send, own, other = lax.optimization_barrier((to_send, own, other))
    received = plane_exchange(to_send)
    factor = factor_rows(ids, ridge_weights.reshape(1, FEAT), own, other)
    sketch = final_mix(ids, received.reshape(256, FEAT))
    return sketch, factor


def solution(mesh):
    return jax.shard_map(
        local,
        mesh=mesh,
        in_specs=(P(("outer", "inner"), None), P(("outer", "inner")), P(), P()),
        out_specs=(P(("outer", "inner"), None), P(("outer", "inner"), None)),
        check_vma=False,
    )
```

```python
import jax
import jax.numpy as jnp
import numpy as np
from jax import lax
from jax.experimental import pallas as pl
from jax.experimental.pallas import tpu as pltpu
from jax.sharding import PartitionSpec as P

precise = lax.Precision.HIGHEST
f32 = jnp.float32
bf16 = jnp.bfloat16
VMEM = pl.BlockSpec(memory_space=pltpu.VMEM)
SMEM = pl.BlockSpec(memory_space=pltpu.SMEM)
FEAT = 1024
NB = 128
HALF = FEAT // 2
PAIRS = ((0, 3), (1, 2))
Z_GROUPS = [[i + 16 * j for j in range(4)] for i in range(16)]
PLANES = [[16 * j + i for i in range(16)] for j in range(4)]


def params(mib=48):
    return pltpu.CompilerParams(vmem_limit_bytes=mib << 20)


def parity_sign(left, right):
    common = left & right
    parity = np.zeros_like(common)
    for shift_by in range(10):
        parity ^= (common >> shift_by) & 1
    return 1 - 2 * parity


def local_table():
    az, c, axy, e = np.meshgrid(range(4), range(2), range(16), range(4), indexing="ij")
    k = (az * 128 + axy * 8 + c * 4 + e).reshape(-1, 1)
    return parity_sign(k, np.arange(512)[None, :]).astype(np.float32).astype(bf16)


def final_table():
    j, i, o, e = (v.reshape(-1, 1) for v in np.meshgrid(range(2), range(16), range(2), range(4), indexing="ij"))
    ip, op, jp, ep = (v.reshape(1, -1) for v in np.meshgrid(range(16), range(2), range(2), range(4), indexing="ij"))
    table = parity_sign(i, ip) * parity_sign(o, op) * (j == jp) * (e == ep)
    return table.astype(np.float32).astype(bf16)


def halves(x):
    high = x.astype(bf16)
    return high, (x - high.astype(f32)).astype(bf16)


def mm(a, b):
    return jnp.dot(a, b, preferred_element_type=f32)


def tmm(a, b):
    return lax.dot_general(a, b, (((0,), (0,)), ((), ())), preferred_element_type=f32)


def turn(index, step):
    return (index + step) & 3


def local_mix_kernel(ids_ref, table_ref, sign_ref, x_ref, *rest):
    outs, signed = rest[:4], rest[4]

    @pl.when(pl.program_id(0) == 0)
    def _():
        signed[...] = (table_ref[...].astype(f32) * (sign_ref[...].astype(f32) * 2.0**-13)).astype(bf16)

    high, low = halves(x_ref[...])
    for step in range(4):
        rows = signed[pl.ds(pl.multiple_of(turn(ids_ref[4], step) * 128, 128), 128), :]
        outs[step][...] = mm(rows, high) + mm(rows, low)


def local_mix(ids, table, signs, matrix, half):
    rows = matrix.shape[0]
    cols = 256
    return pl.pallas_call(
        local_mix_kernel,
        grid=(HALF // cols,),
        out_shape=(jax.ShapeDtypeStruct((128, HALF), f32),) * 4,
        in_specs=[
            SMEM,
            pl.BlockSpec((rows, rows), lambda g: (0, 0)),
            pl.BlockSpec((1, rows), lambda g: (0, 0)),
            pl.BlockSpec((rows, cols), lambda g: (0, g + half * (HALF // cols))),
        ],
        out_specs=(pl.BlockSpec((128, cols), lambda g: (0, g)),) * 4,
        scratch_shapes=[pltpu.VMEM((rows, rows), bf16)],
        compiler_params=params(),
    )(ids, table, signs, matrix)


def select_kernel(ids_ref, keep_ref, y0_ref, y1_ref, y2_ref, y3_ref, v_ref):
    parts = [ref[...] for ref in (y0_ref, y1_ref, y2_ref, y3_ref)]
    shape = parts[0].shape

    def combo(which):
        total = None
        for step, part in enumerate(parts):
            common = which & turn(ids_ref[4], 4 - step)
            sign = (1 - 2 * ((common ^ (common >> 1)) & 1)).astype(f32)
            term = part * jnp.broadcast_to(sign, shape)
            total = term if total is None else total + term
        return total

    v0, v1 = combo(keep_ref[:, 0:1]), combo(keep_ref[:, 1:2])
    upper = (lax.broadcasted_iota(jnp.int32, shape, 0) & 7) < 4
    even = jnp.where(upper, v0, pltpu.roll(v1, 4, axis=0))
    odd = jnp.where(upper, pltpu.roll(v0, shape[0] - 4, axis=0), v1)
    v_ref[:, 0] = even.reshape(16, 8, shape[1])
    v_ref[:, 1] = odd.reshape(16, 8, shape[1])


def select_rows(ids, keep_rows, parts):
    cols = 256
    features = parts[0].shape[1]
    return pl.pallas_call(
        select_kernel,
        grid=(features // cols,),
        out_shape=jax.ShapeDtypeStruct((16, 2, 8, features), f32),
        in_specs=[SMEM, pl.BlockSpec((128, 2), lambda g: (0, 0))]
        + [pl.BlockSpec((128, cols), lambda g: (0, g))] * 4,
        out_specs=pl.BlockSpec((16, 2, 8, cols), lambda g: (0, 0, 0, g)),
        compiler_params=params(),
    )(ids, keep_rows, *parts)


def load_halves(mine_ref, theirs_ref, high, low):
    for part, ref in enumerate((mine_ref, theirs_ref)):
        h, l = halves(ref[...])
        high[256 * part : 256 * part + 256, :] = h
        low[256 * part : 256 * part + 256, :] = l


def strip_blocks(left, right, at, start, g_ref, slot):
    high, low = left
    high_right, low_right = right
    h, l = high[:, at : at + NB], low[:, at : at + NB]
    total = tmm(h, high_right[:, start:]) + (tmm(h, low_right[:, start:]) + tmm(l, high_right[:, start:]))
    for block in range((HALF - start) // NB):
        row = NB * (slot + block)
        g_ref[row : row + NB, :] = total[:, NB * block : NB * block + NB]
    return slot + (HALF - start) // NB


def first_gram_kernel(ids_ref, v_ref, w_ref, *rest):
    outs, (high, low, blocks) = rest[:4], rest[4:]
    load_halves(v_ref, w_ref, high, low)
    for which, strips in enumerate(PAIRS):

        @pl.when(ids_ref[0] == which)
        def _():
            slot = 0
            for strip in strips:
                slot = strip_blocks((high, low), (high, low), NB * strip, NB * strip, blocks, slot)

    for step in range(4):
        outs[step][...] = blocks[pl.ds(pl.multiple_of(turn(ids_ref[2], step) * 160, 8), 160), :]


def sum_split_kernel(ids_ref, *rest):
    parts, outs, total = rest[:4], rest[4:8], rest[8]
    total[...] = (parts[0][...] + parts[1][...]) + (parts[2][...] + parts[3][...])
    for step in range(4):
        outs[step][...] = total[pl.ds(pl.multiple_of(turn(ids_ref[3], step) * 40, 8), 40), :]


def sum_split(ids, parts):
    return pl.pallas_call(
        sum_split_kernel,
        out_shape=(jax.ShapeDtypeStruct((40, NB), f32),) * 4,
        in_specs=[SMEM] + [VMEM] * 4,
        out_specs=(VMEM,) * 4,
        scratch_shapes=[pltpu.VMEM((160, NB), f32)],
        compiler_params=params(),
    )(ids, *parts)


def second_gram_kernel(ids_ref, v1_ref, w1_ref, v2_ref, w2_ref, g_ref, s_ref, high1, low1, high2, low2):
    load_halves(v1_ref, w1_ref, high1, low1)
    load_halves(v2_ref, w2_ref, high2, low2)
    own = pl.ds(pl.multiple_of(ids_ref[0] * 128, 128), 128)
    for half, refs in enumerate(((v1_ref, w1_ref), (v2_ref, w2_ref))):
        for part, ref in enumerate(refs):
            s_ref[:, part, :, half * HALF : half * HALF + HALF] = ref[own, :].reshape(16, 8, HALF)
    for which, strips in enumerate(PAIRS):

        @pl.when(ids_ref[0] == which)
        def _():
            slot = 0
            for strip in strips:
                slot = strip_blocks((high1, low1), (high2, low2), NB * strip, 0, g_ref, slot)
            for strip in strips:
                slot = strip_blocks((high2, low2), (high2, low2), NB * strip, NB * strip, g_ref, slot)


def first_gram(ids, mine, theirs):
    return pl.pallas_call(
        first_gram_kernel,
        out_shape=(jax.ShapeDtypeStruct((160, NB), f32),) * 4,
        in_specs=[SMEM, VMEM, VMEM],
        out_specs=(VMEM,) * 4,
        scratch_shapes=[pltpu.VMEM((512, HALF), bf16)] * 2 + [pltpu.VMEM((5 * NB, NB), f32)],
        compiler_params=params(),
    )(ids, mine, theirs)


def second_gram(ids, mine1, theirs1, mine2, theirs2):
    return pl.pallas_call(
        second_gram_kernel,
        out_shape=(
            jax.ShapeDtypeStruct((13 * NB, NB), f32),
            jax.ShapeDtypeStruct((16, 2, 8, FEAT), f32),
        ),
        in_specs=[SMEM] + [VMEM] * 4,
        out_specs=(VMEM, VMEM),
        scratch_shapes=[pltpu.VMEM((512, HALF), bf16)] * 4,
        compiler_params=params(),
    )(ids, mine1, theirs1, mine2, theirs2)


def final_kernel(ids_ref, table_ref, r_ref, o_ref):
    high, low = halves(r_ref[...])
    total = mm(table_ref[...], high) + mm(table_ref[...], low)
    odd = (lax.broadcasted_iota(jnp.int32, total.shape, 0) >> 2) & 1
    flip = (odd * ids_ref[0]) == 1
    o_ref[...] = total * jnp.where(flip, -32.0, 32.0)


def final_mix(ids, received):
    rows, features = received.shape
    cols = 256
    return pl.pallas_call(
        final_kernel,
        grid=(features // cols,),
        out_shape=jax.ShapeDtypeStruct((rows, features), f32),
        in_specs=[
            SMEM,
            pl.BlockSpec((rows, rows), lambda g: (0, 0)),
            pl.BlockSpec((rows, cols), lambda g: (0, g)),
        ],
        out_specs=pl.BlockSpec((rows, cols), lambda g: (0, g)),
        compiler_params=params(),
    )(ids, jnp.asarray(final_table()), received)


def lane_splat(x, lane):
    return jnp.broadcast_to(x[:, lane : lane + 1], (8, NB))


def thirds(x):
    high = x.astype(bf16).astype(f32)
    rest = x - high
    middle = rest.astype(bf16).astype(f32)
    return high, middle, rest - middle


def outer_sum(left, right):
    lh, lm, ll = thirds(left)
    rh, rm, rl = thirds(right)
    stacked_left = jnp.concatenate([lh, lh, lh, lm, lm, ll], axis=0).astype(bf16)
    stacked_right = jnp.concatenate([rh, rm, rl, rh, rm, rh], axis=0).astype(bf16)
    return tmm(stacked_left, stacked_right)


def tree_sum(terms):
    while len(terms) > 1:
        terms = [x + y for x, y in zip(terms[::2], terms[1::2])]
    return terms[0]


def factor_block(w, upper, inverse):
    lane = lax.broadcasted_iota(jnp.int32, (8, NB), 1)
    sub = lax.broadcasted_iota(jnp.int32, (8, NB), 0)
    pairs = [(a, b) for a in range(8) for b in range(a, 8)]

    def row_splat(row):
        return jnp.broadcast_to(w[row : row + 1, :], (8, NB))

    rho = [row_splat(b) for b in range(8)]
    e = {(a, b): lane_splat(rho[a], b) for a, b in pairs}
    for step in range(16):
        base = 8 * step
        inside = (lane >= base) & (lane < base + 8)
        aug = [jnp.where(inside, jnp.where(lane == base + b, 1.0, 0.0), rho[b]) for b in range(8)]
        u, t = [None] * 8, [None] * 8
        for b in range(8):
            r = lax.rsqrt(e[b, b])
            u[b], t[b] = rho[b] * r, aug[b] * r
            c = {a: e[b, a] * r for a in range(b + 1, 8)}
            for a in range(b + 1, 8):
                for a2 in range(a, 8):
                    e[a, a2] = e[a, a2] - c[a] * c[a2]
            for a in range(b + 1, 8):
                rho[a] = rho[a] - c[a] * u[b]
                aug[a] = aug[a] - c[a] * t[b]
        left, right = u[0], t[0]
        for b in range(1, 8):
            left = jnp.where(sub == b, u[b], left)
            right = jnp.where(sub == b, t[b], right)
        upper[base : base + 8, :] = jnp.where(lane >= base + sub, left, 0.0)
        inverse[base : base + 8, :] = jnp.where(lane <= base + sub, right, 0.0)
        if step == 15:
            break
        if step < 14:
            update = outer_sum(left, right)
        coming = [jnp.where(inside, 0.0, row_splat(base + 8 + a)) for a in range(8)]
        c = {(b, a): lane_splat(u[b], base + 8 + a) for b in range(8) for a in range(8)}
        e = {(a, a2): lane_splat(coming[a], base + 8 + a2) for a, a2 in pairs}
        e = {(a, a2): e[a, a2] - tree_sum([c[b, a] * c[b, a2] for b in range(8)]) for a, a2 in pairs}
        rho = [coming[a] - tree_sum([c[b, a] * t[b] for b in range(8)]) for a in range(8)]
        if step < 14:
            after = base + 16
            rest = lax.broadcasted_iota(jnp.int32, (NB - after, NB), 1)
            cleared = jnp.where((rest >= base) & (rest < base + 8), 0.0, w[after:, :])
            w[after:, :] = cleared - update[after:, :]


def place(ref, slot, a, strip, block, ridge_ref):
    piece = ref[NB * slot : NB * slot + NB, :]
    if ridge_ref is not None and strip == block:
        rows = lax.broadcasted_iota(jnp.int32, (NB, NB), 0)
        cols = lax.broadcasted_iota(jnp.int32, (NB, NB), 1)
        piece = piece + jnp.where(rows == cols, ridge_ref[0:1, NB * strip : NB * strip + NB], 0.0)
    a[NB * strip : NB * strip + NB, NB * block : NB * block + NB] = piece


def highest(left, right, contract):
    return lax.dot_general(
        left, right, ((contract, (0,)), ((), ())), precision=precise, preferred_element_type=f32
    )


def panels(a, w, upper, inverse, first, last, inv_ref=None):
    count = HALF // NB

    def body(panel, carry):
        at = pl.multiple_of(panel * NB, NB)
        w[...] = a[pl.ds(at, NB), pl.ds(at, NB)]
        factor_block(w, upper, inverse)
        if inv_ref is not None:
            inv_ref[panel - first] = inverse[...]
        for fixed in range(first, last):

            @pl.when(panel == fixed)
            def _():
                s0, s1 = NB * fixed, NB * fixed + NB
                a[s0:s1, s0:s1] = upper[...]
                if fixed < count - 1:
                    rows = highest(inverse[...], a[s0:s1, s1:], (1,))
                    a[s0:s1, s1:] = rows
                    for strip in range(fixed + 1, count):
                        b0, t0 = NB * (strip - fixed - 1), NB * strip
                        update = highest(rows[:, b0 : b0 + NB], rows[:, b0:], (0,))
                        a[t0 : t0 + NB, t0:] = a[t0 : t0 + NB, t0:] - update

        return carry

    lax.fori_loop(first, last, body, 0)


def first_factor_kernel(ids_ref, ridge_ref, own_rel, other_rel, a, inv_ref, own_ref, other_ref, w, upper, inverse):
    for back_x in range(4):
        for back_y in range(4):
            source = 160 * back_x + 40 * back_y
            row = turn(ids_ref[2], 4 - back_x) * 160 + turn(ids_ref[3], 4 - back_y) * 40
            target = pl.ds(pl.multiple_of(row, 8), 40)
            own_ref[target, :] = own_rel[source : source + 40, :]
            other_ref[target, :] = other_rel[source : source + 40, :]
    for which in range(2):

        @pl.when(ids_ref[0] == which)
        def _():
            for ref, strips in ((own_ref, PAIRS[which]), (other_ref, PAIRS[1 - which])):
                slot = 0
                for strip in strips:
                    for block in range(strip, 4):
                        place(ref, slot, a, strip, block, ridge_ref)
                        slot += 1

    panels(a, w, upper, inverse, 0, 2, inv_ref)


def middle_factor_kernel(given_ref, a, inv_ref, w, upper, inverse):
    a[...] = given_ref[...]
    panels(a, w, upper, inverse, 2, 4, inv_ref)


def last_factor_kernel(ids_ref, ridge_ref, own_ref, other_ref, u_ref, inv1_ref, inv2_ref, o_ref, r, a, w, upper, inverse):
    position = ids_ref[1]
    for which in range(2):

        @pl.when(ids_ref[0] == which)
        def _():
            for ref, strips in ((own_ref, PAIRS[which]), (other_ref, PAIRS[1 - which])):
                slot = 0
                for strip in strips:
                    for block in range(4):
                        place(ref, slot, r, strip, block, None)
                        slot += 1
                for strip in strips:
                    for block in range(strip, 4):
                        place(ref, slot, a, strip, block, ridge_ref)
                        slot += 1

    for panel in range(4):
        at = NB * panel
        rows = r[at : at + NB, :]
        if panel:
            rows = rows - highest(u_ref[:at, at : at + NB], r[:at, :], (0,))
        inv_ref = (inv1_ref, inv2_ref)[panel // 2]
        r[at : at + NB, :] = highest(inv_ref[panel % 2], rows, (1,))
    for strip in range(4):
        at = NB * strip
        update = highest(r[:, at : at + NB], r[:, at:], (0,))
        a[at : at + NB, at:] = a[at : at + NB, at:] - update
    panels(a, w, upper, inverse, 0, 4)
    lane = lax.broadcasted_iota(jnp.int32, (8, HALF), 1)
    row = pl.multiple_of((position % 64) * 8, 8)
    edge = ((position % 64) // 16) * NB

    @pl.when(position < 64)
    def _():
        o_ref[:, :HALF] = jnp.where(lane >= edge, u_ref[pl.ds(row, 8), :], 0.0)
        o_ref[:, HALF:] = r[pl.ds(row, 8), :]

    @pl.when(position >= 64)
    def _():
        o_ref[:, :HALF] = jnp.zeros((8, HALF), f32)
        o_ref[:, HALF:] = jnp.where(lane >= edge, a[pl.ds(row, 8), :], 0.0)


BLOCK_SCRATCH = [pltpu.VMEM((NB, NB), f32)] * 3
SQUARE = jax.ShapeDtypeStruct((HALF, HALF), f32)
INVERSES = jax.ShapeDtypeStruct((2, NB, NB), f32)


def cost(us):
    return pl.CostEstimate(flops=us * 1_000_000_000, bytes_accessed=2 << 20, transcendentals=0)


def first_factor(ids, ridge, own, other):
    return pl.pallas_call(
        first_factor_kernel,
        out_shape=(SQUARE, INVERSES),
        in_specs=[SMEM, VMEM, VMEM, VMEM],
        out_specs=(VMEM, VMEM),
        scratch_shapes=[pltpu.VMEM((5 * NB, NB), f32)] * 2 + BLOCK_SCRATCH,
        compiler_params=params(),
        cost_estimate=cost(12),
    )(ids, ridge, own, other)


def middle_factor(given):
    return pl.pallas_call(
        middle_factor_kernel,
        out_shape=(SQUARE, INVERSES),
        in_specs=[VMEM],
        out_specs=(VMEM, VMEM),
        scratch_shapes=BLOCK_SCRATCH,
        compiler_params=params(),
        cost_estimate=cost(12),
    )(given)


def last_factor(ids, ridge, own, other, u, inv1, inv2):
    return pl.pallas_call(
        last_factor_kernel,
        out_shape=jax.ShapeDtypeStruct((8, FEAT), f32),
        in_specs=[SMEM] + [VMEM] * 6,
        out_specs=VMEM,
        scratch_shapes=[pltpu.VMEM((HALF, HALF), f32)] * 2 + BLOCK_SCRATCH,
        compiler_params=params(),
        cost_estimate=cost(30),
    )(ids, ridge, own, other, u, inv1, inv2)


def swap_cores(x):
    return lax.ppermute(x, "outer", [(0, 1), (1, 0)])


def along(axis, x, distance):
    stride = {"x": 1, "y": 4, "z": 16}[axis]
    pairs = []
    for source in range(64):
        digit = source // stride % 4
        pairs.append((source, source + ((digit + distance) % 4 - digit) * stride))
    return lax.ppermute(x, "inner", pairs)


def exchange(axis, parts):
    return [parts[0]] + [along(axis, parts[step], step) for step in (1, 3, 2)]


def in_order(parts):
    return [parts[0], parts[1], parts[3], parts[2]]


def shared(axis, x):
    return in_order(exchange(axis, [x] * 4))


def scattered(axis, parts):
    return in_order(exchange(axis, parts))


def total(parts):
    return (parts[0] + parts[2]) + (parts[1] + parts[3])


def plane_exchange(x):
    return lax.all_to_all(x, "inner", 0, 0, axis_index_groups=PLANES, tiled=True)


def copies(piece):
    return jnp.broadcast_to(piece[None], (16,) + piece.shape)


def local(matrix, sign_flip, keep_list, ridge_weights):
    core, inner = lax.axis_index("outer"), lax.axis_index("inner")
    ids = jnp.stack([core, core * 64 + inner, inner & 3, (inner >> 2) & 3, inner >> 4]).astype(jnp.int32)
    keep_here = lax.dynamic_index_in_dim(keep_list.reshape(2, 4, 16, 2), inner >> 4, 1, False)
    keep_rows = jnp.repeat(keep_here.reshape(32, 2), 4, axis=0)
    table, signs = jnp.asarray(local_table()), sign_flip.reshape(1, -1)
    ridge = ridge_weights.reshape(1, FEAT)

    along1 = scattered("z", local_mix(ids, table, signs, matrix, 0))
    mixed2 = local_mix(ids, table, signs, matrix, 1)
    along1, mixed2 = lax.optimization_barrier((along1, mixed2))
    along2 = scattered("z", mixed2)
    mine1 = select_rows(ids, keep_rows, along1).reshape(256, HALF)
    theirs1 = swap_cores(mine1)
    by_y = sum_split(ids, scattered("x", first_gram(ids, mine1, theirs1)))
    piece1 = total(scattered("y", by_y))
    piece1 = total(shared("z", piece1))
    row1 = jnp.concatenate(shared("y", piece1), axis=0)
    own1 = jnp.concatenate(shared("x", row1), axis=0)
    other1 = swap_cores(own1)

    mine2 = select_rows(ids, keep_rows, along2).reshape(256, HALF)
    theirs2 = swap_cores(mine2)
    gram2, to_send = second_gram(ids, mine1, theirs1, mine2, theirs2)
    piece2 = jnp.sum(plane_exchange(gram2.reshape(16, 104, 128)), axis=0)
    piece2 = total(shared("z", piece2))
    own2 = plane_exchange(copies(piece2)).reshape(13 * NB, NB)

    u, inv1 = first_factor(ids, ridge[:, :HALF], own1, other1)
    u, inv2 = middle_factor(u)
    other2 = swap_cores(own2)
    to_send, own2, other2 = lax.optimization_barrier((to_send, own2, other2))
    received = plane_exchange(to_send)
    factor = last_factor(ids, ridge[:, HALF:], own2, other2, u, inv1, inv2)
    sketch = final_mix(ids, received.reshape(256, FEAT))
    return sketch, factor


def solution(mesh):
    return jax.shard_map(
        local,
        mesh=mesh,
        in_specs=(P(("outer", "inner"), None), P(("outer", "inner")), P(), P()),
        out_specs=(P(("outer", "inner"), None), P(("outer", "inner"), None)),
        check_vma=False,
    )
```

```python
import jax
import jax.numpy as jnp
import numpy as np
from jax import lax
from jax.experimental import pallas as pl
from jax.experimental.pallas import tpu as pltpu
from jax.sharding import PartitionSpec as P

precise = lax.Precision.HIGHEST
f32 = jnp.float32
bf16 = jnp.bfloat16
VMEM = pl.BlockSpec(memory_space=pltpu.VMEM)
SMEM = pl.BlockSpec(memory_space=pltpu.SMEM)
FEAT = 1024
NB = 128
HALF = FEAT // 2
PAIRS = ((0, 3), (1, 2))
Z_GROUPS = [[i + 16 * j for j in range(4)] for i in range(16)]
PLANES = [[16 * j + i for i in range(16)] for j in range(4)]


def params(mib=60):
    return pltpu.CompilerParams(vmem_limit_bytes=mib << 20)


def parity_sign(left, right):
    common = left & right
    parity = np.zeros_like(common)
    for shift_by in range(10):
        parity ^= (common >> shift_by) & 1
    return 1 - 2 * parity


def local_table():
    az, c, axy, e = np.meshgrid(range(4), range(2), range(16), range(4), indexing="ij")
    k = (az * 128 + axy * 8 + c * 4 + e).reshape(-1, 1)
    return parity_sign(k, np.arange(512)[None, :]).astype(np.float32).astype(bf16)


def final_table():
    j, i, o, e = (v.reshape(-1, 1) for v in np.meshgrid(range(2), range(16), range(2), range(4), indexing="ij"))
    ip, op, jp, ep = (v.reshape(1, -1) for v in np.meshgrid(range(16), range(2), range(2), range(4), indexing="ij"))
    table = parity_sign(i, ip) * parity_sign(o, op) * (j == jp) * (e == ep)
    return table.astype(np.float32).astype(bf16)


def halves(x):
    high = x.astype(bf16)
    return high, (x - high.astype(f32)).astype(bf16)


def mm(a, b):
    return jnp.dot(a, b, preferred_element_type=f32)


def tmm(a, b):
    return lax.dot_general(a, b, (((0,), (0,)), ((), ())), preferred_element_type=f32)


def local_mix_kernel(table_ref, sign_ref, x_ref, o_ref, signed):
    @pl.when(pl.program_id(0) == 0)
    def _():
        signed[...] = (table_ref[...].astype(f32) * (sign_ref[...].astype(f32) * 2.0**-13)).astype(bf16)

    high, low = halves(x_ref[...])
    o_ref[...] = mm(signed[...], high) + mm(signed[...], low)


def local_mix(matrix, sign_flip):
    rows, features = matrix.shape
    cols = 256
    return pl.pallas_call(
        local_mix_kernel,
        grid=(features // cols,),
        out_shape=jax.ShapeDtypeStruct((rows, features), f32),
        in_specs=[
            pl.BlockSpec((rows, rows), lambda g: (0, 0)),
            pl.BlockSpec((1, rows), lambda g: (0, 0)),
            pl.BlockSpec((rows, cols), lambda g: (0, g)),
        ],
        out_specs=pl.BlockSpec((rows, cols), lambda g: (0, g)),
        scratch_shapes=[pltpu.VMEM((rows, rows), bf16)],
        compiler_params=params(60),
    )(jnp.asarray(local_table()), sign_flip.reshape(1, rows), matrix)


def select_kernel(keep_ref, y_ref, v_ref):
    y0, y1, y2, y3 = (y_ref[z] for z in range(4))
    s, d, s2, d2 = y0 + y1, y0 - y1, y2 + y3, y2 - y3

    def combo(which):
        low = (which & 1) == 1
        first = jnp.where(low, d, s)
        second = jnp.where(low, d2, s2)
        return first + jnp.where((which & 2) == 2, -second, second)

    shape = s.shape
    v0 = combo(jnp.broadcast_to(keep_ref[:, 0:1], shape))
    v1 = combo(jnp.broadcast_to(keep_ref[:, 1:2], shape))
    upper = (lax.broadcasted_iota(jnp.int32, shape, 0) & 7) < 4
    even = jnp.where(upper, v0, pltpu.roll(v1, 4, axis=0))
    odd = jnp.where(upper, pltpu.roll(v0, shape[0] - 4, axis=0), v1)
    v_ref[:, 0] = even.reshape(16, 8, shape[1])
    v_ref[:, 1] = odd.reshape(16, 8, shape[1])


def select_rows(keep_rows, y):
    cols = 256
    features = y.shape[2]
    return pl.pallas_call(
        select_kernel,
        grid=(features // cols,),
        out_shape=jax.ShapeDtypeStruct((16, 2, 8, features), f32),
        in_specs=[
            pl.BlockSpec((128, 2), lambda g: (0, 0)),
            pl.BlockSpec((4, 128, cols), lambda g: (0, 0, g)),
        ],
        out_specs=pl.BlockSpec((16, 2, 8, cols), lambda g: (0, 0, 0, g)),
        compiler_params=params(60),
    )(keep_rows, y)


def gram_kernel(ids_ref, v_ref, w_ref, g_ref, s_ref, high, low, first, second):
    own = pl.ds(pl.multiple_of(ids_ref[0] * 128, 128), 128)
    for part, ref in enumerate((v_ref, w_ref)):
        h, l = halves(ref[...])
        high[256 * part : 256 * part + 256, :] = h
        low[256 * part : 256 * part + 256, :] = l
        s_ref[:, part] = ref[own, :].reshape(16, 8, FEAT)

    def strip_sum(strip):
        at = NB * strip
        h, l = high[:, at : at + NB], low[:, at : at + NB]
        return tmm(h, high[:, at:]) + (tmm(h, low[:, at:]) + tmm(l, high[:, at:]))

    def store(target, slot, value):
        for block in range(value.shape[1] // NB):
            row = NB * (slot + block)
            target[row : row + NB, :] = value[:, NB * block : NB * block + NB]
        return slot + value.shape[1] // NB

    for which, strips in enumerate(PAIRS):

        @pl.when(ids_ref[0] == which)
        def _():
            slot1 = slot2 = 0
            for strip in strips:
                value = strip_sum(strip)
                edge = HALF - NB * strip
                slot1 = store(first, slot1, value[:, :edge])
                slot2 = store(second, slot2, value[:, edge:])
            for strip in strips:
                slot2 = store(second, slot2, strip_sum(strip + 4))

    for piece in range(16):
        g_ref[piece, :40] = first[40 * piece : 40 * piece + 40, :]
        g_ref[piece, 40:] = second[104 * piece : 104 * piece + 104, :]


def gram_half(ids, mine, theirs):
    rows = mine.shape[0]
    return pl.pallas_call(
        gram_kernel,
        out_shape=(
            jax.ShapeDtypeStruct((16, 144, NB), f32),
            jax.ShapeDtypeStruct((16, 2, 8, FEAT), f32),
        ),
        in_specs=[SMEM, VMEM, VMEM],
        out_specs=(VMEM, VMEM),
        scratch_shapes=[pltpu.VMEM((2 * rows, FEAT), bf16)] * 2
        + [pltpu.VMEM((5 * NB, NB), f32), pltpu.VMEM((13 * NB, NB), f32)],
        compiler_params=params(),
    )(ids, mine, theirs)


def final_kernel(ids_ref, table_ref, r_ref, o_ref):
    high, low = halves(r_ref[...])
    total = mm(table_ref[...], high) + mm(table_ref[...], low)
    odd = (lax.broadcasted_iota(jnp.int32, total.shape, 0) >> 2) & 1
    flip = (odd * ids_ref[0]) == 1
    o_ref[...] = total * jnp.where(flip, -32.0, 32.0)


def final_mix(ids, received):
    rows, features = received.shape
    cols = 256
    return pl.pallas_call(
        final_kernel,
        grid=(features // cols,),
        out_shape=jax.ShapeDtypeStruct((rows, features), f32),
        in_specs=[
            SMEM,
            pl.BlockSpec((rows, rows), lambda g: (0, 0)),
            pl.BlockSpec((rows, cols), lambda g: (0, g)),
        ],
        out_specs=pl.BlockSpec((rows, cols), lambda g: (0, g)),
        compiler_params=params(),
    )(ids, jnp.asarray(final_table()), received)


def lane_splat(x, lane):
    return jnp.broadcast_to(x[:, lane : lane + 1], (8, NB))


def thirds(x):
    high = x.astype(bf16).astype(f32)
    rest = x - high
    middle = rest.astype(bf16).astype(f32)
    return high, middle, rest - middle


def outer_sum(left, right):
    lh, lm, ll = thirds(left)
    rh, rm, rl = thirds(right)
    stacked_left = jnp.concatenate([lh, lh, lh, lm, lm, ll], axis=0).astype(bf16)
    stacked_right = jnp.concatenate([rh, rm, rl, rh, rm, rh], axis=0).astype(bf16)
    return tmm(stacked_left, stacked_right)


def tree_sum(terms):
    while len(terms) > 1:
        terms = [x + y for x, y in zip(terms[::2], terms[1::2])]
    return terms[0]


def factor_block(w, upper, inverse):
    lane = lax.broadcasted_iota(jnp.int32, (8, NB), 1)
    sub = lax.broadcasted_iota(jnp.int32, (8, NB), 0)
    pairs = [(a, b) for a in range(8) for b in range(a, 8)]

    def row_splat(row):
        return jnp.broadcast_to(w[row : row + 1, :], (8, NB))

    rho = [row_splat(b) for b in range(8)]
    e = {(a, b): lane_splat(rho[a], b) for a, b in pairs}
    for step in range(16):
        base = 8 * step
        inside = (lane >= base) & (lane < base + 8)
        aug = [jnp.where(inside, jnp.where(lane == base + b, 1.0, 0.0), rho[b]) for b in range(8)]
        u, t = [None] * 8, [None] * 8
        for b in range(8):
            r = lax.rsqrt(e[b, b])
            u[b], t[b] = rho[b] * r, aug[b] * r
            c = {a: e[b, a] * r for a in range(b + 1, 8)}
            for a in range(b + 1, 8):
                for a2 in range(a, 8):
                    e[a, a2] = e[a, a2] - c[a] * c[a2]
            for a in range(b + 1, 8):
                rho[a] = rho[a] - c[a] * u[b]
                aug[a] = aug[a] - c[a] * t[b]
        left, right = u[0], t[0]
        for b in range(1, 8):
            left = jnp.where(sub == b, u[b], left)
            right = jnp.where(sub == b, t[b], right)
        upper[base : base + 8, :] = jnp.where(lane >= base + sub, left, 0.0)
        inverse[base : base + 8, :] = jnp.where(lane <= base + sub, right, 0.0)
        if step == 15:
            break
        if step < 14:
            update = outer_sum(left, right)
        coming = [jnp.where(inside, 0.0, row_splat(base + 8 + a)) for a in range(8)]
        c = {(b, a): lane_splat(u[b], base + 8 + a) for b in range(8) for a in range(8)}
        e = {(a, a2): lane_splat(coming[a], base + 8 + a2) for a, a2 in pairs}
        e = {(a, a2): e[a, a2] - tree_sum([c[b, a] * c[b, a2] for b in range(8)]) for a, a2 in pairs}
        rho = [coming[a] - tree_sum([c[b, a] * t[b] for b in range(8)]) for a in range(8)]
        if step < 14:
            after = base + 16
            rest = lax.broadcasted_iota(jnp.int32, (NB - after, NB), 1)
            cleared = jnp.where((rest >= base) & (rest < base + 8), 0.0, w[after:, :])
            w[after:, :] = cleared - update[after:, :]


def place(ref, slot, a, strip, block, ridge_ref):
    piece = ref[NB * slot : NB * slot + NB, :]
    if ridge_ref is not None and strip == block:
        rows = lax.broadcasted_iota(jnp.int32, (NB, NB), 0)
        cols = lax.broadcasted_iota(jnp.int32, (NB, NB), 1)
        piece = piece + jnp.where(rows == cols, ridge_ref[0:1, NB * strip : NB * strip + NB], 0.0)
    a[NB * strip : NB * strip + NB, NB * block : NB * block + NB] = piece


def highest(left, right, contract):
    return lax.dot_general(
        left, right, ((contract, (0,)), ((), ())), precision=precise, preferred_element_type=f32
    )


def panels(a, w, upper, inverse, first, last, inv_ref=None):
    count = HALF // NB

    def body(panel, carry):
        at = pl.multiple_of(panel * NB, NB)
        w[...] = a[pl.ds(at, NB), pl.ds(at, NB)]
        factor_block(w, upper, inverse)
        if inv_ref is not None:
            inv_ref[panel - first] = inverse[...]
        for fixed in range(first, last):

            @pl.when(panel == fixed)
            def _():
                s0, s1 = NB * fixed, NB * fixed + NB
                a[s0:s1, s0:s1] = upper[...]
                if fixed < count - 1:
                    rows = highest(inverse[...], a[s0:s1, s1:], (1,))
                    a[s0:s1, s1:] = rows
                    for strip in range(fixed + 1, count):
                        b0, t0 = NB * (strip - fixed - 1), NB * strip
                        update = highest(rows[:, b0 : b0 + NB], rows[:, b0:], (0,))
                        a[t0 : t0 + NB, t0:] = a[t0 : t0 + NB, t0:] - update

        return carry

    lax.fori_loop(first, last, body, 0)


def first_factor_kernel(ids_ref, ridge_ref, own_ref, other_ref, a, inv_ref, w, upper, inverse):
    for which in range(2):

        @pl.when(ids_ref[0] == which)
        def _():
            for ref, strips in ((own_ref, PAIRS[which]), (other_ref, PAIRS[1 - which])):
                slot = 0
                for strip in strips:
                    for block in range(strip, 4):
                        place(ref, slot, a, strip, block, ridge_ref)
                        slot += 1

    panels(a, w, upper, inverse, 0, 2, inv_ref)


def middle_factor_kernel(given_ref, a, inv_ref, w, upper, inverse):
    a[...] = given_ref[...]
    panels(a, w, upper, inverse, 2, 4, inv_ref)


def last_factor_kernel(ids_ref, ridge_ref, own_ref, other_ref, u_ref, inv1_ref, inv2_ref, o_ref, r, a, w, upper, inverse):
    position = ids_ref[1]
    for which in range(2):

        @pl.when(ids_ref[0] == which)
        def _():
            for ref, strips in ((own_ref, PAIRS[which]), (other_ref, PAIRS[1 - which])):
                slot = 0
                for strip in strips:
                    for block in range(4):
                        place(ref, slot, r, strip, block, None)
                        slot += 1
                for strip in strips:
                    for block in range(strip, 4):
                        place(ref, slot, a, strip, block, ridge_ref)
                        slot += 1

    for panel in range(4):
        at = NB * panel
        rows = r[at : at + NB, :]
        if panel:
            rows = rows - highest(u_ref[:at, at : at + NB], r[:at, :], (0,))
        inv_ref = (inv1_ref, inv2_ref)[panel // 2]
        r[at : at + NB, :] = highest(inv_ref[panel % 2], rows, (1,))
    for strip in range(4):
        at = NB * strip
        update = highest(r[:, at : at + NB], r[:, at:], (0,))
        a[at : at + NB, at:] = a[at : at + NB, at:] - update
    panels(a, w, upper, inverse, 0, 4)
    lane = lax.broadcasted_iota(jnp.int32, (8, HALF), 1)
    row = pl.multiple_of((position % 64) * 8, 8)
    edge = ((position % 64) // 16) * NB

    @pl.when(position < 64)
    def _():
        o_ref[:, :HALF] = jnp.where(lane >= edge, u_ref[pl.ds(row, 8), :], 0.0)
        o_ref[:, HALF:] = r[pl.ds(row, 8), :]

    @pl.when(position >= 64)
    def _():
        o_ref[:, :HALF] = jnp.zeros((8, HALF), f32)
        o_ref[:, HALF:] = jnp.where(lane >= edge, a[pl.ds(row, 8), :], 0.0)


BLOCK_SCRATCH = [pltpu.VMEM((NB, NB), f32)] * 3
SQUARE = jax.ShapeDtypeStruct((HALF, HALF), f32)
INVERSES = jax.ShapeDtypeStruct((2, NB, NB), f32)


def cost(us):
    return pl.CostEstimate(flops=us * 1_000_000_000, bytes_accessed=2 << 20, transcendentals=0)


def first_factor(ids, ridge, own, other):
    return pl.pallas_call(
        first_factor_kernel,
        out_shape=(SQUARE, INVERSES),
        in_specs=[SMEM, VMEM, VMEM, VMEM],
        out_specs=(VMEM, VMEM),
        scratch_shapes=BLOCK_SCRATCH,
        compiler_params=params(),
        cost_estimate=cost(12),
    )(ids, ridge, own, other)


def middle_factor(given):
    return pl.pallas_call(
        middle_factor_kernel,
        out_shape=(SQUARE, INVERSES),
        in_specs=[VMEM],
        out_specs=(VMEM, VMEM),
        scratch_shapes=BLOCK_SCRATCH,
        compiler_params=params(),
        cost_estimate=cost(12),
    )(given)


def last_factor(ids, ridge, own, other, u, inv1, inv2):
    return pl.pallas_call(
        last_factor_kernel,
        out_shape=jax.ShapeDtypeStruct((8, FEAT), f32),
        in_specs=[SMEM] + [VMEM] * 6,
        out_specs=VMEM,
        scratch_shapes=[pltpu.VMEM((HALF, HALF), f32)] * 2 + BLOCK_SCRATCH,
        compiler_params=params(),
        cost_estimate=cost(30),
    )(ids, ridge, own, other, u, inv1, inv2)


def swap_cores(x):
    return lax.ppermute(x, "outer", [(0, 1), (1, 0)])


def along_z(x, distance):
    return lax.ppermute(x, "inner", [(i, (i + 16 * distance) % 64) for i in range(64)])


def plane_exchange(x):
    return lax.all_to_all(x, "inner", 0, 0, axis_index_groups=PLANES, tiled=True)


def copies(piece):
    return jnp.broadcast_to(piece[None], (16,) + piece.shape)


def local(matrix, sign_flip, keep_list, ridge_weights):
    core, inner = lax.axis_index("outer"), lax.axis_index("inner")
    ids = jnp.stack([core, core * 64 + inner]).astype(jnp.int32)
    keep_here = lax.dynamic_index_in_dim(keep_list.reshape(2, 4, 16, 2), inner >> 4, 1, False)
    keep_rows = jnp.repeat(keep_here.reshape(32, 2), 4, axis=0)
    ridge = ridge_weights.reshape(1, FEAT)

    mixed = local_mix(matrix, sign_flip)
    along = lax.all_to_all(
        mixed.reshape(4, 128, FEAT), "inner", 0, 0, axis_index_groups=Z_GROUPS, tiled=True
    )
    mine = select_rows(keep_rows, along).reshape(256, FEAT)
    theirs = swap_cores(mine)
    gram, to_send = gram_half(ids, mine, theirs)
    piece = jnp.sum(plane_exchange(gram), axis=0)
    piece = (piece + along_z(piece, 2)) + (along_z(piece, 1) + along_z(piece, 3))
    own1 = plane_exchange(copies(piece[:40]))
    later, own1 = lax.optimization_barrier((copies(piece[40:]), own1))
    own1 = own1.reshape(5 * NB, NB)
    own2 = plane_exchange(later).reshape(13 * NB, NB)
    other1 = swap_cores(own1)
    u, inv1 = first_factor(ids, ridge[:, :HALF], own1, other1)
    u, inv2 = middle_factor(u)
    other2 = swap_cores(own2)
    to_send, own2, other2 = lax.optimization_barrier((to_send, own2, other2))
    received = plane_exchange(to_send)
    factor = last_factor(ids, ridge[:, HALF:], own2, other2, u, inv1, inv2)
    sketch = final_mix(ids, received.reshape(256, FEAT))
    return sketch, factor


def solution(mesh):
    return jax.shard_map(
        local,
        mesh=mesh,
        in_specs=(P(("outer", "inner"), None), P(("outer", "inner")), P(), P()),
        out_specs=(P(("outer", "inner"), None), P(("outer", "inner"), None)),
        check_vma=False,
    )
```

```python
import jax
import jax.numpy as jnp
import numpy as np
from jax import lax
from jax.experimental import pallas as pl
from jax.experimental.pallas import tpu as pltpu
from jax.sharding import PartitionSpec as P

f32 = jnp.float32
bf16 = jnp.bfloat16
VMEM = pl.BlockSpec(memory_space=pltpu.VMEM)
SMEM = pl.BlockSpec(memory_space=pltpu.SMEM)
FEAT = 1024
NB = 128
PANELS = FEAT // NB
STRIPS = ((0, 3, 4, 7), (1, 2, 5, 6))
GRAM_ROWS = 144
LEFT = (0, 0, 0, 1, 1, 2)
RIGHT = (0, 1, 2, 0, 1, 0)
Z_GROUPS = [[i + 16 * j for j in range(4)] for i in range(16)]
PLANES = [[16 * j + i for i in range(16)] for j in range(4)]


def params(mib=32):
    return pltpu.CompilerParams(vmem_limit_bytes=mib << 20)


def parity_sign(left, right):
    common = left & right
    parity = np.zeros_like(common)
    for shift_by in range(10):
        parity ^= (common >> shift_by) & 1
    return 1 - 2 * parity


def local_table():
    az, c, axy, e = np.meshgrid(range(4), range(2), range(16), range(4), indexing="ij")
    k = (az * 128 + axy * 8 + c * 4 + e).reshape(-1, 1)
    return parity_sign(k, np.arange(512)[None, :]).astype(np.float32).astype(bf16)


def final_table():
    j, i, o, e = (v.reshape(-1, 1) for v in np.meshgrid(range(2), range(16), range(2), range(4), indexing="ij"))
    op, ip, jp, ep = (v.reshape(1, -1) for v in np.meshgrid(range(2), range(16), range(2), range(4), indexing="ij"))
    table = parity_sign(i, ip) * parity_sign(o, op) * (j == jp) * (e == ep)
    return table.astype(np.float32).astype(bf16)


def halves(x):
    high = x.astype(bf16)
    return high, (x - high.astype(f32)).astype(bf16)


def mm(a, b):
    return jnp.dot(a, b, preferred_element_type=f32)


def tmm(a, b):
    return lax.dot_general(a, b, (((0,), (0,)), ((), ())), preferred_element_type=f32)


def local_mix_kernel(table_ref, sign_ref, x_ref, o_ref, signed):
    @pl.when(pl.program_id(0) == 0)
    def _():
        signed[...] = (table_ref[...].astype(f32) * (sign_ref[...].astype(f32) * 2.0**-13)).astype(bf16)

    high, low = halves(x_ref[...])
    o_ref[...] = mm(signed[...], high) + mm(signed[...], low)


def local_mix(matrix, sign_flip):
    rows, features = matrix.shape
    cols = 256
    return pl.pallas_call(
        local_mix_kernel,
        grid=(features // cols,),
        out_shape=jax.ShapeDtypeStruct((rows, features), f32),
        in_specs=[
            pl.BlockSpec((rows, rows), lambda g: (0, 0)),
            pl.BlockSpec((1, rows), lambda g: (0, 0)),
            pl.BlockSpec((rows, cols), lambda g: (0, g)),
        ],
        out_specs=pl.BlockSpec((rows, cols), lambda g: (0, g)),
        scratch_shapes=[pltpu.VMEM((rows, rows), bf16)],
        compiler_params=params(60),
    )(jnp.asarray(local_table()), sign_flip.reshape(1, rows), matrix)


def select_kernel(keep_ref, y_ref, v_ref):
    y0, y1, y2, y3 = (y_ref[z] for z in range(4))
    s, d, s2, d2 = y0 + y1, y0 - y1, y2 + y3, y2 - y3

    def combo(which):
        low = (which & 1) == 1
        first = jnp.where(low, d, s)
        second = jnp.where(low, d2, s2)
        return first + jnp.where((which & 2) == 2, -second, second)

    shape = s.shape
    v0 = combo(jnp.broadcast_to(keep_ref[:, 0:1], shape))
    v1 = combo(jnp.broadcast_to(keep_ref[:, 1:2], shape))
    upper = (lax.broadcasted_iota(jnp.int32, shape, 0) & 7) < 4
    even = jnp.where(upper, v0, pltpu.roll(v1, 4, axis=0))
    odd = jnp.where(upper, pltpu.roll(v0, shape[0] - 4, axis=0), v1)
    v_ref[:, 0] = even.reshape(16, 8, shape[1])
    v_ref[:, 1] = odd.reshape(16, 8, shape[1])


def select_rows(keep_rows, y):
    cols = 256
    features = y.shape[2]
    return pl.pallas_call(
        select_kernel,
        grid=(features // cols,),
        out_shape=jax.ShapeDtypeStruct((16, 2, 8, features), f32),
        in_specs=[
            pl.BlockSpec((128, 2), lambda g: (0, 0)),
            pl.BlockSpec((4, 128, cols), lambda g: (0, 0, g)),
        ],
        out_specs=pl.BlockSpec((16, 2, 8, cols), lambda g: (0, 0, 0, g)),
        compiler_params=params(),
    )(keep_rows, y)


def gram_kernel(ids_ref, v_ref, w_ref, g_ref, high, low, flat):
    core = ids_ref[0]
    own = pl.ds(pl.multiple_of(core * 128, 128), 128)
    for part, ref in enumerate((v_ref, w_ref)):
        h, l = halves(ref[...])
        high[256 * part : 256 * part + 256, :] = h
        low[256 * part : 256 * part + 256, :] = l
        rows = ref[own, :].reshape(16, 8, FEAT)
        for block in range(PANELS):
            at = GRAM_ROWS + 8 * (PANELS * part + block)
            g_ref[:, at : at + 8] = rows[:, :, NB * block : NB * block + NB]
    for which, strips in enumerate(STRIPS):

        @pl.when(core == which)
        def _():
            row = 0
            for strip in strips:
                at = NB * strip
                h, l = high[:, at : at + NB], low[:, at : at + NB]
                total = tmm(h, high[:, at:]) + (tmm(h, low[:, at:]) + tmm(l, high[:, at:]))
                for block in range(PANELS - strip):
                    flat[row : row + NB, :] = total[:, NB * block : NB * block + NB]
                    row += NB

    for piece in range(16):
        g_ref[piece, :GRAM_ROWS] = flat[GRAM_ROWS * piece : GRAM_ROWS * (piece + 1), :]


def gram_half(ids, mine, theirs):
    rows = mine.shape[0]
    return pl.pallas_call(
        gram_kernel,
        out_shape=jax.ShapeDtypeStruct((16, GRAM_ROWS + 128, NB), f32),
        in_specs=[SMEM, VMEM, VMEM],
        out_specs=VMEM,
        scratch_shapes=[pltpu.VMEM((2 * rows, FEAT), bf16)] * 2 + [pltpu.VMEM((16 * GRAM_ROWS, NB), f32)],
        compiler_params=params(),
    )(ids, mine, theirs)


def final_kernel(ids_ref, table_ref, r_ref, o_ref, high, low):
    for part in range(2):
        for block in range(PANELS):
            at = GRAM_ROWS + 8 * (PANELS * part + block)
            h, l = halves(r_ref[:, at : at + 8].reshape(128, NB))
            high[128 * part : 128 * part + 128, NB * block : NB * block + NB] = h
            low[128 * part : 128 * part + 128, NB * block : NB * block + NB] = l
    total = mm(table_ref[...], high[...]) + mm(table_ref[...], low[...])
    odd = (lax.broadcasted_iota(jnp.int32, total.shape, 0) >> 2) & 1
    flip = (odd * ids_ref[0]) == 1
    o_ref[...] = total * jnp.where(flip, -32.0, 32.0)


def final_mix(ids, received):
    rows = 256
    return pl.pallas_call(
        final_kernel,
        out_shape=jax.ShapeDtypeStruct((rows, FEAT), f32),
        in_specs=[SMEM, VMEM, VMEM],
        out_specs=VMEM,
        scratch_shapes=[pltpu.VMEM((rows, FEAT), bf16)] * 2,
        compiler_params=params(),
        cost_estimate=pl.CostEstimate(flops=2_000_000_000, bytes_accessed=4 << 20, transcendentals=0),
    )(ids, jnp.asarray(final_table()), received)


def lane_splat(x, lane):
    return jnp.broadcast_to(x[:, lane : lane + 1], (8, NB))


def thirds(x):
    high = x.astype(bf16).astype(f32)
    rest = x - high
    middle = rest.astype(bf16).astype(f32)
    return high, middle, rest - middle


def pieces3(x):
    return tuple(part.astype(bf16) for part in thirds(x))


def outer_sum(left, right):
    lh, lm, ll = thirds(left)
    rh, rm, rl = thirds(right)
    stacked_left = jnp.concatenate([lh, lh, lh, lm, lm, ll], axis=0).astype(bf16)
    stacked_right = jnp.concatenate([rh, rm, rl, rh, rm, rh], axis=0).astype(bf16)
    return tmm(stacked_left, stacked_right)


def tree_sum(terms):
    while len(terms) > 1:
        terms = [x + y for x, y in zip(terms[::2], terms[1::2])]
    return terms[0]


def factor_block(w, upper, inverse):
    lane = lax.broadcasted_iota(jnp.int32, (8, NB), 1)
    sub = lax.broadcasted_iota(jnp.int32, (8, NB), 0)
    pairs = [(a, b) for a in range(8) for b in range(a, 8)]

    def row_splat(row):
        return jnp.broadcast_to(w[row : row + 1, :], (8, NB))

    rho = [row_splat(b) for b in range(8)]
    e = {(a, b): lane_splat(rho[a], b) for a, b in pairs}
    for step in range(16):
        base = 8 * step
        inside = (lane >= base) & (lane < base + 8)
        aug = [jnp.where(inside, jnp.where(lane == base + b, 1.0, 0.0), rho[b]) for b in range(8)]
        u, t = [None] * 8, [None] * 8
        for b in range(8):
            r = lax.rsqrt(e[b, b])
            u[b], t[b] = rho[b] * r, aug[b] * r
            c = {a: e[b, a] * r for a in range(b + 1, 8)}
            for a in range(b + 1, 8):
                for a2 in range(a, 8):
                    e[a, a2] = e[a, a2] - c[a] * c[a2]
            for a in range(b + 1, 8):
                rho[a] = rho[a] - c[a] * u[b]
                aug[a] = aug[a] - c[a] * t[b]
        left, right = u[0], t[0]
        for b in range(1, 8):
            left = jnp.where(sub == b, u[b], left)
            right = jnp.where(sub == b, t[b], right)
        upper[base : base + 8, :] = jnp.where(lane >= base + sub, left, 0.0)
        inverse[base : base + 8, :] = jnp.where(lane <= base + sub, right, 0.0)
        if step == 15:
            break
        if step < 14:
            update = outer_sum(left, right)
        coming = [jnp.where(inside, 0.0, row_splat(base + 8 + a)) for a in range(8)]
        c = {(b, a): lane_splat(u[b], base + 8 + a) for b in range(8) for a in range(8)}
        e = {(a, a2): lane_splat(coming[a], base + 8 + a2) for a, a2 in pairs}
        e = {(a, a2): e[a, a2] - tree_sum([c[b, a] * c[b, a2] for b in range(8)]) for a, a2 in pairs}
        rho = [coming[a] - tree_sum([c[b, a] * t[b] for b in range(8)]) for a in range(8)]
        if step < 14:
            after = base + 16
            rest = lax.broadcasted_iota(jnp.int32, (NB - after, NB), 1)
            cleared = jnp.where((rest >= base) & (rest < base + 8), 0.0, w[after:, :])
            w[after:, :] = cleared - update[after:, :]


def factor_kernel(ids_ref, ridge_ref, own_ref, other_ref, o_ref, a, w, upper, inverse, stack1, stack2):
    core, position = ids_ref[0], ids_ref[1]
    eye = lax.broadcasted_iota(jnp.int32, (NB, NB), 0) == lax.broadcasted_iota(jnp.int32, (NB, NB), 1)
    for which in range(2):

        @pl.when(core == which)
        def _():
            for ref, strips in ((own_ref, STRIPS[which]), (other_ref, STRIPS[1 - which])):
                slot = 0
                for strip in strips:
                    for block in range(strip, PANELS):
                        piece = ref[NB * slot : NB * slot + NB, :]
                        if block == strip:
                            ridge = ridge_ref[0:1, NB * strip : NB * strip + NB]
                            piece = piece + jnp.where(eye, ridge, 0.0)
                        a[NB * strip : NB * strip + NB, NB * block : NB * block + NB] = piece
                        slot += 1

    def body(panel, carry):
        at = pl.multiple_of(panel * NB, NB)
        w[...] = a[pl.ds(at, NB), pl.ds(at, NB)]
        factor_block(w, upper, inverse)
        for fixed in range(PANELS):

            @pl.when(panel == fixed)
            def _():
                s0, s1 = NB * fixed, NB * fixed + NB
                a[s0:s1, s0:s1] = upper[...]
                if fixed < PANELS - 1:
                    inv, rest = pieces3(inverse[...]), pieces3(a[s0:s1, s1:])
                    rows = mm(
                        jnp.concatenate([inv[k] for k in LEFT], axis=1),
                        jnp.concatenate([rest[k] for k in RIGHT], axis=0),
                    )
                    a[s0:s1, s1:] = rows
                    width = FEAT - s1
                    parts = pieces3(rows)
                    for k in range(6):
                        stack1[NB * k : NB * k + NB, :width] = parts[LEFT[k]]
                        stack2[NB * k : NB * k + NB, :width] = parts[RIGHT[k]]
                    for strip in range(fixed + 1, PANELS):
                        b0, t0 = NB * (strip - fixed - 1), NB * strip
                        update = tmm(stack1[:, b0 : b0 + NB], stack2[:, b0:width])
                        a[t0 : t0 + NB, t0:] = a[t0 : t0 + NB, t0:] - update

        return carry

    lax.fori_loop(0, PANELS, body, 0)
    out = a[pl.ds(pl.multiple_of(position * 8, 8), 8), :]
    lane = lax.broadcasted_iota(jnp.int32, out.shape, 1)
    o_ref[...] = jnp.where(lane >= (position // 16) * NB, out, 0.0)


def factor_rows(ids, ridge, own, other):
    return pl.pallas_call(
        factor_kernel,
        out_shape=jax.ShapeDtypeStruct((8, FEAT), f32),
        in_specs=[SMEM, VMEM, VMEM, VMEM],
        out_specs=VMEM,
        scratch_shapes=[pltpu.VMEM((FEAT, FEAT), f32)] + [pltpu.VMEM((NB, NB), f32)] * 3
        + [pltpu.VMEM((6 * NB, FEAT), bf16)] * 2,
        compiler_params=params(),
        cost_estimate=pl.CostEstimate(flops=40_000_000_000, bytes_accessed=2 << 20, transcendentals=0),
    )(ids, ridge, own, other)


def swap_cores(x):
    return lax.ppermute(x, "outer", [(0, 1), (1, 0)])


def along_z(x, distance):
    return lax.ppermute(x, "inner", [(i, (i + 16 * distance) % 64) for i in range(64)])


def plane_exchange(x):
    return lax.all_to_all(x, "inner", 0, 0, axis_index_groups=PLANES, tiled=True)


def local(matrix, sign_flip, keep_list, ridge_weights):
    core, inner = lax.axis_index("outer"), lax.axis_index("inner")
    ids = jnp.stack([core, core * 64 + inner]).astype(jnp.int32)
    keep_here = lax.dynamic_index_in_dim(keep_list.reshape(2, 4, 16, 2), inner // 16, 1, False)
    keep_rows = jnp.repeat(keep_here.reshape(32, 2), 4, axis=0)
    mixed = local_mix(matrix, sign_flip)
    along = lax.all_to_all(
        mixed.reshape(4, 128, FEAT), "inner", 0, 0, axis_index_groups=Z_GROUPS, tiled=True
    )
    mine = select_rows(keep_rows, along).reshape(256, FEAT)
    theirs = swap_cores(mine)
    received = plane_exchange(gram_half(ids, mine, theirs))
    piece = jnp.sum(received[:, :GRAM_ROWS], axis=0)
    piece = (piece + along_z(piece, 2)) + (along_z(piece, 1) + along_z(piece, 3))
    own = plane_exchange(jnp.broadcast_to(piece[None], (16, GRAM_ROWS, NB))).reshape(16 * GRAM_ROWS, NB)
    sketch = final_mix(ids, received)
    other = swap_cores(own)
    factor = factor_rows(ids, ridge_weights.reshape(1, FEAT), own, other)
    return sketch, factor


def solution(mesh):
    return jax.shard_map(
        local,
        mesh=mesh,
        in_specs=(P(("outer", "inner"), None), P(("outer", "inner")), P(), P()),
        out_specs=(P(("outer", "inner"), None), P(("outer", "inner"), None)),
        check_vma=False,
    )
```

```python
import jax
import jax.numpy as jnp
import numpy as np
from jax import lax
from jax.experimental import pallas as pl
from jax.experimental.pallas import tpu as pltpu
from jax.sharding import PartitionSpec as P

f32 = jnp.float32
bf16 = jnp.bfloat16
VMEM = pl.BlockSpec(memory_space=pltpu.VMEM)
SMEM = pl.BlockSpec(memory_space=pltpu.SMEM)
FEAT = 1024
NB = 128
PANELS = FEAT // NB
STRIPS = ((0, 3, 4, 7), (1, 2, 5, 6))
GRAM_ROWS = 144
LEFT = (0, 0, 0, 1, 1, 2)
RIGHT = (0, 1, 2, 0, 1, 0)
Z_GROUPS = [[i + 16 * j for j in range(4)] for i in range(16)]
PLANES = [[16 * j + i for i in range(16)] for j in range(4)]


def params(mib=32):
    return pltpu.CompilerParams(vmem_limit_bytes=mib << 20)


def parity_sign(left, right):
    common = left & right
    parity = np.zeros_like(common)
    for shift_by in range(10):
        parity ^= (common >> shift_by) & 1
    return 1 - 2 * parity


def local_table():
    az, c, axy, e = np.meshgrid(range(4), range(2), range(16), range(4), indexing="ij")
    k = (az * 128 + axy * 8 + c * 4 + e).reshape(-1, 1)
    return parity_sign(k, np.arange(512)[None, :]).astype(np.float32).astype(bf16)


def final_table():
    j, i, o, e = (v.reshape(-1, 1) for v in np.meshgrid(range(2), range(16), range(2), range(4), indexing="ij"))
    ip, op, jp, ep = (v.reshape(1, -1) for v in np.meshgrid(range(16), range(2), range(2), range(4), indexing="ij"))
    table = parity_sign(i, ip) * parity_sign(o, op) * (j == jp) * (e == ep)
    return table.astype(np.float32).astype(bf16)


def halves(x):
    high = x.astype(bf16)
    return high, (x - high.astype(f32)).astype(bf16)


def mm(a, b):
    return jnp.dot(a, b, preferred_element_type=f32)


def tmm(a, b):
    return lax.dot_general(a, b, (((0,), (0,)), ((), ())), preferred_element_type=f32)


def local_mix_kernel(table_ref, sign_ref, x_ref, o_ref, signed):
    @pl.when(pl.program_id(0) == 0)
    def _():
        signed[...] = (table_ref[...].astype(f32) * (sign_ref[...].astype(f32) * 2.0**-13)).astype(bf16)

    high, low = halves(x_ref[...])
    o_ref[...] = mm(signed[...], high) + mm(signed[...], low)


def local_mix(matrix, sign_flip):
    rows, features = matrix.shape
    cols = 256
    return pl.pallas_call(
        local_mix_kernel,
        grid=(features // cols,),
        out_shape=jax.ShapeDtypeStruct((rows, features), f32),
        in_specs=[
            pl.BlockSpec((rows, rows), lambda g: (0, 0)),
            pl.BlockSpec((1, rows), lambda g: (0, 0)),
            pl.BlockSpec((rows, cols), lambda g: (0, g)),
        ],
        out_specs=pl.BlockSpec((rows, cols), lambda g: (0, g)),
        scratch_shapes=[pltpu.VMEM((rows, rows), bf16)],
        compiler_params=params(60),
    )(jnp.asarray(local_table()), sign_flip.reshape(1, rows), matrix)


def select_kernel(keep_ref, y_ref, v_ref):
    y0, y1, y2, y3 = (y_ref[z] for z in range(4))
    s, d, s2, d2 = y0 + y1, y0 - y1, y2 + y3, y2 - y3

    def combo(which):
        low = (which & 1) == 1
        first = jnp.where(low, d, s)
        second = jnp.where(low, d2, s2)
        return first + jnp.where((which & 2) == 2, -second, second)

    shape = s.shape
    v0 = combo(jnp.broadcast_to(keep_ref[:, 0:1], shape))
    v1 = combo(jnp.broadcast_to(keep_ref[:, 1:2], shape))
    upper = (lax.broadcasted_iota(jnp.int32, shape, 0) & 7) < 4
    even = jnp.where(upper, v0, pltpu.roll(v1, 4, axis=0))
    odd = jnp.where(upper, pltpu.roll(v0, shape[0] - 4, axis=0), v1)
    v_ref[:, 0] = even.reshape(16, 8, shape[1])
    v_ref[:, 1] = odd.reshape(16, 8, shape[1])


def select_rows(keep_rows, y):
    cols = 256
    features = y.shape[2]
    return pl.pallas_call(
        select_kernel,
        grid=(features // cols,),
        out_shape=jax.ShapeDtypeStruct((16, 2, 8, features), f32),
        in_specs=[
            pl.BlockSpec((128, 2), lambda g: (0, 0)),
            pl.BlockSpec((4, 128, cols), lambda g: (0, 0, g)),
        ],
        out_specs=pl.BlockSpec((16, 2, 8, cols), lambda g: (0, 0, 0, g)),
        compiler_params=params(),
    )(keep_rows, y)


def gram_kernel(ids_ref, v_ref, w_ref, g_ref, s_ref, high, low, flat):
    core = ids_ref[0]
    own = pl.ds(pl.multiple_of(core * 128, 128), 128)
    for part, ref in enumerate((v_ref, w_ref)):
        h, l = halves(ref[...])
        high[256 * part : 256 * part + 256, :] = h
        low[256 * part : 256 * part + 256, :] = l
        s_ref[:, part] = ref[own, :].reshape(16, 8, FEAT)
    for which, strips in enumerate(STRIPS):

        @pl.when(core == which)
        def _():
            row = 0
            for strip in strips:
                at = NB * strip
                h, l = high[:, at : at + NB], low[:, at : at + NB]
                total = tmm(h, high[:, at:]) + (tmm(h, low[:, at:]) + tmm(l, high[:, at:]))
                for block in range(PANELS - strip):
                    flat[row : row + NB, :] = total[:, NB * block : NB * block + NB]
                    row += NB

    for piece in range(16):
        g_ref[piece] = flat[GRAM_ROWS * piece : GRAM_ROWS * (piece + 1), :]


def gram_half(ids, mine, theirs):
    rows = mine.shape[0]
    return pl.pallas_call(
        gram_kernel,
        out_shape=(
            jax.ShapeDtypeStruct((16, GRAM_ROWS, NB), f32),
            jax.ShapeDtypeStruct((16, 2, 8, FEAT), f32),
        ),
        in_specs=[SMEM, VMEM, VMEM],
        out_specs=(VMEM, VMEM),
        scratch_shapes=[pltpu.VMEM((2 * rows, FEAT), bf16)] * 2 + [pltpu.VMEM((16 * GRAM_ROWS, NB), f32)],
        compiler_params=params(),
    )(ids, mine, theirs)


def final_kernel(ids_ref, table_ref, r_ref, o_ref):
    high, low = halves(r_ref[...])
    total = mm(table_ref[...], high) + mm(table_ref[...], low)
    odd = (lax.broadcasted_iota(jnp.int32, total.shape, 0) >> 2) & 1
    flip = (odd * ids_ref[0]) == 1
    o_ref[...] = total * jnp.where(flip, -32.0, 32.0)


def final_mix(ids, received):
    return pl.pallas_call(
        final_kernel,
        out_shape=jax.ShapeDtypeStruct(received.shape, f32),
        in_specs=[SMEM, VMEM, VMEM],
        out_specs=VMEM,
        compiler_params=params(),
    )(ids, jnp.asarray(final_table()), received)


def lane_splat(x, lane):
    return jnp.broadcast_to(x[:, lane : lane + 1], (8, NB))


def thirds(x):
    high = x.astype(bf16).astype(f32)
    rest = x - high
    middle = rest.astype(bf16).astype(f32)
    return high, middle, rest - middle


def pieces3(x):
    return tuple(part.astype(bf16) for part in thirds(x))


def outer_sum(left, right):
    lh, lm, ll = thirds(left)
    rh, rm, rl = thirds(right)
    stacked_left = jnp.concatenate([lh, lh, lh, lm, lm, ll], axis=0).astype(bf16)
    stacked_right = jnp.concatenate([rh, rm, rl, rh, rm, rh], axis=0).astype(bf16)
    return tmm(stacked_left, stacked_right)


def tree_sum(terms):
    while len(terms) > 1:
        terms = [x + y for x, y in zip(terms[::2], terms[1::2])]
    return terms[0]


def row_splat(x, row):
    return jnp.broadcast_to(x[row : row + 1, :], (8, NB))


def by_row(sub, values):
    a = [jnp.where((sub & 1) == 0, values[k], values[k + 1]) for k in (0, 2, 4, 6)]
    b = [jnp.where((sub & 2) == 0, a[k], a[k + 1]) for k in (0, 2)]
    return jnp.where(sub < 4, b[0], b[1])


def factor_block(w, upper, inverse):
    lane = lax.broadcasted_iota(jnp.int32, (8, NB), 1)
    sub = lax.broadcasted_iota(jnp.int32, (8, NB), 0)
    rows = w[0:8, :]
    e = [lane_splat(rows, a) for a in range(8)]
    for step in range(16):
        base = 8 * step
        inside = (lane >= base) & (lane < base + 8)
        aug = jnp.where(inside, jnp.where(lane == base + sub, 1.0, 0.0), rows)
        scales, finished = [], []
        for b in range(8):
            r = lax.rsqrt(row_splat(e[b], b))
            scales.append(r)
            multiplier = jnp.where(sub > b, e[b] * r, 0.0)
            scaled = row_splat(aug, b) * r
            finished.append(scaled)
            if b < 7:
                for a in range(b + 1, 8):
                    e[a] = e[a] - multiplier * (row_splat(e[a], b) * r)
                rows = rows - multiplier * (row_splat(rows, b) * r)
                aug = aug - multiplier * scaled
        scale = by_row(sub, scales)
        if step < 15:
            columns = [lane_splat(rows, base + 8 + a) * scale for a in range(8)]
        left, right = rows * scale, aug * scale
        upper[base : base + 8, :] = jnp.where(lane >= base + sub, left, 0.0)
        inverse[base : base + 8, :] = jnp.where(lane <= base + sub, right, 0.0)
        if step == 15:
            break
        if step < 14:
            update = outer_sum(left, right)
        coming = jnp.where(inside, 0.0, w[base + 8 : base + 16, :])
        start = [lane_splat(coming, base + 8 + a) for a in range(8)]
        c = {(b, a): row_splat(columns[a], b) for b in range(8) for a in range(8)}
        turned = [by_row(sub, [c[b, a] for a in range(8)]) for b in range(8)]
        e = [start[a] - tree_sum([turned[b] * c[b, a] for b in range(8)]) for a in range(8)]
        rows = coming - tree_sum([turned[b] * finished[b] for b in range(8)])
        if step < 14:
            after = base + 16
            rest = lax.broadcasted_iota(jnp.int32, (NB - after, NB), 1)
            cleared = jnp.where((rest >= base) & (rest < base + 8), 0.0, w[after:, :])
            w[after:, :] = cleared - update[after:, :]


def factor_kernel(ids_ref, ridge_ref, own_ref, other_ref, o_ref, a, w, upper, inverse, stack1, stack2):
    core, position = ids_ref[0], ids_ref[1]
    eye = lax.broadcasted_iota(jnp.int32, (NB, NB), 0) == lax.broadcasted_iota(jnp.int32, (NB, NB), 1)
    for which in range(2):

        @pl.when(core == which)
        def _():
            for ref, strips in ((own_ref, STRIPS[which]), (other_ref, STRIPS[1 - which])):
                slot = 0
                for strip in strips:
                    for block in range(strip, PANELS):
                        piece = ref[NB * slot : NB * slot + NB, :]
                        if block == strip:
                            ridge = ridge_ref[0:1, NB * strip : NB * strip + NB]
                            piece = piece + jnp.where(eye, ridge, 0.0)
                        a[NB * strip : NB * strip + NB, NB * block : NB * block + NB] = piece
                        slot += 1

    def body(panel, carry):
        at = pl.multiple_of(panel * NB, NB)
        w[...] = a[pl.ds(at, NB), pl.ds(at, NB)]
        factor_block(w, upper, inverse)
        for fixed in range(PANELS):

            @pl.when(panel == fixed)
            def _():
                s0, s1 = NB * fixed, NB * fixed + NB
                a[s0:s1, s0:s1] = upper[...]
                if fixed < PANELS - 1:
                    inv, rest = pieces3(inverse[...]), pieces3(a[s0:s1, s1:])
                    rows = mm(
                        jnp.concatenate([inv[k] for k in LEFT], axis=1),
                        jnp.concatenate([rest[k] for k in RIGHT], axis=0),
                    )
                    a[s0:s1, s1:] = rows
                    width = FEAT - s1
                    parts = pieces3(rows)
                    for k in range(6):
                        stack1[NB * k : NB * k + NB, :width] = parts[LEFT[k]]
                        stack2[NB * k : NB * k + NB, :width] = parts[RIGHT[k]]
                    for strip in range(fixed + 1, PANELS):
                        b0, t0 = NB * (strip - fixed - 1), NB * strip
                        update = tmm(stack1[:, b0 : b0 + NB], stack2[:, b0:width])
                        a[t0 : t0 + NB, t0:] = a[t0 : t0 + NB, t0:] - update

        return carry

    lax.fori_loop(0, PANELS, body, 0)
    out = a[pl.ds(pl.multiple_of(position * 8, 8), 8), :]
    lane = lax.broadcasted_iota(jnp.int32, out.shape, 1)
    o_ref[...] = jnp.where(lane >= (position // 16) * NB, out, 0.0)


def factor_rows(ids, ridge, own, other):
    return pl.pallas_call(
        factor_kernel,
        out_shape=jax.ShapeDtypeStruct((8, FEAT), f32),
        in_specs=[SMEM, VMEM, VMEM, VMEM],
        out_specs=VMEM,
        scratch_shapes=[pltpu.VMEM((FEAT, FEAT), f32)] + [pltpu.VMEM((NB, NB), f32)] * 3
        + [pltpu.VMEM((6 * NB, FEAT), bf16)] * 2,
        compiler_params=params(),
        cost_estimate=pl.CostEstimate(flops=40_000_000_000, bytes_accessed=2 << 20, transcendentals=0),
    )(ids, ridge, own, other)


def swap_cores(x):
    return lax.ppermute(x, "outer", [(0, 1), (1, 0)])


def along_z(x, distance):
    return lax.ppermute(x, "inner", [(i, (i + 16 * distance) % 64) for i in range(64)])


def plane_exchange(x):
    return lax.all_to_all(x, "inner", 0, 0, axis_index_groups=PLANES, tiled=True)


def local(matrix, sign_flip, keep_list, ridge_weights):
    core, inner = lax.axis_index("outer"), lax.axis_index("inner")
    ids = jnp.stack([core, core * 64 + inner]).astype(jnp.int32)
    keep_here = lax.dynamic_index_in_dim(keep_list.reshape(2, 4, 16, 2), inner // 16, 1, False)
    keep_rows = jnp.repeat(keep_here.reshape(32, 2), 4, axis=0)
    mixed = local_mix(matrix, sign_flip)
    along = lax.all_to_all(
        mixed.reshape(4, 128, FEAT), "inner", 0, 0, axis_index_groups=Z_GROUPS, tiled=True
    )
    mine = select_rows(keep_rows, along).reshape(256, FEAT)
    theirs = swap_cores(mine)
    gram, to_send = gram_half(ids, mine, theirs)
    piece = jnp.sum(plane_exchange(gram), axis=0)
    piece = (piece + along_z(piece, 2)) + (along_z(piece, 1) + along_z(piece, 3))
    own = plane_exchange(jnp.broadcast_to(piece[None], (16, GRAM_ROWS, NB))).reshape(16 * GRAM_ROWS, NB)
    to_send, own = lax.optimization_barrier((to_send, own))
    received = plane_exchange(to_send)
    other = swap_cores(own)
    factor = factor_rows(ids, ridge_weights.reshape(1, FEAT), own, other)
    sketch = final_mix(ids, received.reshape(256, FEAT))
    return sketch, factor


def solution(mesh):
    return jax.shard_map(
        local,
        mesh=mesh,
        in_specs=(P(("outer", "inner"), None), P(("outer", "inner")), P(), P()),
        out_specs=(P(("outer", "inner"), None), P(("outer", "inner"), None)),
        check_vma=False,
    )
```

```python
import jax
import jax.numpy as jnp
import numpy as np
from jax import lax
from jax.experimental import pallas as pl
from jax.experimental.pallas import tpu as pltpu
from jax.sharding import PartitionSpec as P

f32 = jnp.float32
bf16 = jnp.bfloat16
VMEM = pl.BlockSpec(memory_space=pltpu.VMEM)
SMEM = pl.BlockSpec(memory_space=pltpu.SMEM)
FEAT = 1024
NB = 128
PANELS = FEAT // NB
STRIPS = ((0, 3, 4, 7), (1, 2, 5, 6))
GRAM_ROWS = 144
LEFT = (0, 0, 0, 1, 1, 2)
RIGHT = (0, 1, 2, 0, 1, 0)
Z_GROUPS = [[i + 16 * j for j in range(4)] for i in range(16)]
PLANES = [[16 * j + i for i in range(16)] for j in range(4)]


def params(mib=32):
    return pltpu.CompilerParams(vmem_limit_bytes=mib << 20)


def parity_sign(left, right):
    common = left & right
    parity = np.zeros_like(common)
    for shift_by in range(10):
        parity ^= (common >> shift_by) & 1
    return 1 - 2 * parity


def local_table():
    az, c, axy, e = np.meshgrid(range(4), range(2), range(16), range(4), indexing="ij")
    k = (az * 128 + axy * 8 + c * 4 + e).reshape(-1, 1)
    return parity_sign(k, np.arange(512)[None, :]).astype(np.float32).astype(bf16)


def final_table():
    j, i, o, e = (v.reshape(-1, 1) for v in np.meshgrid(range(2), range(16), range(2), range(4), indexing="ij"))
    ip, op, jp, ep = (v.reshape(1, -1) for v in np.meshgrid(range(16), range(2), range(2), range(4), indexing="ij"))
    table = parity_sign(i, ip) * parity_sign(o, op) * (j == jp) * (e == ep)
    return table.astype(np.float32).astype(bf16)


def halves(x):
    high = x.astype(bf16)
    return high, (x - high.astype(f32)).astype(bf16)


def mm(a, b):
    return jnp.dot(a, b, preferred_element_type=f32)


def tmm(a, b):
    return lax.dot_general(a, b, (((0,), (0,)), ((), ())), preferred_element_type=f32)


def local_mix_kernel(table_ref, sign_ref, x_ref, o_ref, signed):
    @pl.when(pl.program_id(0) == 0)
    def _():
        signed[...] = (table_ref[...].astype(f32) * (sign_ref[...].astype(f32) * 2.0**-13)).astype(bf16)

    high, low = halves(x_ref[...])
    o_ref[...] = mm(signed[...], high) + mm(signed[...], low)


def local_mix(matrix, sign_flip):
    rows, features = matrix.shape
    cols = 256
    return pl.pallas_call(
        local_mix_kernel,
        grid=(features // cols,),
        out_shape=jax.ShapeDtypeStruct((rows, features), f32),
        in_specs=[
            pl.BlockSpec((rows, rows), lambda g: (0, 0)),
            pl.BlockSpec((1, rows), lambda g: (0, 0)),
            pl.BlockSpec((rows, cols), lambda g: (0, g)),
        ],
        out_specs=pl.BlockSpec((rows, cols), lambda g: (0, g)),
        scratch_shapes=[pltpu.VMEM((rows, rows), bf16)],
        compiler_params=params(60),
    )(jnp.asarray(local_table()), sign_flip.reshape(1, rows), matrix)


def select_kernel(keep_ref, y_ref, v_ref):
    y0, y1, y2, y3 = (y_ref[z] for z in range(4))
    s, d, s2, d2 = y0 + y1, y0 - y1, y2 + y3, y2 - y3

    def combo(which):
        low = (which & 1) == 1
        first = jnp.where(low, d, s)
        second = jnp.where(low, d2, s2)
        return first + jnp.where((which & 2) == 2, -second, second)

    shape = s.shape
    v0 = combo(jnp.broadcast_to(keep_ref[:, 0:1], shape))
    v1 = combo(jnp.broadcast_to(keep_ref[:, 1:2], shape))
    upper = (lax.broadcasted_iota(jnp.int32, shape, 0) & 7) < 4
    even = jnp.where(upper, v0, pltpu.roll(v1, 4, axis=0))
    odd = jnp.where(upper, pltpu.roll(v0, shape[0] - 4, axis=0), v1)
    v_ref[:, 0] = even.reshape(16, 8, shape[1])
    v_ref[:, 1] = odd.reshape(16, 8, shape[1])


def select_rows(keep_rows, y):
    cols = 256
    features = y.shape[2]
    return pl.pallas_call(
        select_kernel,
        grid=(features // cols,),
        out_shape=jax.ShapeDtypeStruct((16, 2, 8, features), f32),
        in_specs=[
            pl.BlockSpec((128, 2), lambda g: (0, 0)),
            pl.BlockSpec((4, 128, cols), lambda g: (0, 0, g)),
        ],
        out_specs=pl.BlockSpec((16, 2, 8, cols), lambda g: (0, 0, 0, g)),
        compiler_params=params(),
    )(keep_rows, y)


def gram_kernel(ids_ref, v_ref, w_ref, g_ref, s_ref, high, low, flat):
    core = ids_ref[0]
    own = pl.ds(pl.multiple_of(core * 128, 128), 128)
    for part, ref in enumerate((v_ref, w_ref)):
        h, l = halves(ref[...])
        high[256 * part : 256 * part + 256, :] = h
        low[256 * part : 256 * part + 256, :] = l
        s_ref[:, part] = ref[own, :].reshape(16, 8, FEAT)
    for which, strips in enumerate(STRIPS):

        @pl.when(core == which)
        def _():
            row = 0
            for strip in strips:
                at = NB * strip
                h, l = high[:, at : at + NB], low[:, at : at + NB]
                total = tmm(h, high[:, at:]) + (tmm(h, low[:, at:]) + tmm(l, high[:, at:]))
                for block in range(PANELS - strip):
                    flat[row : row + NB, :] = total[:, NB * block : NB * block + NB]
                    row += NB

    for piece in range(16):
        g_ref[piece] = flat[GRAM_ROWS * piece : GRAM_ROWS * (piece + 1), :]


def gram_half(ids, mine, theirs):
    rows = mine.shape[0]
    return pl.pallas_call(
        gram_kernel,
        out_shape=(
            jax.ShapeDtypeStruct((16, GRAM_ROWS, NB), f32),
            jax.ShapeDtypeStruct((16, 2, 8, FEAT), f32),
        ),
        in_specs=[SMEM, VMEM, VMEM],
        out_specs=(VMEM, VMEM),
        scratch_shapes=[pltpu.VMEM((2 * rows, FEAT), bf16)] * 2 + [pltpu.VMEM((16 * GRAM_ROWS, NB), f32)],
        compiler_params=params(),
    )(ids, mine, theirs)


def final_kernel(ids_ref, table_ref, r_ref, o_ref):
    high, low = halves(r_ref[...])
    total = mm(table_ref[...], high) + mm(table_ref[...], low)
    odd = (lax.broadcasted_iota(jnp.int32, total.shape, 0) >> 2) & 1
    flip = (odd * ids_ref[0]) == 1
    o_ref[...] = total * jnp.where(flip, -32.0, 32.0)


def final_mix(ids, received):
    return pl.pallas_call(
        final_kernel,
        out_shape=jax.ShapeDtypeStruct(received.shape, f32),
        in_specs=[SMEM, VMEM, VMEM],
        out_specs=VMEM,
        compiler_params=params(),
    )(ids, jnp.asarray(final_table()), received)


def lane_splat(x, lane):
    return jnp.broadcast_to(x[:, lane : lane + 1], (8, NB))


def thirds(x):
    high = x.astype(bf16).astype(f32)
    rest = x - high
    middle = rest.astype(bf16).astype(f32)
    return high, middle, rest - middle


def pieces3(x):
    return tuple(part.astype(bf16) for part in thirds(x))


def outer_sum(left, right):
    lh, lm, ll = thirds(left)
    rh, rm, rl = thirds(right)
    stacked_left = jnp.concatenate([lh, lh, lh, lm, lm, ll], axis=0).astype(bf16)
    stacked_right = jnp.concatenate([rh, rm, rl, rh, rm, rh], axis=0).astype(bf16)
    return tmm(stacked_left, stacked_right)


def tree_sum(terms):
    while len(terms) > 1:
        terms = [x + y for x, y in zip(terms[::2], terms[1::2])]
    return terms[0]


def row_splat(x, row):
    return jnp.broadcast_to(x[row : row + 1, :], (8, NB))


def by_row(sub, values):
    a = [jnp.where((sub & 1) == 0, values[k], values[k + 1]) for k in (0, 2, 4, 6)]
    b = [jnp.where((sub & 2) == 0, a[k], a[k + 1]) for k in (0, 2)]
    return jnp.where(sub < 4, b[0], b[1])


def factor_block(w, upper, inverse):
    lane = lax.broadcasted_iota(jnp.int32, (8, NB), 1)
    sub = lax.broadcasted_iota(jnp.int32, (8, NB), 0)
    rows = w[0:8, :]
    e = [lane_splat(rows, a) for a in range(8)]
    for step in range(16):
        base = 8 * step
        inside = (lane >= base) & (lane < base + 8)
        aug = jnp.where(inside, jnp.where(lane == base + sub, 1.0, 0.0), rows)
        scales, finished = [], []
        for b in range(8):
            r = lax.rsqrt(row_splat(e[b], b))
            scales.append(r)
            multiplier = jnp.where(sub > b, e[b] * r, 0.0)
            scaled = row_splat(aug, b) * r
            finished.append(scaled)
            if b < 7:
                for a in range(b + 1, 8):
                    e[a] = e[a] - multiplier * (row_splat(e[a], b) * r)
                rows = rows - multiplier * (row_splat(rows, b) * r)
                aug = aug - multiplier * scaled
        scale = by_row(sub, scales)
        if step < 15:
            columns = [lane_splat(rows, base + 8 + a) * scale for a in range(8)]
        left, right = rows * scale, aug * scale
        upper[base : base + 8, :] = jnp.where(lane >= base + sub, left, 0.0)
        inverse[base : base + 8, :] = jnp.where(lane <= base + sub, right, 0.0)
        if step == 15:
            break
        if step < 14:
            update = outer_sum(left, right)
        coming = jnp.where(inside, 0.0, w[base + 8 : base + 16, :])
        start = [lane_splat(coming, base + 8 + a) for a in range(8)]
        c = {(b, a): row_splat(columns[a], b) for b in range(8) for a in range(8)}
        turned = [by_row(sub, [c[b, a] for a in range(8)]) for b in range(8)]
        e = [start[a] - tree_sum([turned[b] * c[b, a] for b in range(8)]) for a in range(8)]
        rows = coming - tree_sum([turned[b] * finished[b] for b in range(8)])
        if step < 14:
            after = base + 16
            rest = lax.broadcasted_iota(jnp.int32, (NB - after, NB), 1)
            cleared = jnp.where((rest >= base) & (rest < base + 8), 0.0, w[after:, :])
            w[after:, :] = cleared - update[after:, :]


def factor_kernel(ids_ref, ridge_ref, own_ref, other_ref, o_ref, a, w, upper, inverse, stack1, stack2):
    core, position = ids_ref[0], ids_ref[1]
    eye = lax.broadcasted_iota(jnp.int32, (NB, NB), 0) == lax.broadcasted_iota(jnp.int32, (NB, NB), 1)
    for which in range(2):

        @pl.when(core == which)
        def _():
            for ref, strips in ((own_ref, STRIPS[which]), (other_ref, STRIPS[1 - which])):
                slot = 0
                for strip in strips:
                    for block in range(strip, PANELS):
                        piece = ref[NB * slot : NB * slot + NB, :]
                        if block == strip:
                            ridge = ridge_ref[0:1, NB * strip : NB * strip + NB]
                            piece = piece + jnp.where(eye, ridge, 0.0)
                        a[NB * strip : NB * strip + NB, NB * block : NB * block + NB] = piece
                        slot += 1

    def body(panel, carry):
        at = pl.multiple_of(panel * NB, NB)
        w[...] = a[pl.ds(at, NB), pl.ds(at, NB)]
        factor_block(w, upper, inverse)
        for fixed in range(PANELS):

            @pl.when(panel == fixed)
            def _():
                s0, s1 = NB * fixed, NB * fixed + NB
                a[s0:s1, s0:s1] = upper[...]
                if fixed < PANELS - 1:
                    inv, rest = pieces3(inverse[...]), pieces3(a[s0:s1, s1:])
                    rows = mm(
                        jnp.concatenate([inv[k] for k in LEFT], axis=1),
                        jnp.concatenate([rest[k] for k in RIGHT], axis=0),
                    )
                    a[s0:s1, s1:] = rows
                    width = FEAT - s1
                    parts = pieces3(rows)
                    for k in range(6):
                        stack1[NB * k : NB * k + NB, :width] = parts[LEFT[k]]
                        stack2[NB * k : NB * k + NB, :width] = parts[RIGHT[k]]
                    for strip in range(fixed + 1, PANELS):
                        b0, t0 = NB * (strip - fixed - 1), NB * strip
                        update = tmm(stack1[:, b0 : b0 + NB], stack2[:, b0:width])
                        a[t0 : t0 + NB, t0:] = a[t0 : t0 + NB, t0:] - update

        return carry

    lax.fori_loop(0, PANELS, body, 0)
    out = a[pl.ds(pl.multiple_of(position * 8, 8), 8), :]
    lane = lax.broadcasted_iota(jnp.int32, out.shape, 1)
    o_ref[...] = jnp.where(lane >= (position // 16) * NB, out, 0.0)


def factor_rows(ids, ridge, own, other):
    return pl.pallas_call(
        factor_kernel,
        out_shape=jax.ShapeDtypeStruct((8, FEAT), f32),
        in_specs=[SMEM, VMEM, VMEM, VMEM],
        out_specs=VMEM,
        scratch_shapes=[pltpu.VMEM((FEAT, FEAT), f32)] + [pltpu.VMEM((NB, NB), f32)] * 3
        + [pltpu.VMEM((6 * NB, FEAT), bf16)] * 2,
        compiler_params=params(),
        cost_estimate=pl.CostEstimate(flops=40_000_000_000, bytes_accessed=2 << 20, transcendentals=0),
    )(ids, ridge, own, other)


def swap_cores(x):
    return lax.ppermute(x, "outer", [(0, 1), (1, 0)])


def along_z(x, distance):
    return lax.ppermute(x, "inner", [(i, (i + 16 * distance) % 64) for i in range(64)])


def plane_exchange(x):
    return lax.all_to_all(x, "inner", 0, 0, axis_index_groups=PLANES, tiled=True)


def local(matrix, sign_flip, keep_list, ridge_weights):
    core, inner = lax.axis_index("outer"), lax.axis_index("inner")
    ids = jnp.stack([core, core * 64 + inner]).astype(jnp.int32)
    keep_here = lax.dynamic_index_in_dim(keep_list.reshape(2, 4, 16, 2), inner // 16, 1, False)
    keep_rows = jnp.repeat(keep_here.reshape(32, 2), 4, axis=0)
    mixed = local_mix(matrix, sign_flip)
    along = lax.all_to_all(
        mixed.reshape(4, 128, FEAT), "inner", 0, 0, axis_index_groups=Z_GROUPS, tiled=True
    )
    mine = select_rows(keep_rows, along).reshape(256, FEAT)
    theirs = swap_cores(mine)
    gram, to_send = gram_half(ids, mine, theirs)
    piece = jnp.sum(plane_exchange(gram), axis=0)
    piece = (piece + along_z(piece, 2)) + (along_z(piece, 1) + along_z(piece, 3))
    own = plane_exchange(jnp.broadcast_to(piece[None], (16, GRAM_ROWS, NB))).reshape(16 * GRAM_ROWS, NB)
    other = swap_cores(own)
    to_send, own, other = lax.optimization_barrier((to_send, own, other))
    received = plane_exchange(to_send)
    factor = factor_rows(ids, ridge_weights.reshape(1, FEAT), own, other)
    sketch = final_mix(ids, received.reshape(256, FEAT))
    return sketch, factor


def solution(mesh):
    return jax.shard_map(
        local,
        mesh=mesh,
        in_specs=(P(("outer", "inner"), None), P(("outer", "inner")), P(), P()),
        out_specs=(P(("outer", "inner"), None), P(("outer", "inner"), None)),
        check_vma=False,
    )
```

```python
import jax
import jax.numpy as jnp
import numpy as np
from jax import lax
from jax.experimental import pallas as pl
from jax.experimental.pallas import tpu as pltpu
from jax.sharding import PartitionSpec as P

f32 = jnp.float32
bf16 = jnp.bfloat16
VMEM = pl.BlockSpec(memory_space=pltpu.VMEM)
SMEM = pl.BlockSpec(memory_space=pltpu.SMEM)
FEAT = 1024
NB = 128
PANELS = FEAT // NB
STRIPS = ((0, 3, 4, 7), (1, 2, 5, 6))
GRAM_ROWS = 144
LEFT = (0, 0, 0, 1, 1, 2)
RIGHT = (0, 1, 2, 0, 1, 0)
Z_GROUPS = [[i + 16 * j for j in range(4)] for i in range(16)]
PLANES = [[16 * j + i for i in range(16)] for j in range(4)]


def params(mib=32):
    return pltpu.CompilerParams(vmem_limit_bytes=mib << 20)


def parity_sign(left, right):
    common = left & right
    parity = np.zeros_like(common)
    for shift_by in range(10):
        parity ^= (common >> shift_by) & 1
    return 1 - 2 * parity


def local_table():
    az, c, axy, e = np.meshgrid(range(4), range(2), range(16), range(4), indexing="ij")
    k = (az * 128 + axy * 8 + c * 4 + e).reshape(-1, 1)
    return parity_sign(k, np.arange(512)[None, :]).astype(np.float32).astype(bf16)


def final_table():
    j, i, o, e = (v.reshape(-1, 1) for v in np.meshgrid(range(2), range(16), range(2), range(4), indexing="ij"))
    ip, op, jp, ep = (v.reshape(1, -1) for v in np.meshgrid(range(16), range(2), range(2), range(4), indexing="ij"))
    table = parity_sign(i, ip) * parity_sign(o, op) * (j == jp) * (e == ep)
    return table.astype(np.float32).astype(bf16)


def halves(x):
    high = x.astype(bf16)
    return high, (x - high.astype(f32)).astype(bf16)


def mm(a, b):
    return jnp.dot(a, b, preferred_element_type=f32)


def tmm(a, b):
    return lax.dot_general(a, b, (((0,), (0,)), ((), ())), preferred_element_type=f32)


def local_mix_kernel(table_hbm, sign_hbm, x_hbm, o_hbm, table, sign, signed, x, out, sems):
    chunks, _, cols = x.shape

    def columns(ref, chunk):
        return ref.at[:, cols * chunk : cols * chunk + cols]

    def load(chunk):
        return pltpu.make_async_copy(columns(x_hbm, chunk), x.at[chunk], sems.at[chunk])

    def store(chunk):
        return pltpu.make_async_copy(out.at[chunk], columns(o_hbm, chunk), sems.at[chunks + chunk])

    get_table = pltpu.make_async_copy(table_hbm, table, sems.at[2 * chunks])
    get_sign = pltpu.make_async_copy(sign_hbm, sign, sems.at[2 * chunks + 1])
    get_sign.start()
    get_table.start()
    for chunk in range(chunks):
        load(chunk).start()
    get_sign.wait()
    get_table.wait()
    signed[...] = (table[...].astype(f32) * (sign[...].astype(f32) * 2.0**-13)).astype(bf16)
    for chunk in range(chunks):
        load(chunk).wait()
        high, low = halves(x[chunk])
        out[chunk] = mm(signed[...], high) + mm(signed[...], low)
        store(chunk).start()
    for chunk in range(chunks):
        store(chunk).wait()


def local_mix(matrix, sign_flip):
    rows, features = matrix.shape
    chunks = 4
    anywhere = pl.BlockSpec(memory_space=pl.ANY)
    block = pltpu.VMEM((chunks, rows, features // chunks), f32)
    return pl.pallas_call(
        local_mix_kernel,
        out_shape=jax.ShapeDtypeStruct((rows, features), f32),
        in_specs=[anywhere] * 3,
        out_specs=anywhere,
        scratch_shapes=[
            pltpu.VMEM((rows, rows), bf16),
            pltpu.VMEM((1, rows), jnp.int32),
            pltpu.VMEM((rows, rows), bf16),
            block,
            block,
            pltpu.SemaphoreType.DMA((2 * chunks + 2,)),
        ],
        compiler_params=params(60),
    )(jnp.asarray(local_table()), sign_flip.reshape(1, rows), matrix)


def select_kernel(keep_ref, y_ref, v_ref):
    y0, y1, y2, y3 = (y_ref[z] for z in range(4))
    s, d, s2, d2 = y0 + y1, y0 - y1, y2 + y3, y2 - y3

    def combo(which):
        low = (which & 1) == 1
        first = jnp.where(low, d, s)
        second = jnp.where(low, d2, s2)
        return first + jnp.where((which & 2) == 2, -second, second)

    shape = s.shape
    v0 = combo(jnp.broadcast_to(keep_ref[:, 0:1], shape))
    v1 = combo(jnp.broadcast_to(keep_ref[:, 1:2], shape))
    upper = (lax.broadcasted_iota(jnp.int32, shape, 0) & 7) < 4
    even = jnp.where(upper, v0, pltpu.roll(v1, 4, axis=0))
    odd = jnp.where(upper, pltpu.roll(v0, shape[0] - 4, axis=0), v1)
    v_ref[:, 0] = even.reshape(16, 8, shape[1])
    v_ref[:, 1] = odd.reshape(16, 8, shape[1])


def select_rows(keep_rows, y):
    cols = 256
    features = y.shape[2]
    return pl.pallas_call(
        select_kernel,
        grid=(features // cols,),
        out_shape=jax.ShapeDtypeStruct((16, 2, 8, features), f32),
        in_specs=[
            pl.BlockSpec((128, 2), lambda g: (0, 0)),
            pl.BlockSpec((4, 128, cols), lambda g: (0, 0, g)),
        ],
        out_specs=pl.BlockSpec((16, 2, 8, cols), lambda g: (0, 0, 0, g)),
        compiler_params=params(),
    )(keep_rows, y)


def gram_kernel(ids_ref, v_ref, w_ref, g_ref, s_ref, high, low, flat):
    core = ids_ref[0]
    own = pl.ds(pl.multiple_of(core * 128, 128), 128)
    for part, ref in enumerate((v_ref, w_ref)):
        h, l = halves(ref[...])
        high[256 * part : 256 * part + 256, :] = h
        low[256 * part : 256 * part + 256, :] = l
        s_ref[:, part] = ref[own, :].reshape(16, 8, FEAT)
    for which, strips in enumerate(STRIPS):

        @pl.when(core == which)
        def _():
            row = 0
            for strip in strips:
                at = NB * strip
                h, l = high[:, at : at + NB], low[:, at : at + NB]
                total = tmm(h, high[:, at:]) + (tmm(h, low[:, at:]) + tmm(l, high[:, at:]))
                for block in range(PANELS - strip):
                    flat[row : row + NB, :] = total[:, NB * block : NB * block + NB]
                    row += NB

    for piece in range(16):
        g_ref[piece] = flat[GRAM_ROWS * piece : GRAM_ROWS * (piece + 1), :]


def gram_half(ids, mine, theirs):
    rows = mine.shape[0]
    return pl.pallas_call(
        gram_kernel,
        out_shape=(
            jax.ShapeDtypeStruct((16, GRAM_ROWS, NB), f32),
            jax.ShapeDtypeStruct((16, 2, 8, FEAT), f32),
        ),
        in_specs=[SMEM, VMEM, VMEM],
        out_specs=(VMEM, VMEM),
        scratch_shapes=[pltpu.VMEM((2 * rows, FEAT), bf16)] * 2 + [pltpu.VMEM((16 * GRAM_ROWS, NB), f32)],
        compiler_params=params(),
    )(ids, mine, theirs)


def final_kernel(ids_ref, table_ref, r_ref, factor_ref, o_ref):
    high, low = halves(r_ref[...])
    total = mm(table_ref[...], high) + mm(table_ref[...], low)
    odd = (lax.broadcasted_iota(jnp.int32, total.shape, 0) >> 2) & 1
    flip = (odd * ids_ref[0]) == 1
    o_ref[...] = total * jnp.where(flip, -32.0, 32.0)


def final_mix(ids, received, factor):
    return pl.pallas_call(
        final_kernel,
        out_shape=jax.ShapeDtypeStruct(received.shape, f32),
        in_specs=[SMEM, VMEM, VMEM, pl.BlockSpec(memory_space=pl.ANY)],
        out_specs=VMEM,
        compiler_params=params(),
    )(ids, jnp.asarray(final_table()), received, factor)


def lane_splat(x, lane):
    return jnp.broadcast_to(x[:, lane : lane + 1], (8, NB))


def thirds(x):
    high = x.astype(bf16).astype(f32)
    rest = x - high
    middle = rest.astype(bf16).astype(f32)
    return high, middle, rest - middle


def pieces3(x):
    return tuple(part.astype(bf16) for part in thirds(x))


def outer_sum(left, right):
    lh, lm, ll = thirds(left)
    rh, rm, rl = thirds(right)
    stacked_left = jnp.concatenate([lh, lh, lh, lm, lm, ll], axis=0).astype(bf16)
    stacked_right = jnp.concatenate([rh, rm, rl, rh, rm, rh], axis=0).astype(bf16)
    return tmm(stacked_left, stacked_right)


def tree_sum(terms):
    while len(terms) > 1:
        terms = [x + y for x, y in zip(terms[::2], terms[1::2])]
    return terms[0]


def row_splat(x, row):
    return jnp.broadcast_to(x[row : row + 1, :], (8, NB))


def by_row(sub, values):
    a = [jnp.where((sub & 1) == 0, values[k], values[k + 1]) for k in (0, 2, 4, 6)]
    b = [jnp.where((sub & 2) == 0, a[k], a[k + 1]) for k in (0, 2)]
    return jnp.where(sub < 4, b[0], b[1])


def factor_block(w, upper, inverse):
    lane = lax.broadcasted_iota(jnp.int32, (8, NB), 1)
    sub = lax.broadcasted_iota(jnp.int32, (8, NB), 0)
    rows = w[0:8, :]
    e = [lane_splat(rows, a) for a in range(8)]
    for step in range(16):
        base = 8 * step
        inside = (lane >= base) & (lane < base + 8)
        aug = jnp.where(inside, jnp.where(lane == base + sub, 1.0, 0.0), rows)
        scales, finished = [], []
        for b in range(8):
            r = lax.rsqrt(row_splat(e[b], b))
            scales.append(r)
            multiplier = jnp.where(sub > b, e[b], 0.0) * r
            scaled = row_splat(aug, b) * r
            finished.append(scaled)
            if b < 7:
                for a in range(b + 1, 8):
                    e[a] = e[a] - multiplier * (row_splat(e[a], b) * r)
                rows = rows - multiplier * (row_splat(rows, b) * r)
                aug = aug - multiplier * scaled
        scale = by_row(sub, scales)
        if step < 15:
            columns = [lane_splat(rows, base + 8 + a) * scale for a in range(8)]
        left, right = rows * scale, aug * scale
        upper[base : base + 8, :] = jnp.where(lane >= base + sub, left, 0.0)
        inverse[base : base + 8, :] = jnp.where(lane <= base + sub, right, 0.0)
        if step == 15:
            break
        if step < 14:
            update = outer_sum(left, right)
        coming = jnp.where(inside, 0.0, w[base + 8 : base + 16, :])
        start = [lane_splat(coming, base + 8 + a) for a in range(8)]
        c = {(b, a): row_splat(columns[a], b) for b in range(8) for a in range(8)}
        turned = [by_row(sub, [c[b, a] for a in range(8)]) for b in range(8)]
        e = [start[a] - tree_sum([turned[b] * c[b, a] for b in range(8)]) for a in range(8)]
        rows = coming - tree_sum([turned[b] * finished[b] for b in range(8)])
        if step < 14:
            after = base + 16
            rest = lax.broadcasted_iota(jnp.int32, (NB - after, NB), 1)
            cleared = jnp.where((rest >= base) & (rest < base + 8), 0.0, w[after:, :])
            w[after:, :] = cleared - update[after:, :]


def factor_kernel(ids_ref, ridge_ref, own_ref, other_ref, o_ref, a, w, upper, inverse, stack1, stack2):
    core, position = ids_ref[0], ids_ref[1]
    eye = lax.broadcasted_iota(jnp.int32, (NB, NB), 0) == lax.broadcasted_iota(jnp.int32, (NB, NB), 1)
    for which in range(2):

        @pl.when(core == which)
        def _():
            for ref, strips in ((own_ref, STRIPS[which]), (other_ref, STRIPS[1 - which])):
                slot = 0
                for strip in strips:
                    for block in range(strip, PANELS):
                        piece = ref[NB * slot : NB * slot + NB, :]
                        if block == strip:
                            ridge = ridge_ref[0:1, NB * strip : NB * strip + NB]
                            piece = piece + jnp.where(eye, ridge, 0.0)
                        a[NB * strip : NB * strip + NB, NB * block : NB * block + NB] = piece
                        slot += 1

    def body(panel, carry):
        at = pl.multiple_of(panel * NB, NB)
        w[...] = a[pl.ds(at, NB), pl.ds(at, NB)]
        factor_block(w, upper, inverse)
        for fixed in range(PANELS):

            @pl.when(panel == fixed)
            def _():
                s0, s1 = NB * fixed, NB * fixed + NB
                a[s0:s1, s0:s1] = upper[...]
                if fixed < PANELS - 1:
                    inv, rest = pieces3(inverse[...]), pieces3(a[s0:s1, s1:])
                    rows = mm(
                        jnp.concatenate([inv[k] for k in LEFT], axis=1),
                        jnp.concatenate([rest[k] for k in RIGHT], axis=0),
                    )
                    a[s0:s1, s1:] = rows
                    width = FEAT - s1
                    parts = pieces3(rows)
                    for k in range(6):
                        stack1[NB * k : NB * k + NB, :width] = parts[LEFT[k]]
                        stack2[NB * k : NB * k + NB, :width] = parts[RIGHT[k]]
                    for strip in range(fixed + 1, PANELS):
                        b0, t0 = NB * (strip - fixed - 1), NB * strip
                        update = tmm(stack1[:, b0 : b0 + NB], stack2[:, b0:width])
                        a[t0 : t0 + NB, t0:] = a[t0 : t0 + NB, t0:] - update

        return carry

    lax.fori_loop(0, PANELS, body, 0)
    out = a[pl.ds(pl.multiple_of(position * 8, 8), 8), :]
    lane = lax.broadcasted_iota(jnp.int32, out.shape, 1)
    o_ref[...] = jnp.where(lane >= (position // 16) * NB, out, 0.0)


def factor_rows(ids, ridge, own, other):
    return pl.pallas_call(
        factor_kernel,
        out_shape=jax.ShapeDtypeStruct((8, FEAT), f32),
        in_specs=[SMEM, VMEM, VMEM, VMEM],
        out_specs=VMEM,
        scratch_shapes=[pltpu.VMEM((FEAT, FEAT), f32)] + [pltpu.VMEM((NB, NB), f32)] * 3
        + [pltpu.VMEM((6 * NB, FEAT), bf16)] * 2,
        compiler_params=params(),
        cost_estimate=pl.CostEstimate(flops=40_000_000_000, bytes_accessed=2 << 20, transcendentals=0),
    )(ids, ridge, own, other)


def swap_cores(x):
    return lax.ppermute(x, "outer", [(0, 1), (1, 0)])


def along_z(x, distance):
    return lax.ppermute(x, "inner", [(i, (i + 16 * distance) % 64) for i in range(64)])


def plane_exchange(x):
    return lax.all_to_all(x, "inner", 0, 0, axis_index_groups=PLANES, tiled=True)


def local(matrix, sign_flip, keep_list, ridge_weights):
    core, inner = lax.axis_index("outer"), lax.axis_index("inner")
    ids = jnp.stack([core, core * 64 + inner]).astype(jnp.int32)
    keep_here = lax.dynamic_index_in_dim(keep_list.reshape(2, 4, 16, 2), inner // 16, 1, False)
    keep_rows = jnp.repeat(keep_here.reshape(32, 2), 4, axis=0)
    mixed = local_mix(matrix, sign_flip)
    along = lax.all_to_all(
        mixed.reshape(4, 128, FEAT), "inner", 0, 0, axis_index_groups=Z_GROUPS, tiled=True
    )
    mine = select_rows(keep_rows, along).reshape(256, FEAT)
    theirs = swap_cores(mine)
    gram, to_send = gram_half(ids, mine, theirs)
    piece = jnp.sum(plane_exchange(gram), axis=0)
    piece = (piece + along_z(piece, 2)) + (along_z(piece, 1) + along_z(piece, 3))
    own = plane_exchange(jnp.broadcast_to(piece[None], (16, GRAM_ROWS, NB))).reshape(16 * GRAM_ROWS, NB)
    to_send, own = lax.optimization_barrier((to_send, own))
    received = plane_exchange(to_send)
    other = swap_cores(own)
    factor = factor_rows(ids, ridge_weights.reshape(1, FEAT), own, other)
    sketch = final_mix(ids, received.reshape(256, FEAT), factor)
    return sketch, factor


def solution(mesh):
    return jax.shard_map(
        local,
        mesh=mesh,
        in_specs=(P(("outer", "inner"), None), P(("outer", "inner")), P(), P()),
        out_specs=(P(("outer", "inner"), None), P(("outer", "inner"), None)),
        check_vma=False,
    )
```

```python
import jax
import jax.numpy as jnp
import numpy as np
from jax import lax
from jax.experimental import pallas as pl
from jax.experimental.pallas import tpu as pltpu
from jax.sharding import PartitionSpec as P

f32 = jnp.float32
bf16 = jnp.bfloat16
VMEM = pl.BlockSpec(memory_space=pltpu.VMEM)
SMEM = pl.BlockSpec(memory_space=pltpu.SMEM)
FEAT = 1024
NB = 128
PANELS = FEAT // NB
STRIPS = ((0, 3, 4, 7), (1, 2, 5, 6))
GRAM_ROWS = 144
DIRECT = 3
LEFT = (0, 0, 0, 1, 1, 2)
RIGHT = (0, 1, 2, 0, 1, 0)
Z_GROUPS = [[i + 16 * j for j in range(4)] for i in range(16)]
PLANES = [[16 * j + i for i in range(16)] for j in range(4)]


def params(mib=32):
    return pltpu.CompilerParams(vmem_limit_bytes=mib << 20)


def parity_sign(left, right):
    common = left & right
    parity = np.zeros_like(common)
    for shift_by in range(10):
        parity ^= (common >> shift_by) & 1
    return 1 - 2 * parity


def local_table():
    az, c, axy, e = np.meshgrid(range(4), range(2), range(16), range(4), indexing="ij")
    k = (az * 128 + axy * 8 + c * 4 + e).reshape(-1, 1)
    return parity_sign(k, np.arange(512)[None, :]).astype(np.float32).astype(bf16)


def final_table():
    j, i, o, e = (v.reshape(-1, 1) for v in np.meshgrid(range(2), range(16), range(2), range(4), indexing="ij"))
    ip, op, jp, ep = (v.reshape(1, -1) for v in np.meshgrid(range(16), range(2), range(2), range(4), indexing="ij"))
    table = parity_sign(i, ip) * parity_sign(o, op) * (j == jp) * (e == ep)
    return table.astype(np.float32).astype(bf16)


def halves(x):
    high = x.astype(bf16)
    return high, (x - high.astype(f32)).astype(bf16)


def mm(a, b):
    return jnp.dot(a, b, preferred_element_type=f32)


def tmm(a, b):
    return lax.dot_general(a, b, (((0,), (0,)), ((), ())), preferred_element_type=f32)


def local_mix_kernel(table_hbm, sign_hbm, x_hbm, o_hbm, table, sign, signed, x, out, sems):
    chunks, _, cols = x.shape

    def columns(ref, chunk):
        return ref.at[:, cols * chunk : cols * chunk + cols]

    def load(chunk):
        return pltpu.make_async_copy(columns(x_hbm, chunk), x.at[chunk], sems.at[chunk])

    def store(chunk):
        return pltpu.make_async_copy(out.at[chunk], columns(o_hbm, chunk), sems.at[chunks + chunk])

    get_table = pltpu.make_async_copy(table_hbm, table, sems.at[2 * chunks])
    get_sign = pltpu.make_async_copy(sign_hbm, sign, sems.at[2 * chunks + 1])
    get_sign.start()
    get_table.start()
    for chunk in range(chunks):
        load(chunk).start()
    get_sign.wait()
    get_table.wait()
    signed[...] = (table[...].astype(f32) * (sign[...].astype(f32) * 2.0**-13)).astype(bf16)
    for chunk in range(chunks):
        load(chunk).wait()
        high, low = halves(x[chunk])
        out[chunk] = mm(signed[...], high) + mm(signed[...], low)
        store(chunk).start()
    for chunk in range(chunks):
        store(chunk).wait()


def local_mix(matrix, sign_flip):
    rows, features = matrix.shape
    chunks = 4
    anywhere = pl.BlockSpec(memory_space=pl.ANY)
    block = pltpu.VMEM((chunks, rows, features // chunks), f32)
    return pl.pallas_call(
        local_mix_kernel,
        out_shape=jax.ShapeDtypeStruct((rows, features), f32),
        in_specs=[anywhere] * 3,
        out_specs=anywhere,
        scratch_shapes=[
            pltpu.VMEM((rows, rows), bf16),
            pltpu.VMEM((1, rows), jnp.int32),
            pltpu.VMEM((rows, rows), bf16),
            block,
            block,
            pltpu.SemaphoreType.DMA((2 * chunks + 2,)),
        ],
        compiler_params=params(60),
    )(jnp.asarray(local_table()), sign_flip.reshape(1, rows), matrix)


def select_kernel(keep_ref, y_ref, v_ref):
    y0, y1, y2, y3 = (y_ref[z] for z in range(4))
    s, d, s2, d2 = y0 + y1, y0 - y1, y2 + y3, y2 - y3

    def combo(which):
        low = (which & 1) == 1
        first = jnp.where(low, d, s)
        second = jnp.where(low, d2, s2)
        return first + jnp.where((which & 2) == 2, -second, second)

    shape = s.shape
    v0 = combo(jnp.broadcast_to(keep_ref[:, 0:1], shape))
    v1 = combo(jnp.broadcast_to(keep_ref[:, 1:2], shape))
    upper = (lax.broadcasted_iota(jnp.int32, shape, 0) & 7) < 4
    even = jnp.where(upper, v0, pltpu.roll(v1, 4, axis=0))
    odd = jnp.where(upper, pltpu.roll(v0, shape[0] - 4, axis=0), v1)
    v_ref[:, 0] = even.reshape(16, 8, shape[1])
    v_ref[:, 1] = odd.reshape(16, 8, shape[1])


def select_rows(keep_rows, y):
    cols = 256
    features = y.shape[2]
    return pl.pallas_call(
        select_kernel,
        grid=(features // cols,),
        out_shape=jax.ShapeDtypeStruct((16, 2, 8, features), f32),
        in_specs=[
            pl.BlockSpec((128, 2), lambda g: (0, 0)),
            pl.BlockSpec((4, 128, cols), lambda g: (0, 0, g)),
        ],
        out_specs=pl.BlockSpec((16, 2, 8, cols), lambda g: (0, 0, 0, g)),
        compiler_params=params(),
    )(keep_rows, y)


def gram_kernel(ids_ref, v_ref, w_ref, g_ref, s_ref, high, low, flat):
    core = ids_ref[0]
    own = pl.ds(pl.multiple_of(core * 128, 128), 128)
    for part, ref in enumerate((v_ref, w_ref)):
        h, l = halves(ref[...])
        high[256 * part : 256 * part + 256, :] = h
        low[256 * part : 256 * part + 256, :] = l
        s_ref[:, part] = ref[own, :].reshape(16, 8, FEAT)
    for which, strips in enumerate(STRIPS):

        @pl.when(core == which)
        def _():
            row = 0
            for strip in strips:
                at = NB * strip
                h, l = high[:, at : at + NB], low[:, at : at + NB]
                total = tmm(h, high[:, at:]) + (tmm(h, low[:, at:]) + tmm(l, high[:, at:]))
                for block in range(PANELS - strip):
                    flat[row : row + NB, :] = total[:, NB * block : NB * block + NB]
                    row += NB

    for piece in range(16):
        g_ref[piece] = flat[GRAM_ROWS * piece : GRAM_ROWS * (piece + 1), :]


def gram_half(ids, mine, theirs):
    rows = mine.shape[0]
    return pl.pallas_call(
        gram_kernel,
        out_shape=(
            jax.ShapeDtypeStruct((16, GRAM_ROWS, NB), f32),
            jax.ShapeDtypeStruct((16, 2, 8, FEAT), f32),
        ),
        in_specs=[SMEM, VMEM, VMEM],
        out_specs=(VMEM, VMEM),
        scratch_shapes=[pltpu.VMEM((2 * rows, FEAT), bf16)] * 2 + [pltpu.VMEM((16 * GRAM_ROWS, NB), f32)],
        compiler_params=params(),
    )(ids, mine, theirs)


def final_kernel(ids_ref, table_ref, r_ref, o_ref):
    high, low = halves(r_ref[...])
    total = mm(table_ref[...], high) + mm(table_ref[...], low)
    odd = (lax.broadcasted_iota(jnp.int32, total.shape, 0) >> 2) & 1
    flip = (odd * ids_ref[0]) == 1
    o_ref[...] = total * jnp.where(flip, -32.0, 32.0)


def final_mix(ids, received):
    return pl.pallas_call(
        final_kernel,
        out_shape=jax.ShapeDtypeStruct(received.shape, f32),
        in_specs=[SMEM, VMEM, VMEM],
        out_specs=VMEM,
        compiler_params=params(),
    )(ids, jnp.asarray(final_table()), received)


def lane_splat(x, lane):
    return jnp.broadcast_to(x[:, lane : lane + 1], (8, NB))


def thirds(x):
    high = x.astype(bf16).astype(f32)
    rest = x - high
    middle = rest.astype(bf16).astype(f32)
    return high, middle, rest - middle


def pieces3(x):
    return tuple(part.astype(bf16) for part in thirds(x))


def outer_sum(left, right):
    lh, lm, ll = thirds(left)
    rh, rm, rl = thirds(right)
    stacked_left = jnp.concatenate([lh, lh, lh, lm, lm, ll], axis=0).astype(bf16)
    stacked_right = jnp.concatenate([rh, rm, rl, rh, rm, rh], axis=0).astype(bf16)
    return tmm(stacked_left, stacked_right)


def tree_sum(terms):
    while len(terms) > 1:
        terms = [x + y for x, y in zip(terms[::2], terms[1::2])]
    return terms[0]


def row_splat(x, row):
    return jnp.broadcast_to(x[row : row + 1, :], (8, NB))


def by_row(sub, values):
    a = [jnp.where((sub & 1) == 0, values[k], values[k + 1]) for k in (0, 2, 4, 6)]
    b = [jnp.where((sub & 2) == 0, a[k], a[k + 1]) for k in (0, 2)]
    return jnp.where(sub < 4, b[0], b[1])


def factor_block(w, upper, inverse):
    lane = lax.broadcasted_iota(jnp.int32, (8, NB), 1)
    sub = lax.broadcasted_iota(jnp.int32, (8, NB), 0)
    groups = NB // 8
    rows = w[0:8, :]
    e = [lane_splat(rows, a) for a in range(8)]
    held = {}
    for step in range(groups):
        base = 8 * step
        inside = (lane >= base) & (lane < base + 8)
        last = min(step + DIRECT, groups - 1)
        near = range(step + 1, last + 1)
        for group in near:
            if group not in held:
                held[group] = w[8 * group : 8 * group + 8, :]
        columns = {group: [lane_splat(held[group], base + b) for b in range(8)] for group in near}
        if near:
            start = [lane_splat(held[step + 1], base + 8 + a) for a in range(8)]
        aug = jnp.where(inside, jnp.where(lane == base + sub, 1.0, 0.0), rows)
        scales, finished = [], []
        multipliers = {group: [] for group in near}
        for b in range(8):
            r = lax.rsqrt(row_splat(e[b], b))
            scales.append(r)
            multiplier = jnp.where(sub > b, e[b], 0.0) * r
            c = {a: row_splat(e[a], b) * r for a in range(b + 1, 8)}
            scaled = row_splat(aug, b) * r
            finished.append(scaled)
            if b < 7:
                for a in range(b + 1, 8):
                    e[a] = e[a] - multiplier * c[a]
                rows = rows - multiplier * (row_splat(rows, b) * r)
                aug = aug - multiplier * scaled
            for group in near:
                column = columns[group]
                multipliers[group].append(column[b] * r)
                for a in range(b + 1, 8):
                    column[a] = column[a] - multipliers[group][b] * c[a]
        scale = by_row(sub, scales)
        left, right = rows * scale, aug * scale
        upper[base : base + 8, :] = jnp.where(lane >= base + sub, left, 0.0)
        inverse[base : base + 8, :] = jnp.where(lane <= base + sub, right, 0.0)
        if not near:
            break
        if last < groups - 1:
            update = outer_sum(left, right)
        m = multipliers[step + 1]
        e = [start[a] - tree_sum([m[b] * row_splat(m[b], a) for b in range(8)]) for a in range(8)]
        for group in near:
            terms = [multipliers[group][b] * finished[b] for b in range(8)]
            held[group] = jnp.where(inside, 0.0, held[group]) - tree_sum(terms)
        rows = held.pop(step + 1)
        if last < groups - 1:
            after = 8 * (last + 1)
            rest = lax.broadcasted_iota(jnp.int32, (NB - after, NB), 1)
            cleared = jnp.where((rest >= base) & (rest < base + 8), 0.0, w[after:, :])
            w[after:, :] = cleared - update[after:, :]


def factor_kernel(ids_ref, ridge_ref, own_ref, other_ref, o_ref, done_ref, a, w, upper, inverse, stack1, stack2):
    core, position = ids_ref[0], ids_ref[1]
    done_ref[0], done_ref[1] = core, position
    eye = lax.broadcasted_iota(jnp.int32, (NB, NB), 0) == lax.broadcasted_iota(jnp.int32, (NB, NB), 1)
    for which in range(2):

        @pl.when(core == which)
        def _():
            for ref, strips in ((own_ref, STRIPS[which]), (other_ref, STRIPS[1 - which])):
                slot = 0
                for strip in strips:
                    for block in range(strip, PANELS):
                        piece = ref[NB * slot : NB * slot + NB, :]
                        if block == strip:
                            ridge = ridge_ref[0:1, NB * strip : NB * strip + NB]
                            piece = piece + jnp.where(eye, ridge, 0.0)
                        a[NB * strip : NB * strip + NB, NB * block : NB * block + NB] = piece
                        slot += 1

    def body(panel, carry):
        at = pl.multiple_of(panel * NB, NB)
        w[...] = a[pl.ds(at, NB), pl.ds(at, NB)]
        factor_block(w, upper, inverse)
        for fixed in range(PANELS):

            @pl.when(panel == fixed)
            def _():
                s0, s1 = NB * fixed, NB * fixed + NB
                a[s0:s1, s0:s1] = upper[...]
                if fixed < PANELS - 1:
                    inv, rest = pieces3(inverse[...]), pieces3(a[s0:s1, s1:])
                    rows = mm(
                        jnp.concatenate([inv[k] for k in LEFT], axis=1),
                        jnp.concatenate([rest[k] for k in RIGHT], axis=0),
                    )
                    a[s0:s1, s1:] = rows
                    width = FEAT - s1
                    parts = pieces3(rows)
                    for k in range(6):
                        stack1[NB * k : NB * k + NB, :width] = parts[LEFT[k]]
                        stack2[NB * k : NB * k + NB, :width] = parts[RIGHT[k]]
                    for strip in range(fixed + 1, PANELS):
                        b0, t0 = NB * (strip - fixed - 1), NB * strip
                        update = tmm(stack1[:, b0 : b0 + NB], stack2[:, b0:width])
                        a[t0 : t0 + NB, t0:] = a[t0 : t0 + NB, t0:] - update

        return carry

    lax.fori_loop(0, PANELS, body, 0)
    out = a[pl.ds(pl.multiple_of(position * 8, 8), 8), :]
    lane = lax.broadcasted_iota(jnp.int32, out.shape, 1)
    o_ref[...] = jnp.where(lane >= (position // 16) * NB, out, 0.0)


def factor_rows(ids, ridge, own, other):
    return pl.pallas_call(
        factor_kernel,
        out_shape=(jax.ShapeDtypeStruct((8, FEAT), f32), jax.ShapeDtypeStruct((2,), jnp.int32)),
        in_specs=[SMEM, VMEM, VMEM, VMEM],
        out_specs=(VMEM, SMEM),
        scratch_shapes=[pltpu.VMEM((FEAT, FEAT), f32)] + [pltpu.VMEM((NB, NB), f32)] * 3
        + [pltpu.VMEM((6 * NB, FEAT), bf16)] * 2,
        compiler_params=params(),
        cost_estimate=pl.CostEstimate(flops=40_000_000_000, bytes_accessed=2 << 20, transcendentals=0),
    )(ids, ridge, own, other)


def swap_cores(x):
    return lax.ppermute(x, "outer", [(0, 1), (1, 0)])


def along_z(x, distance):
    return lax.ppermute(x, "inner", [(i, (i + 16 * distance) % 64) for i in range(64)])


def plane_exchange(x):
    return lax.all_to_all(x, "inner", 0, 0, axis_index_groups=PLANES, tiled=True)


def local(matrix, sign_flip, keep_list, ridge_weights):
    core, inner = lax.axis_index("outer"), lax.axis_index("inner")
    ids = jnp.stack([core, core * 64 + inner]).astype(jnp.int32)
    keep_here = lax.dynamic_index_in_dim(keep_list.reshape(2, 4, 16, 2), inner // 16, 1, False)
    keep_rows = jnp.repeat(keep_here.reshape(32, 2), 4, axis=0)
    mixed = local_mix(matrix, sign_flip)
    along = lax.all_to_all(
        mixed.reshape(4, 128, FEAT), "inner", 0, 0, axis_index_groups=Z_GROUPS, tiled=True
    )
    mine = select_rows(keep_rows, along).reshape(256, FEAT)
    theirs = swap_cores(mine)
    gram, to_send = gram_half(ids, mine, theirs)
    piece = jnp.sum(plane_exchange(gram), axis=0)
    piece = (piece + along_z(piece, 2)) + (along_z(piece, 1) + along_z(piece, 3))
    own = plane_exchange(jnp.broadcast_to(piece[None], (16, GRAM_ROWS, NB))).reshape(16 * GRAM_ROWS, NB)
    to_send, own = lax.optimization_barrier((to_send, own))
    received = plane_exchange(to_send)
    other = swap_cores(own)
    factor, done = factor_rows(ids, ridge_weights.reshape(1, FEAT), own, other)
    sketch = final_mix(done, received.reshape(256, FEAT))
    return sketch, factor


def solution(mesh):
    return jax.shard_map(
        local,
        mesh=mesh,
        in_specs=(P(("outer", "inner"), None), P(("outer", "inner")), P(), P()),
        out_specs=(P(("outer", "inner"), None), P(("outer", "inner"), None)),
        check_vma=False,
    )
```

```python
import jax
import jax.numpy as jnp
import numpy as np
from jax import lax
from jax.experimental import pallas as pl
from jax.experimental.pallas import tpu as pltpu
from jax.sharding import PartitionSpec as P

f32 = jnp.float32
bf16 = jnp.bfloat16
VMEM = pl.BlockSpec(memory_space=pltpu.VMEM)
SMEM = pl.BlockSpec(memory_space=pltpu.SMEM)
ANY = pl.BlockSpec(memory_space=pl.ANY)
FEAT = 1024
NB = 128
PANELS = FEAT // NB
STRIPS = ((0, 3, 4, 7), (1, 2, 5, 6))
GRAM_ROWS = 144
DIRECT = 3
LEFT = (0, 0, 0, 1, 1, 2)
RIGHT = (0, 1, 2, 0, 1, 0)
Z_GROUPS = [[i + 16 * j for j in range(4)] for i in range(16)]
PLANES = [[16 * j + i for i in range(16)] for j in range(4)]


def params(mib=32):
    return pltpu.CompilerParams(vmem_limit_bytes=mib << 20)


def parity_sign(left, right):
    common = left & right
    parity = np.zeros_like(common)
    for shift_by in range(10):
        parity ^= (common >> shift_by) & 1
    return 1 - 2 * parity


def local_table():
    az, c, axy, e = np.meshgrid(range(4), range(2), range(16), range(4), indexing="ij")
    k = (az * 128 + axy * 8 + c * 4 + e).reshape(-1, 1)
    return parity_sign(k, np.arange(512)[None, :]).astype(np.float32).astype(bf16)


def final_table():
    j, i, o, e = (v.reshape(-1, 1) for v in np.meshgrid(range(2), range(16), range(2), range(4), indexing="ij"))
    ip, op, jp, ep = (v.reshape(1, -1) for v in np.meshgrid(range(16), range(2), range(2), range(4), indexing="ij"))
    table = parity_sign(i, ip) * parity_sign(o, op) * (j == jp) * (e == ep)
    return table.astype(np.float32).astype(bf16)


def halves(x):
    high = x.astype(bf16)
    return high, (x - high.astype(f32)).astype(bf16)


def mm(a, b):
    return jnp.dot(a, b, preferred_element_type=f32)


def tmm(a, b):
    return lax.dot_general(a, b, (((0,), (0,)), ((), ())), preferred_element_type=f32)


def local_mix_kernel(table_hbm, sign_hbm, x_hbm, o_hbm, table, sign, signed, x, out, sems):
    chunks, _, cols = x.shape

    def columns(ref, chunk):
        return ref.at[:, cols * chunk : cols * chunk + cols]

    def load(chunk):
        return pltpu.make_async_copy(columns(x_hbm, chunk), x.at[chunk], sems.at[chunk])

    def store(chunk):
        return pltpu.make_async_copy(out.at[chunk], columns(o_hbm, chunk), sems.at[chunks + chunk])

    get_table = pltpu.make_async_copy(table_hbm, table, sems.at[2 * chunks])
    get_sign = pltpu.make_async_copy(sign_hbm, sign, sems.at[2 * chunks + 1])
    get_sign.start()
    get_table.start()
    for chunk in range(chunks):
        load(chunk).start()
    get_sign.wait()
    get_table.wait()
    signed[...] = (table[...].astype(f32) * (sign[...].astype(f32) * 2.0**-13)).astype(bf16)
    for chunk in range(chunks):
        load(chunk).wait()
        high, low = halves(x[chunk])
        out[chunk] = mm(signed[...], high) + mm(signed[...], low)
        store(chunk).start()
    for chunk in range(chunks):
        store(chunk).wait()


def local_mix(matrix, sign_flip):
    rows, features = matrix.shape
    chunks = 4
    anywhere = pl.BlockSpec(memory_space=pl.ANY)
    block = pltpu.VMEM((chunks, rows, features // chunks), f32)
    return pl.pallas_call(
        local_mix_kernel,
        out_shape=jax.ShapeDtypeStruct((rows, features), f32),
        in_specs=[anywhere] * 3,
        out_specs=anywhere,
        scratch_shapes=[
            pltpu.VMEM((rows, rows), bf16),
            pltpu.VMEM((1, rows), jnp.int32),
            pltpu.VMEM((rows, rows), bf16),
            block,
            block,
            pltpu.SemaphoreType.DMA((2 * chunks + 2,)),
        ],
        compiler_params=params(60),
    )(jnp.asarray(local_table()), sign_flip.reshape(1, rows), matrix)


def select_kernel(keep_ref, y_ref, v_ref):
    y0, y1, y2, y3 = (y_ref[z] for z in range(4))
    s, d, s2, d2 = y0 + y1, y0 - y1, y2 + y3, y2 - y3

    def combo(which):
        low = (which & 1) == 1
        first = jnp.where(low, d, s)
        second = jnp.where(low, d2, s2)
        return first + jnp.where((which & 2) == 2, -second, second)

    shape = s.shape
    v0 = combo(jnp.broadcast_to(keep_ref[:, 0:1], shape))
    v1 = combo(jnp.broadcast_to(keep_ref[:, 1:2], shape))
    upper = (lax.broadcasted_iota(jnp.int32, shape, 0) & 7) < 4
    even = jnp.where(upper, v0, pltpu.roll(v1, 4, axis=0))
    odd = jnp.where(upper, pltpu.roll(v0, shape[0] - 4, axis=0), v1)
    v_ref[:, 0] = even.reshape(16, 8, shape[1])
    v_ref[:, 1] = odd.reshape(16, 8, shape[1])


def select_rows(keep_rows, y):
    cols = 256
    features = y.shape[2]
    return pl.pallas_call(
        select_kernel,
        grid=(features // cols,),
        out_shape=jax.ShapeDtypeStruct((16, 2, 8, features), f32),
        in_specs=[
            pl.BlockSpec((128, 2), lambda g: (0, 0)),
            pl.BlockSpec((4, 128, cols), lambda g: (0, 0, g)),
        ],
        out_specs=pl.BlockSpec((16, 2, 8, cols), lambda g: (0, 0, 0, g)),
        compiler_params=params(),
    )(keep_rows, y)


def gram_kernel(ids_ref, v_ref, w_hbm, g_ref, s_hbm, high, low, flat, w_ref, sems):
    core = ids_ref[0]
    fetch = pltpu.make_async_copy(w_hbm, w_ref, sems.at[0])
    fetch.start()
    send_mine = pltpu.make_async_copy(v_ref.at[core], s_hbm.at[:, 0], sems.at[1])
    send_mine.start()
    send_theirs = pltpu.make_async_copy(w_ref.at[core], s_hbm.at[:, 1], sems.at[2])
    for part, ref in enumerate((v_ref, w_ref)):
        if part:
            fetch.wait()
            send_theirs.start()
        h, l = halves(ref[...].reshape(256, FEAT))
        high[256 * part : 256 * part + 256, :] = h
        low[256 * part : 256 * part + 256, :] = l
    for which, strips in enumerate(STRIPS):

        @pl.when(core == which)
        def _():
            row = 0
            for strip in strips:
                at = NB * strip
                h, l = high[:, at : at + NB], low[:, at : at + NB]
                total = tmm(h, high[:, at:]) + (tmm(h, low[:, at:]) + tmm(l, high[:, at:]))
                for block in range(PANELS - strip):
                    flat[row : row + NB, :] = total[:, NB * block : NB * block + NB]
                    row += NB

    for piece in range(16):
        g_ref[piece] = flat[GRAM_ROWS * piece : GRAM_ROWS * (piece + 1), :]
    send_mine.wait()
    send_theirs.wait()


def gram_half(ids, mine, theirs):
    return pl.pallas_call(
        gram_kernel,
        out_shape=(
            jax.ShapeDtypeStruct((16, GRAM_ROWS, NB), f32),
            jax.ShapeDtypeStruct((16, 2, 8, FEAT), f32),
        ),
        in_specs=[SMEM, VMEM, ANY],
        out_specs=(VMEM, ANY),
        scratch_shapes=[pltpu.VMEM((512, FEAT), bf16)] * 2
        + [
            pltpu.VMEM((16 * GRAM_ROWS, NB), f32),
            pltpu.VMEM(mine.shape, f32),
            pltpu.SemaphoreType.DMA((3,)),
        ],
        compiler_params=params(),
    )(ids, mine, theirs)


def final_kernel(ids_ref, table_ref, r_ref, o_hbm, out, sems):
    chunks, rows, cols = out.shape
    odd = (lax.broadcasted_iota(jnp.int32, (rows, cols), 0) >> 2) & 1
    factor = jnp.where((odd * ids_ref[0]) == 1, -32.0, 32.0)

    def store(chunk):
        target = o_hbm.at[:, cols * chunk : cols * chunk + cols]
        return pltpu.make_async_copy(out.at[chunk], target, sems.at[chunk])

    for chunk in range(chunks):
        high, low = halves(r_ref[:, cols * chunk : cols * chunk + cols])
        out[chunk] = (mm(table_ref[...], high) + mm(table_ref[...], low)) * factor
        store(chunk).start()
    for chunk in range(chunks):
        store(chunk).wait()


def final_mix(ids, received):
    rows, features = received.shape
    chunks = 4
    return pl.pallas_call(
        final_kernel,
        out_shape=jax.ShapeDtypeStruct(received.shape, f32),
        in_specs=[SMEM, VMEM, VMEM],
        out_specs=ANY,
        scratch_shapes=[
            pltpu.VMEM((chunks, rows, features // chunks), f32),
            pltpu.SemaphoreType.DMA((chunks,)),
        ],
        compiler_params=params(),
    )(ids, jnp.asarray(final_table()), received)


def lane_splat(x, lane):
    return jnp.broadcast_to(x[:, lane : lane + 1], (8, NB))


def thirds(x):
    high = x.astype(bf16).astype(f32)
    rest = x - high
    middle = rest.astype(bf16).astype(f32)
    return high, middle, rest - middle


def pieces3(x):
    return tuple(part.astype(bf16) for part in thirds(x))


def outer_sum(left, right):
    lh, lm, ll = thirds(left)
    rh, rm, rl = thirds(right)
    stacked_left = jnp.concatenate([lh, lh, lh, lm, lm, ll], axis=0).astype(bf16)
    stacked_right = jnp.concatenate([rh, rm, rl, rh, rm, rh], axis=0).astype(bf16)
    return tmm(stacked_left, stacked_right)


def tree_sum(terms):
    while len(terms) > 1:
        terms = [x + y for x, y in zip(terms[::2], terms[1::2])]
    return terms[0]


def row_splat(x, row):
    return jnp.broadcast_to(x[row : row + 1, :], (8, NB))


def by_row(sub, values):
    a = [jnp.where((sub & 1) == 0, values[k], values[k + 1]) for k in (0, 2, 4, 6)]
    b = [jnp.where((sub & 2) == 0, a[k], a[k + 1]) for k in (0, 2)]
    return jnp.where(sub < 4, b[0], b[1])


def factor_block(w, upper, inverse):
    lane = lax.broadcasted_iota(jnp.int32, (8, NB), 1)
    sub = lax.broadcasted_iota(jnp.int32, (8, NB), 0)
    groups = NB // 8
    rows = w[0:8, :]
    e = [lane_splat(rows, a) for a in range(8)]
    held = {}
    for step in range(groups):
        base = 8 * step
        inside = (lane >= base) & (lane < base + 8)
        last = min(step + DIRECT, groups - 1)
        near = range(step + 1, last + 1)
        for group in near:
            if group not in held:
                held[group] = w[8 * group : 8 * group + 8, :]
        columns = {group: [lane_splat(held[group], base + b) for b in range(8)] for group in near}
        if near:
            start = [lane_splat(held[step + 1], base + 8 + a) for a in range(8)]
        aug = jnp.where(inside, jnp.where(lane == base + sub, 1.0, 0.0), rows)
        scales, finished = [], []
        multipliers = {group: [] for group in near}
        for b in range(8):
            r = lax.rsqrt(row_splat(e[b], b))
            scales.append(r)
            multiplier = jnp.where(sub > b, e[b], 0.0) * r
            c = {a: row_splat(e[a], b) * r for a in range(b + 1, 8)}
            scaled = row_splat(aug, b) * r
            finished.append(scaled)
            if b < 7:
                for a in range(b + 1, 8):
                    e[a] = e[a] - multiplier * c[a]
                rows = rows - multiplier * (row_splat(rows, b) * r)
                aug = aug - multiplier * scaled
            for group in near:
                column = columns[group]
                multipliers[group].append(column[b] * r)
                for a in range(b + 1, 8):
                    column[a] = column[a] - multipliers[group][b] * c[a]
        scale = by_row(sub, scales)
        left, right = rows * scale, aug * scale
        upper[base : base + 8, :] = jnp.where(lane >= base + sub, left, 0.0)
        inverse[base : base + 8, :] = jnp.where(lane <= base + sub, right, 0.0)
        if not near:
            break
        if last < groups - 1:
            update = outer_sum(left, right)
        m = multipliers[step + 1]
        e = [start[a] - tree_sum([m[b] * row_splat(m[b], a) for b in range(8)]) for a in range(8)]
        for group in near:
            terms = [multipliers[group][b] * finished[b] for b in range(8)]
            held[group] = jnp.where(inside, 0.0, held[group]) - tree_sum(terms)
        rows = held.pop(step + 1)
        if last < groups - 1:
            after = 8 * (last + 1)
            rest = lax.broadcasted_iota(jnp.int32, (NB - after, NB), 1)
            cleared = jnp.where((rest >= base) & (rest < base + 8), 0.0, w[after:, :])
            w[after:, :] = cleared - update[after:, :]


def factor_kernel(ids_ref, ridge_ref, own_ref, other_hbm, o_ref, done_ref, other_ref, sem, a, w, upper, inverse, stack1, stack2):
    core, position = ids_ref[0], ids_ref[1]
    done_ref[0], done_ref[1] = core, position
    fetch = pltpu.make_async_copy(other_hbm, other_ref, sem)
    fetch.start()
    eye = lax.broadcasted_iota(jnp.int32, (NB, NB), 0) == lax.broadcasted_iota(jnp.int32, (NB, NB), 1)

    def assemble(ref, strips):
        slot = 0
        for strip in strips:
            for block in range(strip, PANELS):
                piece = ref[NB * slot : NB * slot + NB, :]
                if block == strip:
                    piece = piece + jnp.where(eye, ridge_ref[0:1, NB * strip : NB * strip + NB], 0.0)
                a[NB * strip : NB * strip + NB, NB * block : NB * block + NB] = piece
                slot += 1

    for ref, offset in ((own_ref, 0), (other_ref, 1)):
        if offset:
            fetch.wait()
        for which in range(2):
            pl.when(core == which)(lambda: assemble(ref, STRIPS[which ^ offset]))

    def body(panel, carry):
        at = pl.multiple_of(panel * NB, NB)
        w[...] = a[pl.ds(at, NB), pl.ds(at, NB)]
        factor_block(w, upper, inverse)
        for fixed in range(PANELS):

            @pl.when(panel == fixed)
            def _():
                s0, s1 = NB * fixed, NB * fixed + NB
                a[s0:s1, s0:s1] = upper[...]
                if fixed < PANELS - 1:
                    inv, rest = pieces3(inverse[...]), pieces3(a[s0:s1, s1:])
                    rows = mm(
                        jnp.concatenate([inv[k] for k in LEFT], axis=1),
                        jnp.concatenate([rest[k] for k in RIGHT], axis=0),
                    )
                    a[s0:s1, s1:] = rows
                    width = FEAT - s1
                    parts = pieces3(rows)
                    for k in range(6):
                        stack1[NB * k : NB * k + NB, :width] = parts[LEFT[k]]
                        stack2[NB * k : NB * k + NB, :width] = parts[RIGHT[k]]
                    for strip in range(fixed + 1, PANELS):
                        b0, t0 = NB * (strip - fixed - 1), NB * strip
                        update = tmm(stack1[:, b0 : b0 + NB], stack2[:, b0:width])
                        a[t0 : t0 + NB, t0:] = a[t0 : t0 + NB, t0:] - update

        return carry

    lax.fori_loop(0, PANELS, body, 0)
    out = a[pl.ds(pl.multiple_of(position * 8, 8), 8), :]
    lane = lax.broadcasted_iota(jnp.int32, out.shape, 1)
    o_ref[...] = jnp.where(lane >= (position // 16) * NB, out, 0.0)


def factor_rows(ids, ridge, own, other):
    return pl.pallas_call(
        factor_kernel,
        out_shape=(jax.ShapeDtypeStruct((8, FEAT), f32), jax.ShapeDtypeStruct((2,), jnp.int32)),
        in_specs=[SMEM, VMEM, VMEM, ANY],
        out_specs=(VMEM, SMEM),
        scratch_shapes=[pltpu.VMEM(other.shape, f32), pltpu.SemaphoreType.DMA(())]
        + [pltpu.VMEM((FEAT, FEAT), f32)] + [pltpu.VMEM((NB, NB), f32)] * 3
        + [pltpu.VMEM((6 * NB, FEAT), bf16)] * 2,
        compiler_params=params(),
        cost_estimate=pl.CostEstimate(flops=40_000_000_000, bytes_accessed=2 << 20, transcendentals=0),
    )(ids, ridge, own, other)


def swap_cores(x):
    return lax.ppermute(x, "outer", [(0, 1), (1, 0)])


def along_z(x, distance):
    return lax.ppermute(x, "inner", [(i, (i + 16 * distance) % 64) for i in range(64)])


def plane_exchange(x):
    return lax.all_to_all(x, "inner", 0, 0, axis_index_groups=PLANES, tiled=True)


def local(matrix, sign_flip, keep_list, ridge_weights):
    core, inner = lax.axis_index("outer"), lax.axis_index("inner")
    ids = jnp.stack([core, core * 64 + inner]).astype(jnp.int32)
    keep_here = lax.dynamic_index_in_dim(keep_list.reshape(2, 4, 16, 2), inner // 16, 1, False)
    keep_rows = jnp.repeat(keep_here.reshape(32, 2), 4, axis=0)
    mixed = local_mix(matrix, sign_flip)
    along = lax.all_to_all(
        mixed.reshape(4, 128, FEAT), "inner", 0, 0, axis_index_groups=Z_GROUPS, tiled=True
    )
    mine = select_rows(keep_rows, along).reshape(2, 16, 8, FEAT)
    theirs = swap_cores(mine)
    gram, to_send = gram_half(ids, mine, theirs)
    piece = jnp.sum(plane_exchange(gram), axis=0)
    piece = (piece + along_z(piece, 2)) + (along_z(piece, 1) + along_z(piece, 3))
    own = plane_exchange(jnp.broadcast_to(piece[None], (16, GRAM_ROWS, NB))).reshape(16 * GRAM_ROWS, NB)
    to_send, own = lax.optimization_barrier((to_send, own))
    received = plane_exchange(to_send)
    other = swap_cores(own)
    factor, done = factor_rows(ids, ridge_weights.reshape(1, FEAT), own, other)
    sketch = final_mix(done, received.reshape(256, FEAT))
    return sketch, factor


def solution(mesh):
    return jax.shard_map(
        local,
        mesh=mesh,
        in_specs=(P(("outer", "inner"), None), P(("outer", "inner")), P(), P()),
        out_specs=(P(("outer", "inner"), None), P(("outer", "inner"), None)),
        check_vma=False,
    )
```

```python
import jax
import jax.numpy as jnp
import numpy as np
from jax import lax
from jax.experimental import pallas as pl
from jax.experimental.pallas import tpu as pltpu
from jax.sharding import PartitionSpec as P

f32 = jnp.float32
bf16 = jnp.bfloat16
VMEM = pl.BlockSpec(memory_space=pltpu.VMEM)
SMEM = pl.BlockSpec(memory_space=pltpu.SMEM)
ANY = pl.BlockSpec(memory_space=pl.ANY)
FEAT = 1024
NB = 128
PANELS = FEAT // NB
STRIPS = ((0, 3, 4, 7), (1, 2, 5, 6))
GRAM_ROWS = 144
DIRECT = 3
LEFT = (0, 0, 0, 1, 1, 2)
RIGHT = (0, 1, 2, 0, 1, 0)
Z_GROUPS = [[i + 16 * j for j in range(4)] for i in range(16)]
PLANES = [[16 * j + i for i in range(16)] for j in range(4)]


def params(mib=32):
    return pltpu.CompilerParams(vmem_limit_bytes=mib << 20)


def parity_sign(left, right):
    common = left & right
    parity = np.zeros_like(common)
    for shift_by in range(10):
        parity ^= (common >> shift_by) & 1
    return 1 - 2 * parity


def local_table():
    az, c, axy, e = np.meshgrid(range(4), range(2), range(16), range(4), indexing="ij")
    k = (az * 128 + axy * 8 + c * 4 + e).reshape(-1, 1)
    return parity_sign(k, np.arange(512)[None, :]).astype(np.float32).astype(bf16)


def final_table():
    j, i, o, e = (v.reshape(-1, 1) for v in np.meshgrid(range(2), range(16), range(2), range(4), indexing="ij"))
    ip, op, jp, ep = (v.reshape(1, -1) for v in np.meshgrid(range(16), range(2), range(2), range(4), indexing="ij"))
    table = parity_sign(i, ip) * parity_sign(o, op) * (j == jp) * (e == ep)
    return table.astype(np.float32).astype(bf16)


def halves(x):
    high = x.astype(bf16)
    return high, (x - high.astype(f32)).astype(bf16)


def mm(a, b):
    return jnp.dot(a, b, preferred_element_type=f32)


def tmm(a, b):
    return lax.dot_general(a, b, (((0,), (0,)), ((), ())), preferred_element_type=f32)


def local_mix_kernel(table_hbm, sign_hbm, x_hbm, o_hbm, table, sign, signed, x, out, sems):
    chunks, _, cols = out.shape

    def load(chunk):
        part = pl.ds(128 * chunk, 128)
        return pltpu.make_async_copy(x_hbm.at[part], x.at[part], sems.at[chunk])

    def store(chunk):
        target = o_hbm.at[:, cols * chunk : cols * chunk + cols]
        return pltpu.make_async_copy(out.at[chunk], target, sems.at[chunks + chunk])

    get_table = pltpu.make_async_copy(table_hbm, table, sems.at[2 * chunks])
    get_sign = pltpu.make_async_copy(sign_hbm, sign, sems.at[2 * chunks + 1])
    get_sign.start()
    get_table.start()
    for chunk in range(chunks):
        load(chunk).start()
    get_sign.wait()
    get_table.wait()
    signed[...] = (table[...].astype(f32) * (sign[...].astype(f32) * 2.0**-13)).astype(bf16)
    for chunk in range(chunks):
        load(chunk).wait()
    for chunk in range(chunks):
        high, low = halves(x[:, cols * chunk : cols * chunk + cols])
        out[chunk] = mm(signed[...], high) + mm(signed[...], low)
        store(chunk).start()
    for chunk in range(chunks):
        store(chunk).wait()


def local_mix(matrix, sign_flip):
    rows, features = matrix.shape
    chunks = 4
    anywhere = pl.BlockSpec(memory_space=pl.ANY)
    block = pltpu.VMEM((chunks, rows, features // chunks), f32)
    return pl.pallas_call(
        local_mix_kernel,
        out_shape=jax.ShapeDtypeStruct((rows, features), f32),
        in_specs=[anywhere] * 3,
        out_specs=anywhere,
        scratch_shapes=[
            pltpu.VMEM((rows, rows), bf16),
            pltpu.VMEM((1, rows), jnp.int32),
            pltpu.VMEM((rows, rows), bf16),
            pltpu.VMEM((rows, features), f32),
            block,
            pltpu.SemaphoreType.DMA((2 * chunks + 2,)),
        ],
        compiler_params=params(60),
    )(jnp.asarray(local_table()), sign_flip.reshape(1, rows), matrix)


def select_kernel(keep_ref, y_ref, v_ref):
    y0, y1, y2, y3 = (y_ref[z] for z in range(4))
    s, d, s2, d2 = y0 + y1, y0 - y1, y2 + y3, y2 - y3

    def combo(which):
        low = (which & 1) == 1
        first = jnp.where(low, d, s)
        second = jnp.where(low, d2, s2)
        return first + jnp.where((which & 2) == 2, -second, second)

    shape = s.shape
    v0 = combo(jnp.broadcast_to(keep_ref[:, 0:1], shape))
    v1 = combo(jnp.broadcast_to(keep_ref[:, 1:2], shape))
    upper = (lax.broadcasted_iota(jnp.int32, shape, 0) & 7) < 4
    even = jnp.where(upper, v0, pltpu.roll(v1, 4, axis=0))
    odd = jnp.where(upper, pltpu.roll(v0, shape[0] - 4, axis=0), v1)
    v_ref[:, 0] = even.reshape(16, 8, shape[1])
    v_ref[:, 1] = odd.reshape(16, 8, shape[1])


def select_rows(keep_rows, y):
    cols = 256
    features = y.shape[2]
    return pl.pallas_call(
        select_kernel,
        grid=(features // cols,),
        out_shape=jax.ShapeDtypeStruct((16, 2, 8, features), f32),
        in_specs=[
            pl.BlockSpec((128, 2), lambda g: (0, 0)),
            pl.BlockSpec((4, 128, cols), lambda g: (0, 0, g)),
        ],
        out_specs=pl.BlockSpec((16, 2, 8, cols), lambda g: (0, 0, 0, g)),
        compiler_params=params(),
    )(keep_rows, y)


def gram_kernel(ids_ref, v_ref, w_hbm, g_ref, s_hbm, high, low, flat, w_ref, sems):
    core = ids_ref[0]
    fetch = pltpu.make_async_copy(w_hbm, w_ref, sems.at[0])
    fetch.start()
    send_mine = pltpu.make_async_copy(v_ref.at[core], s_hbm.at[:, 0], sems.at[1])
    send_mine.start()
    send_theirs = pltpu.make_async_copy(w_ref.at[core], s_hbm.at[:, 1], sems.at[2])
    for part, ref in enumerate((v_ref, w_ref)):
        if part:
            fetch.wait()
            send_theirs.start()
        h, l = halves(ref[...].reshape(256, FEAT))
        high[256 * part : 256 * part + 256, :] = h
        low[256 * part : 256 * part + 256, :] = l
    for which, strips in enumerate(STRIPS):

        @pl.when(core == which)
        def _():
            row = 0
            for strip in strips:
                at = NB * strip
                h, l = high[:, at : at + NB], low[:, at : at + NB]
                total = tmm(h, high[:, at:]) + (tmm(h, low[:, at:]) + tmm(l, high[:, at:]))
                for block in range(PANELS - strip):
                    flat[row : row + NB, :] = total[:, NB * block : NB * block + NB]
                    row += NB

    for piece in range(16):
        g_ref[piece] = flat[GRAM_ROWS * piece : GRAM_ROWS * (piece + 1), :]
    send_mine.wait()
    send_theirs.wait()


def gram_half(ids, mine, theirs):
    return pl.pallas_call(
        gram_kernel,
        out_shape=(
            jax.ShapeDtypeStruct((16, GRAM_ROWS, NB), f32),
            jax.ShapeDtypeStruct((16, 2, 8, FEAT), f32),
        ),
        in_specs=[SMEM, VMEM, ANY],
        out_specs=(VMEM, ANY),
        scratch_shapes=[pltpu.VMEM((512, FEAT), bf16)] * 2
        + [
            pltpu.VMEM((16 * GRAM_ROWS, NB), f32),
            pltpu.VMEM(mine.shape, f32),
            pltpu.SemaphoreType.DMA((3,)),
        ],
        compiler_params=params(),
    )(ids, mine, theirs)


def final_kernel(ids_ref, table_ref, r_ref, o_hbm, out, sems):
    chunks, rows, cols = out.shape
    odd = (lax.broadcasted_iota(jnp.int32, (rows, cols), 0) >> 2) & 1
    factor = jnp.where((odd * ids_ref[0]) == 1, -32.0, 32.0)

    def store(chunk):
        target = o_hbm.at[:, cols * chunk : cols * chunk + cols]
        return pltpu.make_async_copy(out.at[chunk], target, sems.at[chunk])

    for chunk in range(chunks):
        high, low = halves(r_ref[:, cols * chunk : cols * chunk + cols])
        out[chunk] = (mm(table_ref[...], high) + mm(table_ref[...], low)) * factor
        store(chunk).start()
    for chunk in range(chunks):
        store(chunk).wait()


def final_mix(ids, received):
    rows, features = received.shape
    chunks = 4
    return pl.pallas_call(
        final_kernel,
        out_shape=jax.ShapeDtypeStruct(received.shape, f32),
        in_specs=[SMEM, VMEM, VMEM],
        out_specs=ANY,
        scratch_shapes=[
            pltpu.VMEM((chunks, rows, features // chunks), f32),
            pltpu.SemaphoreType.DMA((chunks,)),
        ],
        compiler_params=params(),
    )(ids, jnp.asarray(final_table()), received)


def lane_splat(x, lane):
    return jnp.broadcast_to(x[:, lane : lane + 1], (8, NB))


def thirds(x):
    high = x.astype(bf16).astype(f32)
    rest = x - high
    middle = rest.astype(bf16).astype(f32)
    return high, middle, rest - middle


def pieces3(x):
    return tuple(part.astype(bf16) for part in thirds(x))


def square_sum(x):
    parts = thirds(x)
    stacked_left = jnp.concatenate([parts[k] for k in LEFT], axis=0).astype(bf16)
    stacked_right = jnp.concatenate([parts[k] for k in RIGHT], axis=0).astype(bf16)
    return tmm(stacked_left, stacked_right)


def tree_sum(terms):
    while len(terms) > 1:
        terms = [x + y for x, y in zip(terms[::2], terms[1::2])]
    return terms[0]


def row_splat(x, row):
    return jnp.broadcast_to(x[row : row + 1, :], (8, NB))


def by_row(sub, values):
    a = [jnp.where((sub & 1) == 0, values[k], values[k + 1]) for k in (0, 2, 4, 6)]
    b = [jnp.where((sub & 2) == 0, a[k], a[k + 1]) for k in (0, 2)]
    return jnp.where(sub < 4, b[0], b[1])


def factor_block(w, upper, inverse):
    lane = lax.broadcasted_iota(jnp.int32, (8, NB), 1)
    sub = lax.broadcasted_iota(jnp.int32, (8, NB), 0)
    groups = NB // 8
    rows = w[0:8, :]
    e = [lane_splat(rows, a) for a in range(8)]
    held = {}
    for step in range(groups):
        base = 8 * step
        inside = (lane >= base) & (lane < base + 8)
        last = min(step + DIRECT, groups - 1)
        near = range(step + 1, last + 1)
        for group in near:
            if group not in held:
                held[group] = w[8 * group : 8 * group + 8, :]
        columns = {group: [lane_splat(held[group], base + b) for b in range(8)] for group in near}
        if near:
            start = [lane_splat(held[step + 1], base + 8 + a) for a in range(8)]
        aug = jnp.where(inside, jnp.where(lane == base + sub, 1.0, 0.0), rows)
        scales, finished = [], []
        multipliers = {group: [] for group in near}
        for b in range(8):
            r = lax.rsqrt(row_splat(e[b], b))
            scales.append(r)
            multiplier = jnp.where(sub > b, e[b], 0.0) * r
            c = {a: row_splat(e[a], b) * r for a in range(b + 1, 8)}
            scaled = row_splat(aug, b) * r
            finished.append(scaled)
            if b < 7:
                for a in range(b + 1, 8):
                    e[a] = e[a] - multiplier * c[a]
                aug = aug - multiplier * scaled
            for group in near:
                column = columns[group]
                multipliers[group].append(column[b] * r)
                for a in range(b + 1, 8):
                    column[a] = column[a] - multipliers[group][b] * c[a]
        scale = by_row(sub, scales)
        right = aug * scale
        left = right
        for a in range(8):
            left = jnp.where(lane == base + a, e[a] * scale, left)
        upper[base : base + 8, :] = jnp.where(lane >= base + sub, left, 0.0)
        inverse[base : base + 8, :] = jnp.where(lane <= base + sub, right, 0.0)
        if not near:
            break
        if last < groups - 1:
            update = square_sum(right)
        m = multipliers[step + 1]
        e = [start[a] - tree_sum([m[b] * row_splat(m[b], a) for b in range(8)]) for a in range(8)]
        for group in near:
            terms = [multipliers[group][b] * finished[b] for b in range(8)]
            held[group] = jnp.where(inside, 0.0, held[group]) - tree_sum(terms)
        rows = held.pop(step + 1)
        if last < groups - 1:
            after = 8 * (last + 1)
            rest = lax.broadcasted_iota(jnp.int32, (NB - after, NB), 1)
            cleared = jnp.where((rest >= base) & (rest < base + 8), 0.0, w[after:, :])
            w[after:, :] = cleared - update[after:, :]


def factor_kernel(ids_ref, ridge_ref, own_ref, other_hbm, o_ref, done_ref, other_ref, sem, a, w, upper, inverse, stack1, stack2):
    core, position = ids_ref[0], ids_ref[1]
    done_ref[0], done_ref[1] = core, position
    fetch = pltpu.make_async_copy(other_hbm, other_ref, sem)
    fetch.start()
    eye = lax.broadcasted_iota(jnp.int32, (NB, NB), 0) == lax.broadcasted_iota(jnp.int32, (NB, NB), 1)

    def assemble(ref, strips):
        slot = 0
        for strip in strips:
            for block in range(strip, PANELS):
                piece = ref[NB * slot : NB * slot + NB, :]
                if block == strip:
                    piece = piece + jnp.where(eye, ridge_ref[0:1, NB * strip : NB * strip + NB], 0.0)
                a[NB * strip : NB * strip + NB, NB * block : NB * block + NB] = piece
                slot += 1

    for ref, offset in ((own_ref, 0), (other_ref, 1)):
        if offset:
            fetch.wait()
        for which in range(2):
            pl.when(core == which)(lambda: assemble(ref, STRIPS[which ^ offset]))

    def body(panel, carry):
        at = pl.multiple_of(panel * NB, NB)
        w[...] = a[pl.ds(at, NB), pl.ds(at, NB)]
        factor_block(w, upper, inverse)
        for fixed in range(PANELS):

            @pl.when(panel == fixed)
            def _():
                s0, s1 = NB * fixed, NB * fixed + NB
                a[s0:s1, s0:s1] = upper[...]
                if fixed < PANELS - 1:
                    inv, rest = pieces3(inverse[...]), pieces3(a[s0:s1, s1:])
                    rows = mm(
                        jnp.concatenate([inv[k] for k in LEFT], axis=1),
                        jnp.concatenate([rest[k] for k in RIGHT], axis=0),
                    )
                    a[s0:s1, s1:] = rows
                    width = FEAT - s1
                    parts = pieces3(rows)
                    for k in range(6):
                        stack1[NB * k : NB * k + NB, :width] = parts[LEFT[k]]
                        stack2[NB * k : NB * k + NB, :width] = parts[RIGHT[k]]
                    for strip in range(fixed + 1, PANELS):
                        b0, t0 = NB * (strip - fixed - 1), NB * strip
                        update = tmm(stack1[:, b0 : b0 + NB], stack2[:, b0:width])
                        a[t0 : t0 + NB, t0:] = a[t0 : t0 + NB, t0:] - update

        return carry

    lax.fori_loop(0, PANELS, body, 0)
    out = a[pl.ds(pl.multiple_of(position * 8, 8), 8), :]
    lane = lax.broadcasted_iota(jnp.int32, out.shape, 1)
    o_ref[...] = jnp.where(lane >= (position // 16) * NB, out, 0.0)


def factor_rows(ids, ridge, own, other):
    return pl.pallas_call(
        factor_kernel,
        out_shape=(jax.ShapeDtypeStruct((8, FEAT), f32), jax.ShapeDtypeStruct((2,), jnp.int32)),
        in_specs=[SMEM, VMEM, VMEM, ANY],
        out_specs=(VMEM, SMEM),
        scratch_shapes=[pltpu.VMEM(other.shape, f32), pltpu.SemaphoreType.DMA(())]
        + [pltpu.VMEM((FEAT, FEAT), f32)] + [pltpu.VMEM((NB, NB), f32)] * 3
        + [pltpu.VMEM((6 * NB, FEAT), bf16)] * 2,
        compiler_params=params(),
        cost_estimate=pl.CostEstimate(flops=40_000_000_000, bytes_accessed=2 << 20, transcendentals=0),
    )(ids, ridge, own, other)


def swap_cores(x):
    return lax.ppermute(x, "outer", [(0, 1), (1, 0)])


def along_z(x, distance):
    return lax.ppermute(x, "inner", [(i, (i + 16 * distance) % 64) for i in range(64)])


def plane_exchange(x):
    return lax.all_to_all(x, "inner", 0, 0, axis_index_groups=PLANES, tiled=True)


def local(matrix, sign_flip, keep_list, ridge_weights):
    core, inner = lax.axis_index("outer"), lax.axis_index("inner")
    ids = jnp.stack([core, core * 64 + inner]).astype(jnp.int32)
    keep_here = lax.dynamic_index_in_dim(keep_list.reshape(2, 4, 16, 2), inner // 16, 1, False)
    keep_rows = jnp.repeat(keep_here.reshape(32, 2), 4, axis=0)
    mixed = local_mix(matrix, sign_flip)
    along = lax.all_to_all(
        mixed.reshape(4, 128, FEAT), "inner", 0, 0, axis_index_groups=Z_GROUPS, tiled=True
    )
    mine = select_rows(keep_rows, along).reshape(2, 16, 8, FEAT)
    theirs = swap_cores(mine)
    gram, to_send = gram_half(ids, mine, theirs)
    piece = jnp.sum(plane_exchange(gram), axis=0)
    piece = (piece + along_z(piece, 2)) + (along_z(piece, 1) + along_z(piece, 3))
    own = plane_exchange(jnp.broadcast_to(piece[None], (16, GRAM_ROWS, NB))).reshape(16 * GRAM_ROWS, NB)
    to_send, own = lax.optimization_barrier((to_send, own))
    received = plane_exchange(to_send)
    other = swap_cores(own)
    factor, done = factor_rows(ids, ridge_weights.reshape(1, FEAT), own, other)
    sketch = final_mix(done, received.reshape(256, FEAT))
    return sketch, factor


def solution(mesh):
    return jax.shard_map(
        local,
        mesh=mesh,
        in_specs=(P(("outer", "inner"), None), P(("outer", "inner")), P(), P()),
        out_specs=(P(("outer", "inner"), None), P(("outer", "inner"), None)),
        check_vma=False,
    )
```

```python
import jax
import jax.numpy as jnp
import numpy as np
from jax import lax
from jax.experimental import pallas as pl
from jax.experimental.pallas import tpu as pltpu
from jax.sharding import PartitionSpec as P

f32 = jnp.float32
bf16 = jnp.bfloat16
VMEM = pl.BlockSpec(memory_space=pltpu.VMEM)
SMEM = pl.BlockSpec(memory_space=pltpu.SMEM)
ANY = pl.BlockSpec(memory_space=pl.ANY)
FEAT = 1024
NB = 128
PANELS = FEAT // NB
STRIPS = ((0, 3, 4, 7), (1, 2, 5, 6))
GRAM_ROWS = 144
DIRECT = 3
LEFT = (0, 0, 0, 1, 1, 2)
RIGHT = (0, 1, 2, 0, 1, 0)
Z_GROUPS = [[i + 16 * j for j in range(4)] for i in range(16)]
PLANES = [[16 * j + i for i in range(16)] for j in range(4)]


def params(mib=32):
    return pltpu.CompilerParams(vmem_limit_bytes=mib << 20)


def parity_sign(left, right):
    common = left & right
    parity = np.zeros_like(common)
    for shift_by in range(10):
        parity ^= (common >> shift_by) & 1
    return 1 - 2 * parity


def local_table():
    az, c, axy, e = np.meshgrid(range(4), range(2), range(16), range(4), indexing="ij")
    k = (az * 128 + axy * 8 + c * 4 + e).reshape(-1, 1)
    return parity_sign(k, np.arange(512)[None, :]).astype(np.float32).astype(bf16)


def final_table():
    j, i, o, e = (v.reshape(-1, 1) for v in np.meshgrid(range(2), range(16), range(2), range(4), indexing="ij"))
    ip, op, jp, ep = (v.reshape(1, -1) for v in np.meshgrid(range(16), range(2), range(2), range(4), indexing="ij"))
    table = parity_sign(i, ip) * parity_sign(o, op) * (j == jp) * (e == ep)
    return table.astype(np.float32).astype(bf16)


def halves(x):
    high = x.astype(bf16)
    return high, (x - high.astype(f32)).astype(bf16)


def mm(a, b):
    return jnp.dot(a, b, preferred_element_type=f32)


def tmm(a, b):
    return lax.dot_general(a, b, (((0,), (0,)), ((), ())), preferred_element_type=f32)


def local_mix_kernel(table_hbm, sign_hbm, x_hbm, o_hbm, table, sign, signed, x, out, sems):
    chunks, _, cols = out.shape

    def load(chunk):
        part = pl.ds(128 * chunk, 128)
        return pltpu.make_async_copy(x_hbm.at[part], x.at[part], sems.at[chunk])

    def store(chunk):
        target = o_hbm.at[:, cols * chunk : cols * chunk + cols]
        return pltpu.make_async_copy(out.at[chunk], target, sems.at[chunks + chunk])

    get_table = pltpu.make_async_copy(table_hbm, table, sems.at[2 * chunks])
    get_sign = pltpu.make_async_copy(sign_hbm, sign, sems.at[2 * chunks + 1])
    get_sign.start()
    get_table.start()
    for chunk in range(chunks):
        load(chunk).start()
    get_sign.wait()
    get_table.wait()
    signed[...] = (table[...].astype(f32) * (sign[...].astype(f32) * 2.0**-13)).astype(bf16)
    for chunk in range(chunks):
        load(chunk).wait()
    for chunk in range(chunks):
        high, low = halves(x[:, cols * chunk : cols * chunk + cols])
        out[chunk] = mm(signed[...], high) + mm(signed[...], low)
        store(chunk).start()
    for chunk in range(chunks):
        store(chunk).wait()


def local_mix(matrix, sign_flip):
    rows, features = matrix.shape
    chunks = 4
    anywhere = pl.BlockSpec(memory_space=pl.ANY)
    block = pltpu.VMEM((chunks, rows, features // chunks), f32)
    return pl.pallas_call(
        local_mix_kernel,
        out_shape=jax.ShapeDtypeStruct((rows, features), f32),
        in_specs=[anywhere] * 3,
        out_specs=anywhere,
        scratch_shapes=[
            pltpu.VMEM((rows, rows), bf16),
            pltpu.VMEM((1, rows), jnp.int32),
            pltpu.VMEM((rows, rows), bf16),
            pltpu.VMEM((rows, features), f32),
            block,
            pltpu.SemaphoreType.DMA((2 * chunks + 2,)),
        ],
        compiler_params=params(60),
    )(jnp.asarray(local_table()), sign_flip.reshape(1, rows), matrix)


def select_kernel(keep_ref, y_ref, v_ref):
    y0, y1, y2, y3 = (y_ref[z] for z in range(4))
    s, d, s2, d2 = y0 + y1, y0 - y1, y2 + y3, y2 - y3

    def combo(which):
        low = (which & 1) == 1
        first = jnp.where(low, d, s)
        second = jnp.where(low, d2, s2)
        return first + jnp.where((which & 2) == 2, -second, second)

    shape = s.shape
    v0 = combo(jnp.broadcast_to(keep_ref[:, 0:1], shape))
    v1 = combo(jnp.broadcast_to(keep_ref[:, 1:2], shape))
    upper = (lax.broadcasted_iota(jnp.int32, shape, 0) & 7) < 4
    even = jnp.where(upper, v0, pltpu.roll(v1, 4, axis=0))
    odd = jnp.where(upper, pltpu.roll(v0, shape[0] - 4, axis=0), v1)
    v_ref[:, 0] = even.reshape(16, 8, shape[1])
    v_ref[:, 1] = odd.reshape(16, 8, shape[1])


def select_rows(keep_rows, y):
    cols = 256
    features = y.shape[2]
    return pl.pallas_call(
        select_kernel,
        grid=(features // cols,),
        out_shape=jax.ShapeDtypeStruct((16, 2, 8, features), f32),
        in_specs=[
            pl.BlockSpec((128, 2), lambda g: (0, 0)),
            pl.BlockSpec((4, 128, cols), lambda g: (0, 0, g)),
        ],
        out_specs=pl.BlockSpec((16, 2, 8, cols), lambda g: (0, 0, 0, g)),
        compiler_params=params(),
    )(keep_rows, y)


def gram_kernel(ids_ref, v_ref, w_hbm, g_ref, s_hbm, high, low, flat, w_ref, sems):
    core = ids_ref[0]
    fetch = pltpu.make_async_copy(w_hbm, w_ref, sems.at[0])
    fetch.start()
    send_mine = pltpu.make_async_copy(v_ref.at[core], s_hbm.at[:, 0], sems.at[1])
    send_mine.start()
    send_theirs = pltpu.make_async_copy(w_ref.at[core], s_hbm.at[:, 1], sems.at[2])
    for part, ref in enumerate((v_ref, w_ref)):
        if part:
            fetch.wait()
            send_theirs.start()
        h, l = halves(ref[...].reshape(256, FEAT))
        high[256 * part : 256 * part + 256, :] = h
        low[256 * part : 256 * part + 256, :] = l
    for which, strips in enumerate(STRIPS):

        @pl.when(core == which)
        def _():
            row = 0
            for strip in strips:
                at = NB * strip
                h, l = high[:, at : at + NB], low[:, at : at + NB]
                total = tmm(h, high[:, at:]) + (tmm(h, low[:, at:]) + tmm(l, high[:, at:]))
                for block in range(PANELS - strip):
                    flat[row : row + NB, :] = total[:, NB * block : NB * block + NB]
                    row += NB

    for piece in range(16):
        g_ref[piece] = flat[GRAM_ROWS * piece : GRAM_ROWS * (piece + 1), :]
    send_mine.wait()
    send_theirs.wait()


def gram_half(ids, mine, theirs):
    return pl.pallas_call(
        gram_kernel,
        out_shape=(
            jax.ShapeDtypeStruct((16, GRAM_ROWS, NB), f32),
            jax.ShapeDtypeStruct((16, 2, 8, FEAT), f32),
        ),
        in_specs=[SMEM, VMEM, ANY],
        out_specs=(VMEM, ANY),
        scratch_shapes=[pltpu.VMEM((512, FEAT), bf16)] * 2
        + [
            pltpu.VMEM((16 * GRAM_ROWS, NB), f32),
            pltpu.VMEM(mine.shape, f32),
            pltpu.SemaphoreType.DMA((3,)),
        ],
        compiler_params=params(),
    )(ids, mine, theirs)


def final_kernel(ids_ref, table_ref, r_ref, o_hbm, out, sems):
    chunks, rows, cols = out.shape
    odd = (lax.broadcasted_iota(jnp.int32, (rows, cols), 0) >> 2) & 1
    factor = jnp.where((odd * ids_ref[0]) == 1, -32.0, 32.0)

    def store(chunk):
        target = o_hbm.at[:, cols * chunk : cols * chunk + cols]
        return pltpu.make_async_copy(out.at[chunk], target, sems.at[chunk])

    for chunk in range(chunks):
        high, low = halves(r_ref[:, cols * chunk : cols * chunk + cols])
        out[chunk] = (mm(table_ref[...], high) + mm(table_ref[...], low)) * factor
        store(chunk).start()
    for chunk in range(chunks):
        store(chunk).wait()


def final_mix(ids, received):
    rows, features = received.shape
    chunks = 4
    return pl.pallas_call(
        final_kernel,
        out_shape=jax.ShapeDtypeStruct(received.shape, f32),
        in_specs=[SMEM, VMEM, VMEM],
        out_specs=ANY,
        scratch_shapes=[
            pltpu.VMEM((chunks, rows, features // chunks), f32),
            pltpu.SemaphoreType.DMA((chunks,)),
        ],
        compiler_params=params(),
    )(ids, jnp.asarray(final_table()), received)


def lane_splat(x, lane):
    return jnp.broadcast_to(x[:, lane : lane + 1], (8, NB))


def thirds(x):
    high = x.astype(bf16).astype(f32)
    rest = x - high
    middle = rest.astype(bf16).astype(f32)
    return high, middle, rest - middle


def pieces3(x):
    return tuple(part.astype(bf16) for part in thirds(x))


def square_sum(x):
    parts = thirds(x)
    stacked_left = jnp.concatenate([parts[k] for k in LEFT], axis=0).astype(bf16)
    stacked_right = jnp.concatenate([parts[k] for k in RIGHT], axis=0).astype(bf16)
    return tmm(stacked_left, stacked_right)


def tree_sum(terms):
    while len(terms) > 1:
        terms = [x + y for x, y in zip(terms[::2], terms[1::2])]
    return terms[0]


def row_splat(x, row):
    return jnp.broadcast_to(x[row : row + 1, :], (8, NB))


def by_row(sub, values):
    a = [jnp.where((sub & 1) == 0, values[k], values[k + 1]) for k in (0, 2, 4, 6)]
    b = [jnp.where((sub & 2) == 0, a[k], a[k + 1]) for k in (0, 2)]
    return jnp.where(sub < 4, b[0], b[1])


def factor_block(w, upper, inverse):
    lane = lax.broadcasted_iota(jnp.int32, (8, NB), 1)
    sub = lax.broadcasted_iota(jnp.int32, (8, NB), 0)
    groups = NB // 8
    rows = w[0:8, :]
    e = [lane_splat(rows, a) for a in range(8)]
    held = {}
    for step in range(groups):
        base = 8 * step
        inside = (lane >= base) & (lane < base + 8)
        last = min(step + DIRECT, groups - 1)
        near = range(step + 1, last + 1)
        for group in near:
            if group not in held:
                held[group] = w[8 * group : 8 * group + 8, :]
        columns = {group: [lane_splat(held[group], base + b) for b in range(8)] for group in near}
        if near:
            start = [lane_splat(held[step + 1], base + 8 + a) for a in range(8)]
        aug = jnp.where(inside, jnp.where(lane == base + sub, 1.0, 0.0), rows)
        scales, finished = [], []
        multipliers = {group: [] for group in near}
        for b in range(8):
            r = lax.rsqrt(row_splat(e[b], b))
            scales.append(r)
            multiplier = jnp.where(sub > b, e[b], 0.0) * r
            c = {a: row_splat(e[a], b) * r for a in range(b + 1, 8)}
            scaled = row_splat(aug, b) * r
            finished.append(scaled)
            if b < 7:
                for a in range(b + 1, 8):
                    e[a] = e[a] - multiplier * c[a]
                aug = aug - multiplier * scaled
            for group in near:
                column = columns[group]
                multipliers[group].append(column[b] * r)
                for a in range(b + 1, 8):
                    column[a] = column[a] - multipliers[group][b] * c[a]
        scale = by_row(sub, scales)
        right = aug * scale
        left = right
        for a in range(8):
            left = jnp.where(lane == base + a, e[a] * scale, left)
        upper[base : base + 8, :] = jnp.where(lane >= base + sub, left, 0.0)
        inverse[base : base + 8, :] = jnp.where(lane <= base + sub, right, 0.0)
        if not near:
            break
        if last < groups - 1:
            update = square_sum(right)
        m = multipliers[step + 1]
        e = [start[a] - tree_sum([m[b] * row_splat(m[b], a) for b in range(8)]) for a in range(8)]
        for group in near:
            terms = [multipliers[group][b] * finished[b] for b in range(8)]
            held[group] = jnp.where(inside, 0.0, held[group]) - tree_sum(terms)
        rows = held.pop(step + 1)
        if last < groups - 1:
            after = 8 * (last + 1)
            rest = lax.broadcasted_iota(jnp.int32, (NB - after, NB), 1)
            cleared = jnp.where((rest >= base) & (rest < base + 8), 0.0, w[after:, :])
            w[after:, :] = cleared - update[after:, :]


def factor_kernel(ids_ref, ridge_ref, own_ref, other_hbm, o_ref, done_ref, other_ref, sem, a, w, upper, inverse, stack1, stack2):
    core, position = ids_ref[0], ids_ref[1]
    done_ref[0], done_ref[1] = core, position
    fetch = pltpu.make_async_copy(other_hbm, other_ref, sem)
    fetch.start()
    eye = lax.broadcasted_iota(jnp.int32, (NB, NB), 0) == lax.broadcasted_iota(jnp.int32, (NB, NB), 1)

    def assemble(ref, strips):
        slot = 0
        for strip in strips:
            for block in range(strip, PANELS):
                piece = ref[NB * slot : NB * slot + NB, :]
                if block == strip:
                    piece = piece + jnp.where(eye, ridge_ref[0:1, NB * strip : NB * strip + NB], 0.0)
                a[NB * strip : NB * strip + NB, NB * block : NB * block + NB] = piece
                slot += 1

    for ref, offset in ((own_ref, 0), (other_ref, 1)):
        if offset:
            fetch.wait()
        for which in range(2):
            pl.when(core == which)(lambda: assemble(ref, STRIPS[which ^ offset]))

    def body(panel, carry):
        at = pl.multiple_of(panel * NB, NB)
        w[...] = a[pl.ds(at, NB), pl.ds(at, NB)]
        factor_block(w, upper, inverse)
        for fixed in range(PANELS):

            @pl.when(panel == fixed)
            def _():
                s0, s1 = NB * fixed, NB * fixed + NB
                a[s0:s1, s0:s1] = upper[...]
                if fixed < PANELS - 1:
                    inv, rest = pieces3(inverse[...]), pieces3(a[s0:s1, s1:])
                    rows = mm(
                        jnp.concatenate([inv[k] for k in LEFT], axis=1),
                        jnp.concatenate([rest[k] for k in RIGHT], axis=0),
                    )
                    a[s0:s1, s1:] = rows
                    width = FEAT - s1
                    parts = pieces3(rows)
                    for k in range(6):
                        stack1[NB * k : NB * k + NB, :width] = parts[LEFT[k]]
                        stack2[NB * k : NB * k + NB, :width] = parts[RIGHT[k]]
                    for strip in range(fixed + 1, PANELS):
                        b0, t0 = NB * (strip - fixed - 1), NB * strip
                        update = tmm(stack1[:, b0 : b0 + NB], stack2[:, b0:width])
                        a[t0 : t0 + NB, t0:] = a[t0 : t0 + NB, t0:] - update

        return carry

    lax.fori_loop(0, PANELS, body, 0)
    out = a[pl.ds(pl.multiple_of(position * 8, 8), 8), :]
    lane = lax.broadcasted_iota(jnp.int32, out.shape, 1)
    o_ref[...] = jnp.where(lane >= (position // 16) * NB, out, 0.0)


def factor_rows(ids, ridge, own, other):
    return pl.pallas_call(
        factor_kernel,
        out_shape=(jax.ShapeDtypeStruct((8, FEAT), f32), jax.ShapeDtypeStruct((2,), jnp.int32)),
        in_specs=[SMEM, VMEM, VMEM, ANY],
        out_specs=(VMEM, SMEM),
        scratch_shapes=[pltpu.VMEM(other.shape, f32), pltpu.SemaphoreType.DMA(())]
        + [pltpu.VMEM((FEAT, FEAT), f32)] + [pltpu.VMEM((NB, NB), f32)] * 3
        + [pltpu.VMEM((6 * NB, FEAT), bf16)] * 2,
        compiler_params=params(),
        cost_estimate=pl.CostEstimate(flops=40_000_000_000, bytes_accessed=2 << 20, transcendentals=0),
    )(ids, ridge, own, other)


def swap_cores(x):
    return lax.ppermute(x, "outer", [(0, 1), (1, 0)])


def plane_exchange(x):
    return lax.all_to_all(x, "inner", 0, 0, axis_index_groups=PLANES, tiled=True)


def local(matrix, sign_flip, keep_list, ridge_weights):
    core, inner = lax.axis_index("outer"), lax.axis_index("inner")
    ids = jnp.stack([core, core * 64 + inner]).astype(jnp.int32)
    keep_here = lax.dynamic_index_in_dim(keep_list.reshape(2, 4, 16, 2), inner // 16, 1, False)
    keep_rows = jnp.repeat(keep_here.reshape(32, 2), 4, axis=0)
    mixed = local_mix(matrix, sign_flip)
    along = lax.all_to_all(
        mixed.reshape(4, 128, FEAT), "inner", 0, 0, axis_index_groups=Z_GROUPS, tiled=True
    )
    mine = select_rows(keep_rows, along).reshape(2, 16, 8, FEAT)
    theirs = swap_cores(mine)
    gram, to_send = gram_half(ids, mine, theirs)
    piece = jnp.sum(plane_exchange(gram), axis=0)
    by_plane = jnp.broadcast_to(piece[None], (4, GRAM_ROWS, NB))
    by_plane = lax.all_to_all(by_plane, "inner", 0, 0, axis_index_groups=Z_GROUPS, tiled=True)
    piece = (by_plane[0] + by_plane[1]) + (by_plane[2] + by_plane[3])
    own = plane_exchange(jnp.broadcast_to(piece[None], (16, GRAM_ROWS, NB))).reshape(16 * GRAM_ROWS, NB)
    to_send, own = lax.optimization_barrier((to_send, own))
    received = plane_exchange(to_send)
    other = swap_cores(own)
    factor, done = factor_rows(ids, ridge_weights.reshape(1, FEAT), own, other)
    sketch = final_mix(done, received.reshape(256, FEAT))
    return sketch, factor


def solution(mesh):
    return jax.shard_map(
        local,
        mesh=mesh,
        in_specs=(P(("outer", "inner"), None), P(("outer", "inner")), P(), P()),
        out_specs=(P(("outer", "inner"), None), P(("outer", "inner"), None)),
        check_vma=False,
    )
```

```python
import jax
import jax.numpy as jnp
import numpy as np
from jax import lax
from jax.experimental import pallas as pl
from jax.experimental.pallas import tpu as pltpu
from jax.sharding import PartitionSpec as P

f32 = jnp.float32
bf16 = jnp.bfloat16
VMEM = pl.BlockSpec(memory_space=pltpu.VMEM)
SMEM = pl.BlockSpec(memory_space=pltpu.SMEM)
ANY = pl.BlockSpec(memory_space=pl.ANY)
FEAT = 1024
NB = 128
PANELS = FEAT // NB
STRIPS = ((0, 3, 4, 7), (1, 2, 5, 6))
GRAM_ROWS = 144
DIRECT = 3
LEFT = (0, 0, 0, 1, 1, 2)
RIGHT = (0, 1, 2, 0, 1, 0)
Z_GROUPS = [[i + 16 * j for j in range(4)] for i in range(16)]
PLANES = [[16 * j + i for i in range(16)] for j in range(4)]


def params(mib=32):
    return pltpu.CompilerParams(vmem_limit_bytes=mib << 20)


def parity_sign(left, right):
    common = left & right
    parity = np.zeros_like(common)
    for shift_by in range(10):
        parity ^= (common >> shift_by) & 1
    return 1 - 2 * parity


def local_table():
    az, c, axy, e = np.meshgrid(range(4), range(2), range(16), range(4), indexing="ij")
    k = (az * 128 + axy * 8 + c * 4 + e).reshape(-1, 1)
    return parity_sign(k, np.arange(512)[None, :]).astype(np.float32).astype(bf16)


def final_table():
    j, i, o, e = (v.reshape(-1, 1) for v in np.meshgrid(range(2), range(16), range(2), range(4), indexing="ij"))
    ip, op, jp, ep = (v.reshape(1, -1) for v in np.meshgrid(range(16), range(2), range(2), range(4), indexing="ij"))
    table = parity_sign(i, ip) * parity_sign(o, op) * (j == jp) * (e == ep)
    return table.astype(np.float32).astype(bf16)


def halves(x):
    high = x.astype(bf16)
    return high, (x - high.astype(f32)).astype(bf16)


def mm(a, b):
    return jnp.dot(a, b, preferred_element_type=f32)


def tmm(a, b):
    return lax.dot_general(a, b, (((0,), (0,)), ((), ())), preferred_element_type=f32)


def local_mix_kernel(table_hbm, sign_hbm, x_hbm, o_hbm, table, sign, signed, x, out, sems):
    chunks, _, cols = out.shape

    def load(chunk):
        part = pl.ds(128 * chunk, 128)
        return pltpu.make_async_copy(x_hbm.at[part], x.at[part], sems.at[chunk])

    def store(chunk):
        target = o_hbm.at[:, cols * chunk : cols * chunk + cols]
        return pltpu.make_async_copy(out.at[chunk], target, sems.at[chunks + chunk])

    get_table = pltpu.make_async_copy(table_hbm, table, sems.at[2 * chunks])
    get_sign = pltpu.make_async_copy(sign_hbm, sign, sems.at[2 * chunks + 1])
    get_sign.start()
    get_table.start()
    for chunk in range(chunks):
        load(chunk).start()
    get_sign.wait()
    get_table.wait()
    signed[...] = (table[...].astype(f32) * (sign[...].astype(f32) * 2.0**-13)).astype(bf16)
    for chunk in range(chunks):
        load(chunk).wait()
    for chunk in range(chunks):
        high, low = halves(x[:, cols * chunk : cols * chunk + cols])
        out[chunk] = mm(signed[...], high) + mm(signed[...], low)
        store(chunk).start()
    for chunk in range(chunks):
        store(chunk).wait()


def local_mix(matrix, sign_flip):
    rows, features = matrix.shape
    chunks = 4
    anywhere = pl.BlockSpec(memory_space=pl.ANY)
    block = pltpu.VMEM((chunks, rows, features // chunks), f32)
    return pl.pallas_call(
        local_mix_kernel,
        out_shape=jax.ShapeDtypeStruct((rows, features), f32),
        in_specs=[anywhere] * 3,
        out_specs=anywhere,
        scratch_shapes=[
            pltpu.VMEM((rows, rows), bf16),
            pltpu.VMEM((1, rows), jnp.int32),
            pltpu.VMEM((rows, rows), bf16),
            pltpu.VMEM((rows, features), f32),
            block,
            pltpu.SemaphoreType.DMA((2 * chunks + 2,)),
        ],
        compiler_params=params(60),
    )(jnp.asarray(local_table()), sign_flip.reshape(1, rows), matrix)


def select_kernel(keep_ref, y_ref, v_ref):
    y0, y1, y2, y3 = (y_ref[z] for z in range(4))
    s, d, s2, d2 = y0 + y1, y0 - y1, y2 + y3, y2 - y3

    def combo(which):
        low = (which & 1) == 1
        first = jnp.where(low, d, s)
        second = jnp.where(low, d2, s2)
        return first + jnp.where((which & 2) == 2, -second, second)

    shape = s.shape
    v0 = combo(jnp.broadcast_to(keep_ref[:, 0:1], shape))
    v1 = combo(jnp.broadcast_to(keep_ref[:, 1:2], shape))
    upper = (lax.broadcasted_iota(jnp.int32, shape, 0) & 7) < 4
    even = jnp.where(upper, v0, pltpu.roll(v1, 4, axis=0))
    odd = jnp.where(upper, pltpu.roll(v0, shape[0] - 4, axis=0), v1)
    v_ref[:, 0] = even.reshape(16, 8, shape[1])
    v_ref[:, 1] = odd.reshape(16, 8, shape[1])


def select_rows(keep_rows, y):
    cols = 256
    features = y.shape[2]
    return pl.pallas_call(
        select_kernel,
        grid=(features // cols,),
        out_shape=jax.ShapeDtypeStruct((16, 2, 8, features), f32),
        in_specs=[
            pl.BlockSpec((128, 2), lambda g: (0, 0)),
            pl.BlockSpec((4, 128, cols), lambda g: (0, 0, g)),
        ],
        out_specs=pl.BlockSpec((16, 2, 8, cols), lambda g: (0, 0, 0, g)),
        compiler_params=params(),
    )(keep_rows, y)


def gram_kernel(ids_ref, v_ref, w_hbm, g_ref, s_hbm, high, low, flat, w_ref, sems):
    core = ids_ref[0]
    fetch = pltpu.make_async_copy(w_hbm, w_ref, sems.at[0])
    fetch.start()
    send_mine = pltpu.make_async_copy(v_ref.at[core], s_hbm.at[:, 0], sems.at[1])
    send_mine.start()
    send_theirs = pltpu.make_async_copy(w_ref.at[core], s_hbm.at[:, 1], sems.at[2])
    for part, ref in enumerate((v_ref, w_ref)):
        if part:
            fetch.wait()
            send_theirs.start()
        h, l = halves(ref[...].reshape(256, FEAT))
        high[256 * part : 256 * part + 256, :] = h
        low[256 * part : 256 * part + 256, :] = l
    for which, strips in enumerate(STRIPS):

        @pl.when(core == which)
        def _():
            row = 0
            for strip in strips:
                at = NB * strip
                h, l = high[:, at : at + NB], low[:, at : at + NB]
                total = tmm(h, high[:, at:]) + (tmm(h, low[:, at:]) + tmm(l, high[:, at:]))
                for block in range(PANELS - strip):
                    flat[row : row + NB, :] = total[:, NB * block : NB * block + NB]
                    row += NB

    for piece in range(16):
        g_ref[piece] = flat[GRAM_ROWS * piece : GRAM_ROWS * (piece + 1), :]
    send_mine.wait()
    send_theirs.wait()


def gram_half(ids, mine, theirs):
    return pl.pallas_call(
        gram_kernel,
        out_shape=(
            jax.ShapeDtypeStruct((16, GRAM_ROWS, NB), f32),
            jax.ShapeDtypeStruct((16, 2, 8, FEAT), f32),
        ),
        in_specs=[SMEM, VMEM, ANY],
        out_specs=(VMEM, ANY),
        scratch_shapes=[pltpu.VMEM((512, FEAT), bf16)] * 2
        + [
            pltpu.VMEM((16 * GRAM_ROWS, NB), f32),
            pltpu.VMEM(mine.shape, f32),
            pltpu.SemaphoreType.DMA((3,)),
        ],
        compiler_params=params(),
    )(ids, mine, theirs)


def final_kernel(ids_ref, table_ref, r_ref, o_hbm, out, sems):
    chunks, rows, cols = out.shape
    odd = (lax.broadcasted_iota(jnp.int32, (rows, cols), 0) >> 2) & 1
    factor = jnp.where((odd * ids_ref[0]) == 1, -32.0, 32.0)

    def store(chunk):
        target = o_hbm.at[:, cols * chunk : cols * chunk + cols]
        return pltpu.make_async_copy(out.at[chunk], target, sems.at[chunk])

    for chunk in range(chunks):
        high, low = halves(r_ref[:, cols * chunk : cols * chunk + cols])
        out[chunk] = (mm(table_ref[...], high) + mm(table_ref[...], low)) * factor
        store(chunk).start()
    for chunk in range(chunks):
        store(chunk).wait()


def final_mix(ids, received):
    rows, features = received.shape
    chunks = 4
    return pl.pallas_call(
        final_kernel,
        out_shape=jax.ShapeDtypeStruct(received.shape, f32),
        in_specs=[SMEM, VMEM, VMEM],
        out_specs=ANY,
        scratch_shapes=[
            pltpu.VMEM((chunks, rows, features // chunks), f32),
            pltpu.SemaphoreType.DMA((chunks,)),
        ],
        compiler_params=params(),
    )(ids, jnp.asarray(final_table()), received)


def lane_splat(x, lane):
    return jnp.broadcast_to(x[:, lane : lane + 1], (8, NB))


def thirds(x):
    high = x.astype(bf16).astype(f32)
    rest = x - high
    middle = rest.astype(bf16).astype(f32)
    return high, middle, rest - middle


def pieces3(x):
    return tuple(part.astype(bf16) for part in thirds(x))


def square_sum(x):
    parts = thirds(x)
    stacked_left = jnp.concatenate([parts[k] for k in LEFT], axis=0).astype(bf16)
    stacked_right = jnp.concatenate([parts[k] for k in RIGHT], axis=0).astype(bf16)
    return tmm(stacked_left, stacked_right)


def tree_sum(terms):
    while len(terms) > 1:
        terms = [x + y for x, y in zip(terms[::2], terms[1::2])]
    return terms[0]


def row_splat(x, row):
    return jnp.broadcast_to(x[row : row + 1, :], (8, NB))


def by_row(sub, values):
    a = [jnp.where((sub & 1) == 0, values[k], values[k + 1]) for k in (0, 2, 4, 6)]
    b = [jnp.where((sub & 2) == 0, a[k], a[k + 1]) for k in (0, 2)]
    return jnp.where(sub < 4, b[0], b[1])


def factor_block(w, upper, inverse):
    lane = lax.broadcasted_iota(jnp.int32, (8, NB), 1)
    sub = lax.broadcasted_iota(jnp.int32, (8, NB), 0)
    groups = NB // 8
    rows = w[0:8, :]
    e = [lane_splat(rows, a) for a in range(8)]
    held = {}
    for step in range(groups):
        base = 8 * step
        inside = (lane >= base) & (lane < base + 8)
        last = min(step + DIRECT, groups - 1)
        near = range(step + 1, last + 1)
        for group in near:
            if group not in held:
                held[group] = w[8 * group : 8 * group + 8, :]
        columns = {group: [lane_splat(held[group], base + b) for b in range(8)] for group in near}
        if near:
            start = [lane_splat(held[step + 1], base + 8 + a) for a in range(8)]
        aug = jnp.where(inside, jnp.where(lane == base + sub, 1.0, 0.0), rows)
        scales, finished = [], []
        multipliers = {group: [] for group in near}
        for b in range(8):
            r = lax.rsqrt(row_splat(e[b], b))
            scales.append(r)
            multiplier = jnp.where(sub > b, e[b], 0.0) * r
            c = {a: row_splat(e[a], b) * r for a in range(b + 1, 8)}
            scaled = row_splat(aug, b) * r
            finished.append(scaled)
            if b < 7:
                for a in range(b + 1, 8):
                    e[a] = e[a] - multiplier * c[a]
                aug = aug - multiplier * scaled
            for group in near:
                column = columns[group]
                multipliers[group].append(column[b] * r)
                for a in range(b + 1, 8):
                    column[a] = column[a] - multipliers[group][b] * c[a]
        scale = by_row(sub, scales)
        right = aug * scale
        left = right
        for a in range(8):
            left = jnp.where(lane == base + a, e[a] * scale, left)
        upper[base : base + 8, :] = jnp.where(lane >= base + sub, left, 0.0)
        inverse[base : base + 8, :] = jnp.where(lane <= base + sub, right, 0.0)
        if not near:
            break
        if last < groups - 1:
            update = square_sum(right)
        m = multipliers[step + 1]
        e = [start[a] - tree_sum([m[b] * row_splat(m[b], a) for b in range(8)]) for a in range(8)]
        for group in near:
            terms = [multipliers[group][b] * finished[b] for b in range(8)]
            held[group] = jnp.where(inside, 0.0, held[group]) - tree_sum(terms)
        rows = held.pop(step + 1)
        if last < groups - 1:
            after = 8 * (last + 1)
            rest = lax.broadcasted_iota(jnp.int32, (NB - after, NB), 1)
            cleared = jnp.where((rest >= base) & (rest < base + 8), 0.0, w[after:, :])
            w[after:, :] = cleared - update[after:, :]


def factor_kernel(ids_ref, ridge_ref, own_ref, other_hbm, o_ref, done_ref, other_ref, sem, a, w, upper, inverse, stack1, stack2):
    core, position = ids_ref[0], ids_ref[1]
    done_ref[0], done_ref[1] = core, position
    fetch = pltpu.make_async_copy(other_hbm, other_ref, sem)
    fetch.start()
    eye = lax.broadcasted_iota(jnp.int32, (NB, NB), 0) == lax.broadcasted_iota(jnp.int32, (NB, NB), 1)

    def assemble(ref, strips):
        slot = 0
        for strip in strips:
            for block in range(strip, PANELS):
                piece = ref[NB * slot : NB * slot + NB, :]
                if block == strip:
                    piece = piece + jnp.where(eye, ridge_ref[0:1, NB * strip : NB * strip + NB], 0.0)
                a[NB * strip : NB * strip + NB, NB * block : NB * block + NB] = piece
                slot += 1

    for ref, offset in ((own_ref, 0), (other_ref, 1)):
        if offset:
            fetch.wait()
        for which in range(2):
            pl.when(core == which)(lambda: assemble(ref, STRIPS[which ^ offset]))

    def body(panel, carry):
        at = pl.multiple_of(panel * NB, NB)
        w[...] = a[pl.ds(at, NB), pl.ds(at, NB)]
        factor_block(w, upper, inverse)
        for fixed in range(PANELS):

            @pl.when(panel == fixed)
            def _():
                s0, s1 = NB * fixed, NB * fixed + NB
                a[s0:s1, s0:s1] = upper[...]
                if fixed < PANELS - 1:
                    inv, rest = pieces3(inverse[...]), pieces3(a[s0:s1, s1:])
                    rows = mm(
                        jnp.concatenate([inv[k] for k in LEFT], axis=1),
                        jnp.concatenate([rest[k] for k in RIGHT], axis=0),
                    )
                    a[s0:s1, s1:] = rows
                    width = FEAT - s1
                    parts = pieces3(rows)
                    for k in range(6):
                        stack1[NB * k : NB * k + NB, :width] = parts[LEFT[k]]
                        stack2[NB * k : NB * k + NB, :width] = parts[RIGHT[k]]
                    for strip in range(fixed + 1, PANELS, 2):
                        t0, high = NB * strip, min(NB * strip + 2 * NB, FEAT)
                        b0 = t0 - s1
                        update = tmm(stack1[:, b0 : high - s1], stack2[:, b0:width])
                        a[t0 : t0 + NB, t0:] = a[t0 : t0 + NB, t0:] - update[:NB]
                        if high - t0 > NB:
                            t1 = t0 + NB
                            a[t1:high, t1:] = a[t1:high, t1:] - update[NB:, NB:]

        return carry

    lax.fori_loop(0, PANELS, body, 0)
    out = a[pl.ds(pl.multiple_of(position * 8, 8), 8), :]
    lane = lax.broadcasted_iota(jnp.int32, out.shape, 1)
    o_ref[...] = jnp.where(lane >= (position // 16) * NB, out, 0.0)


def factor_rows(ids, ridge, own, other):
    return pl.pallas_call(
        factor_kernel,
        out_shape=(jax.ShapeDtypeStruct((8, FEAT), f32), jax.ShapeDtypeStruct((2,), jnp.int32)),
        in_specs=[SMEM, VMEM, VMEM, ANY],
        out_specs=(VMEM, SMEM),
        scratch_shapes=[pltpu.VMEM(other.shape, f32), pltpu.SemaphoreType.DMA(())]
        + [pltpu.VMEM((FEAT, FEAT), f32)] + [pltpu.VMEM((NB, NB), f32)] * 3
        + [pltpu.VMEM((6 * NB, FEAT), bf16)] * 2,
        compiler_params=params(),
        cost_estimate=pl.CostEstimate(flops=40_000_000_000, bytes_accessed=2 << 20, transcendentals=0),
    )(ids, ridge, own, other)


def swap_cores(x):
    return lax.ppermute(x, "outer", [(0, 1), (1, 0)])


def along_z(x, distance):
    return lax.ppermute(x, "inner", [(i, (i + 16 * distance) % 64) for i in range(64)])


def plane_exchange(x):
    return lax.all_to_all(x, "inner", 0, 0, axis_index_groups=PLANES, tiled=True)


def local(matrix, sign_flip, keep_list, ridge_weights):
    core, inner = lax.axis_index("outer"), lax.axis_index("inner")
    ids = jnp.stack([core, core * 64 + inner]).astype(jnp.int32)
    keep_here = lax.dynamic_index_in_dim(keep_list.reshape(2, 4, 16, 2), inner // 16, 1, False)
    keep_rows = jnp.repeat(keep_here.reshape(32, 2), 4, axis=0)
    mixed = local_mix(matrix, sign_flip)
    along = lax.all_to_all(
        mixed.reshape(4, 128, FEAT), "inner", 0, 0, axis_index_groups=Z_GROUPS, tiled=True
    )
    mine = select_rows(keep_rows, along).reshape(2, 16, 8, FEAT)
    theirs = swap_cores(mine)
    gram, to_send = gram_half(ids, mine, theirs)
    piece = jnp.sum(plane_exchange(gram), axis=0)
    piece = (piece + along_z(piece, 2)) + (along_z(piece, 1) + along_z(piece, 3))
    own = plane_exchange(jnp.broadcast_to(piece[None], (16, GRAM_ROWS, NB))).reshape(16 * GRAM_ROWS, NB)
    to_send, own = lax.optimization_barrier((to_send, own))
    received = plane_exchange(to_send)
    other = swap_cores(own)
    factor, done = factor_rows(ids, ridge_weights.reshape(1, FEAT), own, other)
    sketch = final_mix(done, received.reshape(256, FEAT))
    return sketch, factor


def solution(mesh):
    return jax.shard_map(
        local,
        mesh=mesh,
        in_specs=(P(("outer", "inner"), None), P(("outer", "inner")), P(), P()),
        out_specs=(P(("outer", "inner"), None), P(("outer", "inner"), None)),
        check_vma=False,
    )
```

```python
import jax
import jax.numpy as jnp
import numpy as np
from jax import lax
from jax.experimental import pallas as pl
from jax.experimental.pallas import tpu as pltpu
from jax.sharding import PartitionSpec as P

f32 = jnp.float32
bf16 = jnp.bfloat16
VMEM = pl.BlockSpec(memory_space=pltpu.VMEM)
SMEM = pl.BlockSpec(memory_space=pltpu.SMEM)
ANY = pl.BlockSpec(memory_space=pl.ANY)
FEAT = 1024
NB = 128
PANELS = FEAT // NB
STRIPS = ((0, 3, 4, 7), (1, 2, 5, 6))
GRAM_ROWS = 144
DIRECT = 3
LEFT = (0, 0, 0, 1, 1, 2)
RIGHT = (0, 1, 2, 0, 1, 0)
Z_GROUPS = [[i + 16 * j for j in range(4)] for i in range(16)]
PLANES = [[16 * j + i for i in range(16)] for j in range(4)]


def params(mib=32):
    return pltpu.CompilerParams(vmem_limit_bytes=mib << 20)


def parity_sign(left, right):
    common = left & right
    parity = np.zeros_like(common)
    for shift_by in range(10):
        parity ^= (common >> shift_by) & 1
    return 1 - 2 * parity


def local_table():
    az, c, axy, e = np.meshgrid(range(4), range(2), range(16), range(4), indexing="ij")
    k = (az * 128 + axy * 8 + c * 4 + e).reshape(-1, 1)
    return parity_sign(k, np.arange(512)[None, :]).astype(np.float32).astype(bf16)


def final_table():
    j, i, o, e = (v.reshape(-1, 1) for v in np.meshgrid(range(2), range(16), range(2), range(4), indexing="ij"))
    ip, op, jp, ep = (v.reshape(1, -1) for v in np.meshgrid(range(16), range(2), range(2), range(4), indexing="ij"))
    table = parity_sign(i, ip) * parity_sign(o, op) * (j == jp) * (e == ep)
    return table.astype(np.float32).astype(bf16)


def halves(x):
    high = x.astype(bf16)
    return high, (x - high.astype(f32)).astype(bf16)


def mm(a, b):
    return jnp.dot(a, b, preferred_element_type=f32)


def tmm(a, b):
    return lax.dot_general(a, b, (((0,), (0,)), ((), ())), preferred_element_type=f32)


def local_mix_kernel(table_hbm, sign_hbm, x_hbm, o_hbm, table, sign, signed, x, out, sems):
    chunks, _, cols = out.shape

    def load(chunk):
        part = pl.ds(128 * chunk, 128)
        return pltpu.make_async_copy(x_hbm.at[part], x.at[part], sems.at[chunk])

    def store(chunk):
        target = o_hbm.at[:, cols * chunk : cols * chunk + cols]
        return pltpu.make_async_copy(out.at[chunk], target, sems.at[chunks + chunk])

    get_table = pltpu.make_async_copy(table_hbm, table, sems.at[2 * chunks])
    get_sign = pltpu.make_async_copy(sign_hbm, sign, sems.at[2 * chunks + 1])
    get_sign.start()
    get_table.start()
    for chunk in range(chunks):
        load(chunk).start()
    get_sign.wait()
    get_table.wait()
    signed[...] = (table[...].astype(f32) * (sign[...].astype(f32) * 2.0**-13)).astype(bf16)
    for chunk in range(chunks):
        load(chunk).wait()
    for chunk in range(chunks):
        high, low = halves(x[:, cols * chunk : cols * chunk + cols])
        out[chunk] = mm(signed[...], high) + mm(signed[...], low)
        store(chunk).start()
    for chunk in range(chunks):
        store(chunk).wait()


def local_mix(matrix, sign_flip):
    rows, features = matrix.shape
    chunks = 4
    anywhere = pl.BlockSpec(memory_space=pl.ANY)
    block = pltpu.VMEM((chunks, rows, features // chunks), f32)
    return pl.pallas_call(
        local_mix_kernel,
        out_shape=jax.ShapeDtypeStruct((rows, features), f32),
        in_specs=[anywhere] * 3,
        out_specs=anywhere,
        scratch_shapes=[
            pltpu.VMEM((rows, rows), bf16),
            pltpu.VMEM((1, rows), jnp.int32),
            pltpu.VMEM((rows, rows), bf16),
            pltpu.VMEM((rows, features), f32),
            block,
            pltpu.SemaphoreType.DMA((2 * chunks + 2,)),
        ],
        compiler_params=params(60),
    )(jnp.asarray(local_table()), sign_flip.reshape(1, rows), matrix)


def select_kernel(keep_ref, y_ref, v_ref):
    y0, y1, y2, y3 = (y_ref[z] for z in range(4))
    s, d, s2, d2 = y0 + y1, y0 - y1, y2 + y3, y2 - y3

    def combo(which):
        low = (which & 1) == 1
        first = jnp.where(low, d, s)
        second = jnp.where(low, d2, s2)
        return first + jnp.where((which & 2) == 2, -second, second)

    shape = s.shape
    v0 = combo(jnp.broadcast_to(keep_ref[:, 0:1], shape))
    v1 = combo(jnp.broadcast_to(keep_ref[:, 1:2], shape))
    upper = (lax.broadcasted_iota(jnp.int32, shape, 0) & 7) < 4
    even = jnp.where(upper, v0, pltpu.roll(v1, 4, axis=0))
    odd = jnp.where(upper, pltpu.roll(v0, shape[0] - 4, axis=0), v1)
    v_ref[:, 0] = even.reshape(16, 8, shape[1])
    v_ref[:, 1] = odd.reshape(16, 8, shape[1])


def select_rows(keep_rows, y):
    cols = 512
    features = y.shape[2]
    return pl.pallas_call(
        select_kernel,
        grid=(features // cols,),
        out_shape=jax.ShapeDtypeStruct((16, 2, 8, features), f32),
        in_specs=[
            pl.BlockSpec((128, 2), lambda g: (0, 0)),
            pl.BlockSpec((4, 128, cols), lambda g: (0, 0, g)),
        ],
        out_specs=pl.BlockSpec((16, 2, 8, cols), lambda g: (0, 0, 0, g)),
        compiler_params=params(),
    )(keep_rows, y)


def gram_kernel(ids_ref, v_ref, w_hbm, g_ref, s_hbm, high, low, flat, w_ref, sems):
    core = ids_ref[0]
    fetch = pltpu.make_async_copy(w_hbm, w_ref, sems.at[0])
    fetch.start()
    send_mine = pltpu.make_async_copy(v_ref.at[core], s_hbm.at[:, 0], sems.at[1])
    send_mine.start()
    send_theirs = pltpu.make_async_copy(w_ref.at[core], s_hbm.at[:, 1], sems.at[2])
    for part, ref in enumerate((v_ref, w_ref)):
        if part:
            fetch.wait()
            send_theirs.start()
        h, l = halves(ref[...].reshape(256, FEAT))
        high[256 * part : 256 * part + 256, :] = h
        low[256 * part : 256 * part + 256, :] = l
    for which, strips in enumerate(STRIPS):

        @pl.when(core == which)
        def _():
            row = 0
            for strip in strips:
                at = NB * strip
                h, l = high[:, at : at + NB], low[:, at : at + NB]
                total = tmm(h, high[:, at:]) + (tmm(h, low[:, at:]) + tmm(l, high[:, at:]))
                for block in range(PANELS - strip):
                    flat[row : row + NB, :] = total[:, NB * block : NB * block + NB]
                    row += NB

    for piece in range(16):
        g_ref[piece] = flat[GRAM_ROWS * piece : GRAM_ROWS * (piece + 1), :]
    send_mine.wait()
    send_theirs.wait()


def gram_half(ids, mine, theirs):
    return pl.pallas_call(
        gram_kernel,
        out_shape=(
            jax.ShapeDtypeStruct((16, GRAM_ROWS, NB), f32),
            jax.ShapeDtypeStruct((16, 2, 8, FEAT), f32),
        ),
        in_specs=[SMEM, VMEM, ANY],
        out_specs=(VMEM, ANY),
        scratch_shapes=[pltpu.VMEM((512, FEAT), bf16)] * 2
        + [
            pltpu.VMEM((16 * GRAM_ROWS, NB), f32),
            pltpu.VMEM(mine.shape, f32),
            pltpu.SemaphoreType.DMA((3,)),
        ],
        compiler_params=params(),
    )(ids, mine, theirs)


def final_kernel(ids_ref, table_ref, r_ref, o_hbm, out, sems):
    chunks, rows, cols = out.shape
    odd = (lax.broadcasted_iota(jnp.int32, (rows, cols), 0) >> 2) & 1
    factor = jnp.where((odd * ids_ref[0]) == 1, -32.0, 32.0)

    def store(chunk):
        target = o_hbm.at[:, cols * chunk : cols * chunk + cols]
        return pltpu.make_async_copy(out.at[chunk], target, sems.at[chunk])

    for chunk in range(chunks):
        high, low = halves(r_ref[:, cols * chunk : cols * chunk + cols])
        out[chunk] = (mm(table_ref[...], high) + mm(table_ref[...], low)) * factor
        store(chunk).start()
    for chunk in range(chunks):
        store(chunk).wait()


def final_mix(ids, received):
    rows, features = received.shape
    chunks = 4
    return pl.pallas_call(
        final_kernel,
        out_shape=jax.ShapeDtypeStruct(received.shape, f32),
        in_specs=[SMEM, VMEM, VMEM],
        out_specs=ANY,
        scratch_shapes=[
            pltpu.VMEM((chunks, rows, features // chunks), f32),
            pltpu.SemaphoreType.DMA((chunks,)),
        ],
        compiler_params=params(),
    )(ids, jnp.asarray(final_table()), received)


def lane_splat(x, lane):
    return jnp.broadcast_to(x[:, lane : lane + 1], (8, NB))


def thirds(x):
    high = x.astype(bf16).astype(f32)
    rest = x - high
    middle = rest.astype(bf16).astype(f32)
    return high, middle, rest - middle


def pieces3(x):
    return tuple(part.astype(bf16) for part in thirds(x))


def square_sum(x):
    parts = thirds(x)
    stacked_left = jnp.concatenate([parts[k] for k in LEFT], axis=0).astype(bf16)
    stacked_right = jnp.concatenate([parts[k] for k in RIGHT], axis=0).astype(bf16)
    return tmm(stacked_left, stacked_right)


def tree_sum(terms):
    while len(terms) > 1:
        terms = [x + y for x, y in zip(terms[::2], terms[1::2])]
    return terms[0]


def row_splat(x, row):
    return jnp.broadcast_to(x[row : row + 1, :], (8, NB))


def by_row(sub, values):
    a = [jnp.where((sub & 1) == 0, values[k], values[k + 1]) for k in (0, 2, 4, 6)]
    b = [jnp.where((sub & 2) == 0, a[k], a[k + 1]) for k in (0, 2)]
    return jnp.where(sub < 4, b[0], b[1])


def factor_block(w, upper, inverse):
    lane = lax.broadcasted_iota(jnp.int32, (8, NB), 1)
    sub = lax.broadcasted_iota(jnp.int32, (8, NB), 0)
    groups = NB // 8
    rows = w[0:8, :]
    e = [lane_splat(rows, a) for a in range(8)]
    held = {}
    for step in range(groups):
        base = 8 * step
        inside = (lane >= base) & (lane < base + 8)
        last = min(step + DIRECT, groups - 1)
        near = range(step + 1, last + 1)
        for group in near:
            if group not in held:
                held[group] = w[8 * group : 8 * group + 8, :]
        columns = {group: [lane_splat(held[group], base + b) for b in range(8)] for group in near}
        if near:
            start = [lane_splat(held[step + 1], base + 8 + a) for a in range(8)]
        aug = jnp.where(inside, jnp.where(lane == base + sub, 1.0, 0.0), rows)
        scales, finished = [], []
        multipliers = {group: [] for group in near}
        for b in range(8):
            r = lax.rsqrt(row_splat(e[b], b))
            scales.append(r)
            multiplier = jnp.where(sub > b, e[b], 0.0) * r
            c = {a: row_splat(e[a], b) * r for a in range(b + 1, 8)}
            scaled = row_splat(aug, b) * r
            finished.append(scaled)
            if b < 7:
                for a in range(b + 1, 8):
                    e[a] = e[a] - multiplier * c[a]
                aug = aug - multiplier * scaled
            for group in near:
                column = columns[group]
                multipliers[group].append(column[b] * r)
                for a in range(b + 1, 8):
                    column[a] = column[a] - multipliers[group][b] * c[a]
        scale = by_row(sub, scales)
        right = aug * scale
        left = right
        for a in range(8):
            left = jnp.where(lane == base + a, e[a] * scale, left)
        upper[base : base + 8, :] = jnp.where(lane >= base + sub, left, 0.0)
        inverse[base : base + 8, :] = jnp.where(lane <= base + sub, right, 0.0)
        if not near:
            break
        if last < groups - 1:
            update = square_sum(right)
        m = multipliers[step + 1]
        e = [start[a] - tree_sum([m[b] * row_splat(m[b], a) for b in range(8)]) for a in range(8)]
        for group in near:
            terms = [multipliers[group][b] * finished[b] for b in range(8)]
            held[group] = jnp.where(inside, 0.0, held[group]) - tree_sum(terms)
        rows = held.pop(step + 1)
        if last < groups - 1:
            after = 8 * (last + 1)
            rest = lax.broadcasted_iota(jnp.int32, (NB - after, NB), 1)
            cleared = jnp.where((rest >= base) & (rest < base + 8), 0.0, w[after:, :])
            w[after:, :] = cleared - update[after:, :]


def factor_kernel(ids_ref, ridge_ref, own_ref, other_hbm, o_ref, done_ref, other_ref, sem, a, w, upper, inverse, stack1, stack2):
    core, position = ids_ref[0], ids_ref[1]
    done_ref[0], done_ref[1] = core, position
    fetch = pltpu.make_async_copy(other_hbm, other_ref, sem)
    fetch.start()
    eye = lax.broadcasted_iota(jnp.int32, (NB, NB), 0) == lax.broadcasted_iota(jnp.int32, (NB, NB), 1)

    def assemble(ref, strips):
        slot = 0
        for strip in strips:
            for block in range(strip, PANELS):
                piece = ref[NB * slot : NB * slot + NB, :]
                if block == strip:
                    piece = piece + jnp.where(eye, ridge_ref[0:1, NB * strip : NB * strip + NB], 0.0)
                a[NB * strip : NB * strip + NB, NB * block : NB * block + NB] = piece
                slot += 1

    for ref, offset in ((own_ref, 0), (other_ref, 1)):
        if offset:
            fetch.wait()
        for which in range(2):
            pl.when(core == which)(lambda: assemble(ref, STRIPS[which ^ offset]))

    def body(panel, carry):
        at = pl.multiple_of(panel * NB, NB)
        w[...] = a[pl.ds(at, NB), pl.ds(at, NB)]
        factor_block(w, upper, inverse)
        for fixed in range(PANELS):

            @pl.when(panel == fixed)
            def _():
                s0, s1 = NB * fixed, NB * fixed + NB
                a[s0:s1, s0:s1] = upper[...]
                if fixed < PANELS - 1:
                    inv, rest = pieces3(inverse[...]), pieces3(a[s0:s1, s1:])
                    rows = mm(
                        jnp.concatenate([inv[k] for k in LEFT], axis=1),
                        jnp.concatenate([rest[k] for k in RIGHT], axis=0),
                    )
                    a[s0:s1, s1:] = rows
                    width = FEAT - s1
                    parts = pieces3(rows)
                    for k in range(6):
                        stack1[NB * k : NB * k + NB, :width] = parts[LEFT[k]]
                        stack2[NB * k : NB * k + NB, :width] = parts[RIGHT[k]]
                    for strip in range(fixed + 1, PANELS):
                        b0, t0 = NB * (strip - fixed - 1), NB * strip
                        update = tmm(stack1[:, b0 : b0 + NB], stack2[:, b0:width])
                        a[t0 : t0 + NB, t0:] = a[t0 : t0 + NB, t0:] - update

        return carry

    lax.fori_loop(0, PANELS, body, 0)
    out = a[pl.ds(pl.multiple_of(position * 8, 8), 8), :]
    lane = lax.broadcasted_iota(jnp.int32, out.shape, 1)
    o_ref[...] = jnp.where(lane >= (position // 16) * NB, out, 0.0)


def factor_rows(ids, ridge, own, other):
    return pl.pallas_call(
        factor_kernel,
        out_shape=(jax.ShapeDtypeStruct((8, FEAT), f32), jax.ShapeDtypeStruct((2,), jnp.int32)),
        in_specs=[SMEM, VMEM, VMEM, ANY],
        out_specs=(VMEM, SMEM),
        scratch_shapes=[pltpu.VMEM(other.shape, f32), pltpu.SemaphoreType.DMA(())]
        + [pltpu.VMEM((FEAT, FEAT), f32)] + [pltpu.VMEM((NB, NB), f32)] * 3
        + [pltpu.VMEM((6 * NB, FEAT), bf16)] * 2,
        compiler_params=params(),
        cost_estimate=pl.CostEstimate(flops=40_000_000_000, bytes_accessed=2 << 20, transcendentals=0),
    )(ids, ridge, own, other)


def swap_cores(x):
    return lax.ppermute(x, "outer", [(0, 1), (1, 0)])


def along_z(x, distance):
    return lax.ppermute(x, "inner", [(i, (i + 16 * distance) % 64) for i in range(64)])


def plane_exchange(x):
    return lax.all_to_all(x, "inner", 0, 0, axis_index_groups=PLANES, tiled=True)


def local(matrix, sign_flip, keep_list, ridge_weights):
    core, inner = lax.axis_index("outer"), lax.axis_index("inner")
    ids = jnp.stack([core, core * 64 + inner]).astype(jnp.int32)
    keep_here = lax.dynamic_index_in_dim(keep_list.reshape(2, 4, 16, 2), inner // 16, 1, False)
    keep_rows = jnp.repeat(keep_here.reshape(32, 2), 4, axis=0)
    mixed = local_mix(matrix, sign_flip)
    along = lax.all_to_all(
        mixed.reshape(4, 128, FEAT), "inner", 0, 0, axis_index_groups=Z_GROUPS, tiled=True
    )
    mine = select_rows(keep_rows, along).reshape(2, 16, 8, FEAT)
    theirs = swap_cores(mine)
    gram, to_send = gram_half(ids, mine, theirs)
    piece = jnp.sum(plane_exchange(gram), axis=0)
    piece = (piece + along_z(piece, 2)) + (along_z(piece, 1) + along_z(piece, 3))
    own = plane_exchange(jnp.broadcast_to(piece[None], (16, GRAM_ROWS, NB))).reshape(16 * GRAM_ROWS, NB)
    to_send, own = lax.optimization_barrier((to_send, own))
    received = plane_exchange(to_send)
    other = swap_cores(own)
    factor, done = factor_rows(ids, ridge_weights.reshape(1, FEAT), own, other)
    sketch = final_mix(done, received.reshape(256, FEAT))
    return sketch, factor


def solution(mesh):
    return jax.shard_map(
        local,
        mesh=mesh,
        in_specs=(P(("outer", "inner"), None), P(("outer", "inner")), P(), P()),
        out_specs=(P(("outer", "inner"), None), P(("outer", "inner"), None)),
        check_vma=False,
    )
```
